32 devices in a mesh: group: 4 (over x, core), sub: 8 (over z, y).
Axes of the slice: x: 2, y: 2, z: 4, core: 2. Of those that a mesh axis runs over, the one named last changes fastest.
Arguments:
- schur: bfloat16 [4, 8, 1024, 1024], P('group', 'sub'), as said below
- local_inverse: bfloat16 [4, 8, 1024, 1024], P('group', 'sub'), as said below
- rhs_parts: bfloat16 [4, 8, 1024, 128], P('group', 'sub'), may hold values from -6 to 6
- basis: bfloat16 [4, 8, 32, 1024], P('group', 'sub'), may hold values from -0.1875 to 0.1875
- coarse_map: int32 [4, 8, 32], P('group', 'sub'), may hold values from 0 to 1023
- coarse_inverse: bfloat16 [4, 1024, 1024], P('group', 'sub'), as said below
- shared_rows: int32 [4, 8, 2, 4, 256], P('group', 'sub'), may hold values from 0 to 1023, as said below
- shared_counts: int32 [4, 8, 4], P('group', 'sub'), may hold values from 0 to 256, as said below
Outputs:
- solution: float32 [4, 8, 1024, 128], P('group', 'sub')
- residual: float32 [4, 8, 1024, 128], P('group', 'sub')
The draws below stay inside these ranges and needn't reach their ends.
Inputs may be any that keep to these rules, and one draw needn't show every extreme that they name: `schur`: each subdomain matrix is symmetric positive definite. `local_inverse`: each subdomain matrix is symmetric positive definite. `coarse_inverse`: each group's matrix is symmetric positive definite. `shared_rows`: own rows of direction d lie in rows d * 256 to (d + 1) * 256 - 1 and are distinct within a list; the own rows of direction 0 of (g, s) are the partner rows of direction 1 of (g, s + 1) and the reverse, likewise directions 2 and 3 between (g, s) and (g + 1, s); entries past the count are rows of the same block. `shared_counts`: the count of direction 0 of (g, s) equals the count of direction 1 of (g, s + 1), that of direction 2 of (g, s) the count of direction 3 of (g + 1, s); counts are 0 where no neighbour exists; some count equals 256.
All inputs are finite; a program needn't handle non-finite values.
Results may differ from the reference program's by a relative error of at most 0.014.
Values may be sent and summed in bfloat16 or wider, within the bound.
No kernel may reach another device: no remote copies, remote signals or barrier semaphores. Data moves between devices by JAX's collectives and lax.ppermute only.
A program may use at most 64 MiB of HBM per device.

```python
import math
import jax
import jax.numpy as jnp
from jax import lax

NL = 1024
NRHS = 128
NC = 32
NC0 = 1024
ITERS = 3
CAP = 256
SUBS = 8
GROUPS = 4


def spd_stack(key, total_count, matrix_order):

    def single(position):
        sub_key = jax.random.fold_in(key, position)
        noise_key, diag_key = jax.random.split(sub_key)
        noise_draw = jax.random.normal(noise_key, (matrix_order, matrix_order), jnp.float32)
        diagonal = jax.random.uniform(diag_key, (matrix_order,), jnp.float32, 1.2, 3.0)
        symmetric = (noise_draw + noise_draw.T) * (0.45 / math.sqrt(2.0 * matrix_order))
        return (symmetric + jnp.diag(diagonal)).astype(jnp.bfloat16)
    return lax.map(single, jnp.arange(total_count))


def draw_schur(key, part):
    return spd_stack(jax.random.fold_in(key, 11), GROUPS * SUBS, NL).reshape(GROUPS, SUBS, NL, NL)


def draw_local_inverse(key, part):
    return spd_stack(jax.random.fold_in(key, 23), GROUPS * SUBS, NL).reshape(GROUPS, SUBS, NL, NL)


def draw_coarse_inverse(key, part):
    return spd_stack(jax.random.fold_in(key, 37), GROUPS, NC0)


def interface_plan(key):
    zone_rows = NL // 4
    keys = jax.random.split(jax.random.fold_in(key, 41), 6)
    base = jnp.broadcast_to(jnp.arange(zone_rows, dtype=jnp.int32), (GROUPS, SUBS, zone_rows))
    chain_low = jax.random.permutation(keys[0], base, axis=2, independent=True)
    chain_high = jax.random.permutation(keys[1], base, axis=2, independent=True)
    group_low = jax.random.permutation(keys[2], base, axis=2, independent=True)
    group_high = jax.random.permutation(keys[3], base, axis=2, independent=True)
    sub_pos = jnp.arange(SUBS, dtype=jnp.int32)[None, :]
    group_pos = jnp.arange(GROUPS, dtype=jnp.int32)[:, None]
    chain_count = jax.random.randint(keys[4], (GROUPS, SUBS), zone_rows // 4, zone_rows + 1, dtype=jnp.int32)
    chain_count = chain_count.at[0, 0].set(zone_rows)
    chain_count = jnp.where(sub_pos < SUBS - 1, chain_count, 0)
    group_count = jax.random.randint(keys[5], (GROUPS, SUBS), zone_rows // 4, zone_rows + 1, dtype=jnp.int32)
    group_count = group_count.at[0, 0].set(zone_rows)
    group_count = jnp.where(group_pos < GROUPS - 1, group_count, 0)
    own = jnp.stack([chain_low, zone_rows + jnp.roll(chain_high, 1, axis=1), 2 * zone_rows + group_low, 3 * zone_rows + jnp.roll(group_high, 1, axis=0)], axis=2)
    partner = jnp.stack([zone_rows + chain_high, jnp.roll(chain_low, 1, axis=1), 3 * zone_rows + group_high, 2 * zone_rows + jnp.roll(group_low, 1, axis=0)], axis=2)
    rows_all = jnp.stack([own, partner], axis=2).astype(jnp.int32)
    counts_all = jnp.stack([chain_count, jnp.where(sub_pos > 0, jnp.roll(chain_count, 1, axis=1), 0), group_count, jnp.where(group_pos > 0, jnp.roll(group_count, 1, axis=0), 0)], axis=2).astype(jnp.int32)
    return (rows_all, counts_all)


def draw_shared_rows(key, part):
    return interface_plan(key)[0]


def draw_shared_counts(key, part):
    return interface_plan(key)[1]


def plant(values, stream_key, smallest, largest):
    spot = [jax.random.randint(jax.random.fold_in(stream_key, axis), (), 0, length) for axis, length in enumerate(values.shape)]
    main_axis = values.shape.index(max(values.shape))
    next_to = spot[:main_axis] + [(spot[main_axis] + 1) % values.shape[main_axis]] + spot[main_axis + 1:]
    return values.at[tuple(spot)].set(smallest).at[tuple(next_to)].set(largest)


def levels(key, extent, pieces, least, largest):
    gain, own = 1.0, jax.random.fold_in(key, 6)
    for dim, parts in pieces:
        draws = jnp.exp(jax.random.uniform(jax.random.fold_in(own, dim), (parts,), jnp.float32, least / len(pieces), largest / len(pieces)))
        gain = gain * jnp.repeat(draws, extent[dim] // parts).reshape([-1 if axis == dim else 1 for axis in range(len(extent))])
    return gain


def noise(rng, shape, deviation, most, cuts=(), kind=jnp.bfloat16):
    array = jax.random.normal(rng, shape, jnp.float32) * deviation
    if len(cuts) > 0:
        array = levels(rng, shape, cuts, -0.22, 0.18) * array
    return jnp.clip(array, min=-most, max=most).astype(kind)


def setup_inputs(seed: int = 0) -> dict:
    arg_keys = jax.random.split(jax.random.key(seed), 9)
    return {
        "schur": draw_schur(jax.random.fold_in(arg_keys[8], 71), 0),
        "local_inverse": draw_local_inverse(jax.random.fold_in(arg_keys[8], 71), 0),
        "rhs_parts": noise(arg_keys[2], (GROUPS, SUBS, NL, NRHS), 1.0, 6.0, ((0, 4), (1, 8))),
        "basis": noise(arg_keys[3], (GROUPS, SUBS, NC, NL), NL ** -0.5, 0.1875, ((0, 4), (1, 8))),
        "coarse_map": plant(jax.random.randint(arg_keys[4], (GROUPS, SUBS, NC), 0, NC0), jax.random.fold_in(arg_keys[4], 1), 0, NC0 - 1).astype(jnp.int32),
        "coarse_inverse": draw_coarse_inverse(jax.random.fold_in(arg_keys[8], 71), 0),
        "shared_rows": draw_shared_rows(jax.random.fold_in(arg_keys[8], 71), 0),
        "shared_counts": draw_shared_counts(jax.random.fold_in(arg_keys[8], 71), 0),
    }


def pick_rows(tables, indices):
    return jax.vmap(jax.vmap(lambda source_block, rows_at: source_block[rows_at]))(tables, indices)

def add_rows(bases, indices, additions):

    def single(base_block, rows_at, extra):
        return base_block.at[rows_at.reshape(-1)].add(extra.reshape(-1, base_block.shape[-1]))
    return jax.vmap(jax.vmap(single))(bases, indices, additions)

def count_rows(indices, live_mask):

    def single(rows_at, mask_rows):
        return jnp.ones((NL,), jnp.float32).at[rows_at.reshape(-1)].add(mask_rows.reshape(-1))
    return jax.vmap(jax.vmap(single))(indices, live_mask)

def assemble(blocks, own_rows, partner_rows, live_mask):
    blocks = blocks.astype(jnp.float32)
    zero_sub = jnp.zeros_like(blocks[:, :1])
    zero_group = jnp.zeros_like(blocks[:1])
    next_chain = jnp.concatenate([blocks[:, 1:], zero_sub], axis=1)
    prev_chain = jnp.concatenate([zero_sub, blocks[:, :-1]], axis=1)
    next_group = jnp.concatenate([blocks[1:], zero_group], axis=0)
    prev_group = jnp.concatenate([zero_group, blocks[:-1]], axis=0)
    received = jnp.stack([pick_rows(next_chain, partner_rows[:, :, 0]), pick_rows(prev_chain, partner_rows[:, :, 1]), pick_rows(next_group, partner_rows[:, :, 2]), pick_rows(prev_group, partner_rows[:, :, 3])], axis=2)
    values = received * live_mask[..., None]
    return add_rows(blocks, own_rows, values)

def batch_apply(matrices, vectors, transpose_left):
    lead = matrices.shape[:2]
    flat_mats = matrices.reshape((-1,) + matrices.shape[2:])
    flat_vecs = vectors.reshape((-1,) + vectors.shape[2:])

    def single(pair):
        left = pair[0].T if transpose_left else pair[0]
        return jnp.dot(left.astype(jnp.float32), pair[1].astype(jnp.float32), preferred_element_type=jnp.float32)
    result = lax.map(single, (flat_mats, flat_vecs))
    return result.reshape(lead + result.shape[1:])

def gram_matrix(left, right, weight):
    return jnp.einsum('gsir,gsic->rc', left * weight[..., None], right, precision=lax.Precision.HIGHEST)

def spd_solve(matrix, rhs_block):
    factor = jnp.linalg.cholesky(matrix)
    half = lax.linalg.triangular_solve(factor, rhs_block, left_side=True, lower=True)
    return lax.linalg.triangular_solve(factor, half, left_side=True, lower=True, transpose_a=True)

def contract(blocks, mixing):
    return jnp.einsum('gsir,rc->gsic', blocks, mixing, precision=lax.Precision.HIGHEST)

def reference(schur, local_inverse, rhs_parts, basis, coarse_map, coarse_inverse, shared_rows, shared_counts):
    live_mask = (jnp.arange(CAP, dtype=jnp.int32) < shared_counts[..., None]).astype(jnp.float32)
    own_rows = shared_rows[:, :, 0]
    partner_rows = shared_rows[:, :, 1]
    weight = 1.0 / count_rows(own_rows, live_mask)

    def precondition(resid):
        scaled = (weight[..., None] * resid).astype(jnp.bfloat16)
        local_part = batch_apply(local_inverse, scaled, False)
        coarse_local = batch_apply(basis, scaled, False)

        def group_sum(mapping, terms):
            return jnp.zeros((NC0, NRHS), jnp.float32).at[mapping.reshape(-1)].add(terms.reshape(-1, NRHS))
        coarse_residual = jax.vmap(group_sum)(coarse_map, coarse_local)
        coarse_rounded = coarse_residual.astype(jnp.bfloat16)
        coarse_values = lax.map(lambda pair: jnp.dot(pair[0].astype(jnp.float32), pair[1].astype(jnp.float32), preferred_element_type=jnp.float32), (coarse_inverse, coarse_rounded)).astype(jnp.bfloat16)
        picked = jax.vmap(lambda values_group, mapping: values_group[mapping])(coarse_values, coarse_map)
        coarse_part = batch_apply(basis, picked, True)
        smoothed = weight[..., None] * (local_part + coarse_part)
        return assemble(smoothed, own_rows, partner_rows, live_mask)
    residual = assemble(rhs_parts.astype(jnp.float32), own_rows, partner_rows, live_mask)
    solution = jnp.zeros_like(residual)
    precond = precondition(residual)
    direction = precond
    inner = gram_matrix(precond, residual, weight)
    for iteration in range(ITERS):
        local_image = batch_apply(schur, direction.astype(jnp.bfloat16), False)
        image = assemble(local_image, own_rows, partner_rows, live_mask)
        curvature = gram_matrix(direction, image, weight)
        step_size = spd_solve(curvature, inner)
        solution = solution + contract(direction, step_size)
        residual = residual - contract(image, step_size)
        if iteration + 1 < ITERS:
            precond = precondition(residual)
            inner_next = gram_matrix(precond, residual, weight)
            conjugacy = spd_solve(inner, inner_next)
            direction = precond + contract(direction, conjugacy)
            inner = inner_next
    return (solution, residual)
```

```python
import jax
import jax.numpy as jnp
from jax import lax
from jax.sharding import PartitionSpec as P

ITERS = 3
HIGHEST = lax.Precision.HIGHEST


def halves(x):
    high = lax.reduce_precision(x, 8, 7)
    return jnp.concatenate([high, x - high], axis=-1).astype(jnp.bfloat16)


def times(matrix, x):
    both = jnp.dot(matrix, halves(x), preferred_element_type=jnp.float32)
    n = x.shape[-1]
    return both[:, :n] + both[:, n:]


def times_t(matrix, x):
    both = lax.dot_general(
        matrix, halves(x), (((0,), (0,)), ((), ())), preferred_element_type=jnp.float32
    )
    n = x.shape[-1]
    return both[:, :n] + both[:, n:]


def swap(x, axis, bit):
    return lax.ppermute(x, axis, [(i, i ^ bit) for i in range(lax.axis_size(axis))])


def bits_of(axis):
    count = lax.axis_size(axis)
    if count & (count - 1):
        raise ValueError("axis size")
    return [1 << b for b in range(count.bit_length() - 1)]


def total(x):
    group_bits, sub_bits = bits_of("group"), bits_of("sub")
    order = []
    for i in range(max(len(group_bits), len(sub_bits))):
        if i < len(group_bits):
            order.append(("group", group_bits[i]))
        if i < len(sub_bits):
            order.append(("sub", sub_bits[i]))
    for axis, bit in order:
        x = x + swap(x, axis, bit)
    return x


def gather_sub(x):
    for bit in bits_of("sub"):
        x = jnp.concatenate([x, swap(x, "sub", bit)], axis=0)
    return x


def one_hot(rows, count):
    return rows[:, None] == jnp.arange(count, dtype=jnp.int32)[None, :]


def selected_inverse(coarse_map, inverse_rows):
    modes = coarse_map.shape[0]
    rows_here, coarse_total = inverse_rows.shape
    maps = gather_sub(coarse_map)
    count = maps.shape[0] // modes
    columns = one_hot(maps, coarse_total).astype(jnp.bfloat16)
    picked_columns = lax.dot_general(
        inverse_rows, columns, (((1,), (1,)), ((), ())), preferred_element_type=jnp.float32
    ).astype(jnp.bfloat16)
    first = lax.axis_index("sub") * rows_here
    rows = one_hot(maps - first, rows_here).astype(jnp.bfloat16)
    table = jnp.dot(rows, picked_columns, preferred_element_type=jnp.float32).astype(jnp.bfloat16)
    table = table.reshape(count, modes, count, modes)
    pieces = [
        jnp.concatenate([table[j, :, j ^ k] for k in range(count)], axis=-1) for j in range(count)
    ]
    for bit in reversed(bits_of("sub")):
        sent = swap(jnp.concatenate(pieces[bit:], axis=0), "sub", bit)
        pieces = [pieces[j] + sent[j * modes : (j + 1) * modes] for j in range(bit)]
    return pieces[0]


def neighbour_tables(rows, counts):
    own, partner = rows[0], rows[1]
    capacity = own.shape[1]

    def table(d, zone):
        live = jnp.arange(capacity, dtype=jnp.int32)[:, None] < counts[d]
        to = (one_hot(own[d] - d * capacity, capacity) & live).astype(jnp.bfloat16)
        source = one_hot(partner[d] - zone * capacity, capacity).astype(jnp.bfloat16)
        return lax.dot_general(
            to, source, (((0,), (0,)), ((), ())), preferred_element_type=jnp.float32
        )

    return [table(d, d ^ 1) for d in range(4)]


def line(axis, step):
    count = lax.axis_size(axis)
    return [(i, i + step) for i in range(count) if 0 <= i + step < count]


def shards(
    schur, local_inverse, rhs_parts, basis, coarse_map, coarse_inverse, shared_rows, shared_counts
):
    schur, local_inverse, basis = schur[0, 0], local_inverse[0, 0], basis[0, 0]
    rhs = rhs_parts[0, 0].astype(jnp.float32)
    zone = shared_rows.shape[-1]
    columns = rhs.shape[1]
    tables = neighbour_tables(shared_rows[0, 0], shared_counts[0, 0])
    weight = 1.0 / (1.0 + jnp.concatenate([t.sum(axis=1) for t in tables]))[:, None]
    tables = [t.astype(jnp.bfloat16) for t in tables]
    chosen = selected_inverse(coarse_map[0, 0], coarse_inverse[0])

    def assemble(block):
        received = [
            lax.ppermute(block[(d ^ 1) * zone : ((d ^ 1) + 1) * zone], axis, line(axis, step))
            for d, (axis, step) in enumerate(
                (("sub", -1), ("sub", 1), ("group", -1), ("group", 1))
            )
        ]
        return block + jnp.concatenate([times(t, r) for t, r in zip(tables, received)], axis=0)

    def precondition(block):
        scaled = weight * block
        coarse = gather_sub(times(basis, scaled))
        local = times(local_inverse, scaled)
        picked = times(chosen, coarse)
        return assemble(weight * (local + times_t(basis, picked)))

    def operator(block):
        return assemble(times(schur, block))

    def spd_solve(matrix, block):
        factor = jnp.linalg.cholesky(matrix)
        half = lax.linalg.triangular_solve(factor, block, left_side=True, lower=True)
        return lax.linalg.triangular_solve(
            factor, half, left_side=True, lower=True, transpose_a=True
        )

    def mix(block, mixing):
        return jnp.dot(block, mixing, precision=HIGHEST)

    r = assemble(rhs)
    z = precondition(r)
    w = operator(z)
    x = None
    for iteration in range(ITERS):
        last = iteration + 1 == ITERS
        grams = total(
            lax.dot_general(
                weight * z,
                jnp.concatenate([r, w], axis=1),
                (((0,), (0,)), ((), ())),
                precision=HIGHEST,
            )
        )
        inner, cross = grams[:, :columns], grams[:, columns:]
        if not last:
            m = precondition(w)
            n = operator(m)
        if iteration == 0:
            curvature = cross
            p, s = z, w
            if not last:
                q, t = m, n
        else:
            beta = spd_solve(inner_old, inner)
            curvature = cross - jnp.dot(
                beta.T, jnp.dot(curvature, beta, precision=HIGHEST), precision=HIGHEST
            )
            p, s = z + mix(p, beta), w + mix(s, beta)
            if not last:
                q, t = m + mix(q, beta), n + mix(t, beta)
        alpha = spd_solve(curvature, inner)
        x = mix(p, alpha) if x is None else x + mix(p, alpha)
        r = r - mix(s, alpha)
        if not last:
            z, w = z - mix(q, alpha), w - mix(t, alpha)
        inner_old = inner
    return x[None, None], r[None, None]


def solution(mesh):
    placed = (
        P("group", "sub", None, None),
        P("group", "sub", None, None),
        P("group", "sub", None, None),
        P("group", "sub", None, None),
        P("group", "sub", None),
        P("group", "sub", None),
        P("group", "sub", None, None, None),
        P("group", "sub", None),
    )
    return jax.shard_map(
        shards,
        mesh=mesh,
        in_specs=placed,
        out_specs=(P("group", "sub", None, None), P("group", "sub", None, None)),
        check_vma=False,
    )
```

```python
import jax
import jax.numpy as jnp
from jax import lax
from jax.experimental import pallas as pl
from jax.experimental.pallas import tpu as pltpu
from jax.sharding import PartitionSpec as P

ITERS = 3
HIGHEST = lax.Precision.HIGHEST


def halves(x):
    high = lax.reduce_precision(x, 8, 7)
    return jnp.concatenate([high, x - high], axis=-1).astype(jnp.bfloat16)


def times(matrix, x):
    both = jnp.dot(matrix, halves(x), preferred_element_type=jnp.float32)
    n = x.shape[-1]
    return both[:, :n] + both[:, n:]


def times_t(matrix, x):
    both = lax.dot_general(
        matrix, halves(x), (((0,), (0,)), ((), ())), preferred_element_type=jnp.float32
    )
    n = x.shape[-1]
    return both[:, :n] + both[:, n:]


def swap(x, axis, bit):
    return lax.ppermute(x, axis, [(i, i ^ bit) for i in range(lax.axis_size(axis))])


def bits_of(axis):
    count = lax.axis_size(axis)
    if count & (count - 1):
        raise ValueError("axis size")
    return [1 << b for b in range(count.bit_length() - 1)]


def total(x):
    group_bits, sub_bits = bits_of("group"), bits_of("sub")
    order = []
    for i in range(max(len(group_bits), len(sub_bits))):
        if i < len(group_bits):
            order.append(("group", group_bits[i]))
        if i < len(sub_bits):
            order.append(("sub", sub_bits[i]))
    for axis, bit in order:
        x = x + swap(x, axis, bit)
    return x


def gather_sub(x):
    count = lax.axis_size("sub")
    copies = jnp.broadcast_to(x[None], (count,) + x.shape)
    out = lax.all_to_all(copies, "sub", 0, 0)
    return out.reshape((-1,) + x.shape[1:])


def one_hot(rows, count):
    return rows[:, None] == jnp.arange(count, dtype=jnp.int32)[None, :]


def selected_inverse(coarse_map, inverse_rows):
    modes = coarse_map.shape[0]
    rows_here, coarse_total = inverse_rows.shape
    maps = gather_sub(coarse_map)
    count = maps.shape[0] // modes
    columns = one_hot(maps, coarse_total).astype(jnp.bfloat16)
    picked_columns = lax.dot_general(
        inverse_rows, columns, (((1,), (1,)), ((), ())), preferred_element_type=jnp.float32
    ).astype(jnp.bfloat16)
    first = lax.axis_index("sub") * rows_here
    rows = one_hot(maps - first, rows_here).astype(jnp.bfloat16)
    table = jnp.dot(rows, picked_columns, preferred_element_type=jnp.float32).astype(jnp.bfloat16)
    table = table.reshape(count, modes, count * modes)
    return lax.all_to_all(table, "sub", 0, 0).sum(axis=0)


def eliminate(matrix, block, tile=8):
    n, width = matrix.shape[0], block.shape[1]
    sublane = lax.broadcasted_iota(jnp.int32, (tile, 1), 0)
    left = [matrix[i : i + tile] for i in range(0, n, tile)]
    right = [block[i : i + tile] for i in range(0, n, tile)]
    for k in range(n // tile):
        pivot_left, pivot_right = left[k], right[k]
        at = k * tile
        spread = [
            jnp.broadcast_to(pivot_left[:, at + j : at + j + 1], (tile, n)) for j in range(tile)
        ]
        for j in range(tile):
            inverse = 1.0 / spread[j][j : j + 1]
            here = sublane == j
            column = spread[j]

            def cleared(rows, column=column, inverse=inverse, here=here, j=j):
                pivot = rows[j : j + 1] * inverse
                return jnp.where(here, pivot, rows - column * pivot)

            for i in range(j + 1, tile):
                spread[i] = cleared(spread[i])
            pivot_left, pivot_right = cleared(pivot_left), cleared(pivot_right)
        for i in range(n // tile):
            if i == k:
                continue
            old = left[i]
            new_left, new_right = old, right[i]
            for j in range(tile):
                scale = jnp.broadcast_to(old[:, at + j : at + j + 1], (tile, n))
                new_left = new_left - scale * pivot_left[j : j + 1]
                new_right = new_right - scale * pivot_right[j : j + 1]
            left[i], right[i] = new_left, new_right
        left[k], right[k] = pivot_left, pivot_right
    return jnp.concatenate(right, axis=0)


def exact(a, b):
    return jnp.dot(a, b, precision=HIGHEST, preferred_element_type=jnp.float32)


def symmetric(a):
    return (a + a.T) * 0.5


def first_step_kernel(grams, alpha):
    n = alpha.shape[0]
    alpha[...] = eliminate(symmetric(grams[:, n:]), grams[:, :n])


def next_step_kernel(grams, inner_inverse, curvature_old, alpha, beta, curvature):
    n = alpha.shape[0]
    mixing = exact(inner_inverse[...], grams[:, :n])
    bent = grams[:, n:] - exact(mixing.T, exact(curvature_old[...], mixing))
    beta[...] = mixing
    curvature[...] = bent
    alpha[...] = eliminate(symmetric(bent), grams[:, :n])


def inverse_kernel(grams, out):
    n = out.shape[0]
    rows = lax.broadcasted_iota(jnp.int32, (n, n), 0)
    columns = lax.broadcasted_iota(jnp.int32, (n, n), 1)
    out[...] = eliminate(symmetric(grams[:, :n]), (rows == columns).astype(jnp.float32))


def small(kernel, count, name, *args):
    n = args[0].shape[0]
    square = jax.ShapeDtypeStruct((n, n), jnp.float32)
    return pl.pallas_call(
        kernel,
        out_shape=[square] * count,
        name=name,
        cost_estimate=pl.CostEstimate(flops=8 * n**3, bytes_accessed=6 * 4 * n * n, transcendentals=0),
    )(*args)


def neighbour_tables(rows, counts):
    own, partner = rows[0], rows[1]
    capacity = own.shape[1]

    def table(d, zone):
        live = jnp.arange(capacity, dtype=jnp.int32)[:, None] < counts[d]
        to = (one_hot(own[d] - d * capacity, capacity) & live).astype(jnp.bfloat16)
        source = one_hot(partner[d] - zone * capacity, capacity).astype(jnp.bfloat16)
        return lax.dot_general(
            to, source, (((0,), (0,)), ((), ())), preferred_element_type=jnp.float32
        )

    return [table(d, d ^ 1) for d in range(4)]


def line(axis, step):
    count = lax.axis_size(axis)
    return [(i, i + step) for i in range(count) if 0 <= i + step < count]


def shards(
    schur, local_inverse, rhs_parts, basis, coarse_map, coarse_inverse, shared_rows, shared_counts
):
    schur, local_inverse, basis = schur[0, 0], local_inverse[0, 0], basis[0, 0]
    rhs = rhs_parts[0, 0].astype(jnp.float32)
    zone = shared_rows.shape[-1]
    columns = rhs.shape[1]
    tables = neighbour_tables(shared_rows[0, 0], shared_counts[0, 0])
    weight = 1.0 / (1.0 + jnp.concatenate([t.sum(axis=1) for t in tables]))[:, None]
    tables = [t.astype(jnp.bfloat16) for t in tables]
    chosen = selected_inverse(coarse_map[0, 0], coarse_inverse[0])

    def assemble(block):
        received = [
            lax.ppermute(block[(d ^ 1) * zone : ((d ^ 1) + 1) * zone], axis, line(axis, step))
            for d, (axis, step) in enumerate(
                (("sub", -1), ("sub", 1), ("group", -1), ("group", 1))
            )
        ]
        return block + jnp.concatenate([times(t, r) for t, r in zip(tables, received)], axis=0)

    def precondition(block):
        scaled = weight * block
        coarse = gather_sub(times(basis, scaled))
        local = times(local_inverse, scaled)
        picked = times(chosen, coarse)
        return assemble(weight * (local + times_t(basis, picked)))

    def operator(block):
        return assemble(times(schur, block))

    def mix(block, mixing):
        return jnp.dot(block, mixing, precision=HIGHEST)

    r = assemble(rhs)
    z = precondition(r)
    w = operator(z)
    x = None
    for iteration in range(ITERS):
        last = iteration + 1 == ITERS
        grams = total(
            lax.dot_general(
                weight * z,
                jnp.concatenate([r, w], axis=1),
                (((0,), (0,)), ((), ())),
                precision=HIGHEST,
            )
        )
        if not last:
            m = precondition(w)
            n = operator(m)
        if iteration == 0:
            (alpha,) = small(first_step_kernel, 1, "first_step", grams)
            curvature = grams[:, columns:]
            p, s = z, w
            if not last:
                q, t = m, n
        else:
            alpha, beta, curvature = small(
                next_step_kernel, 3, "next_step", grams, inner_inverse, curvature
            )
            p, s = z + mix(p, beta), w + mix(s, beta)
            if not last:
                q, t = m + mix(q, beta), n + mix(t, beta)
        x = mix(p, alpha) if x is None else x + mix(p, alpha)
        r = r - mix(s, alpha)
        if not last:
            z, w = z - mix(q, alpha), w - mix(t, alpha)
            (inner_inverse,) = small(inverse_kernel, 1, "inverse", grams)
    return x[None, None], r[None, None]


def solution(mesh):
    placed = (
        P("group", "sub", None, None),
        P("group", "sub", None, None),
        P("group", "sub", None, None),
        P("group", "sub", None, None),
        P("group", "sub", None),
        P("group", "sub", None),
        P("group", "sub", None, None, None),
        P("group", "sub", None),
    )
    return jax.shard_map(
        shards,
        mesh=mesh,
        in_specs=placed,
        out_specs=(P("group", "sub", None, None), P("group", "sub", None, None)),
        check_vma=False,
    )
```

```python
import jax
import jax.numpy as jnp
from jax import lax
from jax.experimental import pallas as pl
from jax.experimental.pallas import tpu as pltpu
from jax.sharding import PartitionSpec as P

ITERS = 3
HIGHEST = lax.Precision.HIGHEST


def swap(x, axis, bit):
    return lax.ppermute(x, axis, [(i, i ^ bit) for i in range(lax.axis_size(axis))])


def bits_of(axis):
    count = lax.axis_size(axis)
    if count & (count - 1):
        raise ValueError("axis size")
    return [1 << b for b in range(count.bit_length() - 1)]


def total(x):
    group_bits, sub_bits = bits_of("group"), bits_of("sub")
    order = []
    for i in range(max(len(group_bits), len(sub_bits))):
        if i < len(group_bits):
            order.append(("group", group_bits[i]))
        if i < len(sub_bits):
            order.append(("sub", sub_bits[i]))
    for axis, bit in order:
        x = x + swap(x, axis, bit)
    return x


def gather_sub(x):
    count = lax.axis_size("sub")
    copies = jnp.broadcast_to(x[None], (count,) + x.shape)
    out = lax.all_to_all(copies, "sub", 0, 0)
    return out.reshape((-1,) + x.shape[1:])


def one_hot(rows, count):
    return rows[:, None] == jnp.arange(count, dtype=jnp.int32)[None, :]


def selected_inverse(coarse_map, inverse_rows):
    modes = coarse_map.shape[0]
    rows_here, coarse_total = inverse_rows.shape
    maps = gather_sub(coarse_map)
    count = maps.shape[0] // modes
    columns = one_hot(maps, coarse_total).astype(jnp.bfloat16)
    picked_columns = lax.dot_general(
        inverse_rows, columns, (((1,), (1,)), ((), ())), preferred_element_type=jnp.float32
    ).astype(jnp.bfloat16)
    first = lax.axis_index("sub") * rows_here
    rows = one_hot(maps - first, rows_here).astype(jnp.bfloat16)
    table = jnp.dot(rows, picked_columns, preferred_element_type=jnp.float32).astype(jnp.bfloat16)
    table = table.reshape(count, modes, count * modes)
    return lax.all_to_all(table, "sub", 0, 0).sum(axis=0)


def eliminate(matrix, block, tile=8):
    n, width = matrix.shape[0], block.shape[1]
    sublane = lax.broadcasted_iota(jnp.int32, (tile, 1), 0)
    left = [matrix[i : i + tile] for i in range(0, n, tile)]
    right = [block[i : i + tile] for i in range(0, n, tile)]
    for k in range(n // tile):
        pivot_left, pivot_right = left[k], right[k]
        at = k * tile
        spread = [
            jnp.broadcast_to(pivot_left[:, at + j : at + j + 1], (tile, n)) for j in range(tile)
        ]
        for j in range(tile):
            inverse = 1.0 / spread[j][j : j + 1]
            here = sublane == j
            column = spread[j]

            def cleared(rows, column=column, inverse=inverse, here=here, j=j):
                pivot = rows[j : j + 1] * inverse
                return jnp.where(here, pivot, rows - column * pivot)

            for i in range(j + 1, tile):
                spread[i] = cleared(spread[i])
            pivot_left, pivot_right = cleared(pivot_left), cleared(pivot_right)
        for i in range(n // tile):
            if i == k:
                continue
            old = left[i]
            new_left, new_right = old, right[i]
            for j in range(tile):
                scale = jnp.broadcast_to(old[:, at + j : at + j + 1], (tile, n))
                new_left = new_left - scale * pivot_left[j : j + 1]
                new_right = new_right - scale * pivot_right[j : j + 1]
            left[i], right[i] = new_left, new_right
        left[k], right[k] = pivot_left, pivot_right
    return jnp.concatenate(right, axis=0)


def exact(a, b):
    return jnp.dot(a, b, precision=HIGHEST, preferred_element_type=jnp.float32)


def symmetric(a):
    return (a + a.T) * 0.5


def halves(x):
    high = x.astype(jnp.bfloat16)
    low = (x - high.astype(jnp.float32)).astype(jnp.bfloat16)
    return jnp.concatenate([high, low], axis=1)


def folded(both):
    n = both.shape[1] // 2
    return both[:, :n] + both[:, n:]


def times(matrix, x, contracting=1):
    dims = (((contracting,), (0,)), ((), ()))
    if x.dtype == jnp.bfloat16:
        return lax.dot_general(matrix, x, dims, preferred_element_type=jnp.float32)
    return folded(lax.dot_general(matrix, halves(x), dims, preferred_element_type=jnp.float32))


def mixer(mixing):
    both = halves(mixing)
    return jnp.concatenate([both, both], axis=0)


def mix(block, mixer_value):
    return folded(jnp.dot(halves(block), mixer_value, preferred_element_type=jnp.float32))


def local_gram(weighted, right):
    n = weighted.shape[1]
    both = lax.dot_general(
        halves(weighted),
        halves(right),
        (((0,), (0,)), ((), ())),
        preferred_element_type=jnp.float32,
    )
    both = both[:n] + both[n:]
    return both[:, :n] + both[:, n:]


def zone_of(parity, slot):
    flip = parity[slot // 2]
    return 2 * (slot // 2) + (flip if slot % 2 == 0 else 1 - flip)


def assemble_into(parity, tables, slots, received, out):
    zone = slots[0].shape[0]
    for slot in range(4):
        start = pl.multiple_of(zone_of(parity, slot) * zone, zone)
        value = slots[slot][...].astype(jnp.float32) + times(tables[slot], received[slot][...])
        out[pl.ds(start, zone)] = value


def slots_from(parity, block, slots):
    zone = slots[0].shape[0]
    for slot in range(4):
        pair = 2 * (slot // 2)
        swapped = parity[slot // 2] == (1 if slot % 2 == 0 else 0)
        low, high = block[pair * zone : (pair + 1) * zone], block[(pair + 1) * zone : (pair + 2) * zone]
        slots[slot][...] = jnp.where(swapped, high, low)


def coarse_pieces(basis, scaled, pieces):
    piece = times(basis[...], scaled)
    for i in range(pieces.shape[0]):
        pieces[i] = piece


def tables_kernel(parity, rows, counts, tables, weight):
    capacity = rows.shape[2]
    place = lax.broadcasted_iota(jnp.int32, (capacity, capacity), 0)
    entry = lax.broadcasted_iota(jnp.int32, (1, capacity), 1)
    for slot in range(4):
        d = zone_of(parity, slot)
        partner_zone = zone_of(parity, slot ^ 1)
        own = rows[0, pl.ds(d, 1)] - d * capacity
        partner = rows[1, pl.ds(d, 1)] - partner_zone * capacity
        own = jnp.where(entry < counts[d], own, -1)
        to = (place == own).astype(jnp.float32).astype(jnp.bfloat16)
        source = (place == partner).astype(jnp.float32).astype(jnp.bfloat16)
        table = lax.dot_general(
            to, source, (((1,), (1,)), ((), ())), preferred_element_type=jnp.float32
        )
        tables[slot] = table.astype(jnp.bfloat16)
        ones = jnp.ones((capacity, weight.shape[1]), jnp.bfloat16)
        shared = jnp.dot(table.astype(jnp.bfloat16), ones, preferred_element_type=jnp.float32)
        weight[pl.ds(pl.multiple_of(d * capacity, capacity), capacity)] = 1.0 / (1.0 + shared)


def start_kernel(parity, tables, weight, basis, *refs):
    slots, received, (block, pieces) = refs[:4], refs[4:8], refs[8:]
    assemble_into(parity, tables, slots, received, block)
    coarse_pieces(basis, weight[...] * block[...], pieces)


def gram_start_kernel(parity, tables, weight, basis, z, r, *refs):
    slots, received, (block, pieces, grams) = refs[:4], refs[4:8], refs[8:]
    n = z.shape[1]
    assemble_into(parity, tables, slots, received, block)
    coarse_pieces(basis, weight[...] * block[...], pieces)
    weighted = weight[...] * z[...]
    grams[:, :n] = local_gram(weighted, r[...])
    grams[:, n:] = local_gram(weighted, block[...])


def local_kernel(weight, matrix, block, out):
    out[...] = times(matrix[...], weight[...] * block[...])


def finish_kernel(parity, weight, basis, chosen, pieces, local, *slots):
    count, modes, n = pieces.shape
    picked = times(chosen[...], pieces[...].reshape(count * modes, n))
    smoothed = weight[...] * (local[...] + times(basis[...], picked, contracting=0))
    slots_from(parity, smoothed, slots)


def operator_kernel(parity, tables, matrix, *refs):
    slots, received, (block, out) = refs[:4], refs[4:8], (refs[8], refs[9:])
    assemble_into(parity, tables, slots, received, block)
    slots_from(parity, times(matrix[...], block[...]), out)


def first_update_kernel(parity, tables, weight, basis, grams, z, w, r, m, *refs):
    slots, received = refs[:4], refs[4:8]
    x, r_out, z_out, w_out, image, grams_out, pieces = refs[8:]
    n = z.shape[1]
    assemble_into(parity, tables, slots, received, image)
    alpha = mixer(eliminate(symmetric(grams[:, n:]), grams[:, :n]))
    w_new = w[...] - mix(image[...], alpha)
    w_out[...] = w_new
    coarse_pieces(basis, weight[...] * w_new, pieces)
    x[...] = mix(z[...], alpha)
    r_new = r[...] - mix(w[...], alpha)
    r_out[...] = r_new
    z_new = z[...] - mix(m[...], alpha)
    z_out[...] = z_new
    weighted = weight[...] * z_new
    grams_out[:, :n] = local_gram(weighted, r_new)
    grams_out[:, n:] = local_gram(weighted, w_new)


def step_sizes(grams, inner_inverse, curvature):
    n = grams.shape[0]
    beta = exact(inner_inverse[...], grams[:, :n])
    bent = grams[:, n:] - exact(beta.T, exact(curvature[...], beta))
    return beta, bent, eliminate(symmetric(bent), grams[:, :n])


def next_update_kernel(
    parity, tables, weight, basis, grams, inner_inverse, curvature, z, w, r, m, p, s, q, t, x, *refs
):
    slots, received = refs[:4], refs[4:8]
    (
        x_out, r_out, z_out, w_out, p_out, s_out, q_out, t_out, curvature_out, grams_out, pieces
    ) = refs[8:]
    n = z.shape[1]
    assemble_into(parity, tables, slots, received, t_out)
    beta, bent, alpha = step_sizes(grams, inner_inverse, curvature)
    curvature_out[...] = bent
    beta, alpha = mixer(beta), mixer(alpha)
    t_out[...] = t_out[...] + mix(t[...], beta)
    w_new = w[...] - mix(t_out[...], alpha)
    w_out[...] = w_new
    coarse_pieces(basis, weight[...] * w_new, pieces)
    p_out[...] = z[...] + mix(p[...], beta)
    s_out[...] = w[...] + mix(s[...], beta)
    q_out[...] = m[...] + mix(q[...], beta)
    x_out[...] = x[...] + mix(p_out[...], alpha)
    r_new = r[...] - mix(s_out[...], alpha)
    r_out[...] = r_new
    z_new = z[...] - mix(q_out[...], alpha)
    z_out[...] = z_new
    weighted = weight[...] * z_new
    grams_out[:, :n] = local_gram(weighted, r_new)
    grams_out[:, n:] = local_gram(weighted, w_new)


def last_update_kernel(grams, inner_inverse, curvature, z, w, r, p, s, x, x_out, r_out):
    beta, _, alpha = step_sizes(grams, inner_inverse, curvature)
    beta, alpha = mixer(beta), mixer(alpha)
    x_out[...] = x[...] + mix(z[...] + mix(p[...], beta), alpha)
    r_out[...] = r[...] - mix(w[...] + mix(s[...], beta), alpha)


def inverse_kernel(grams, out):
    n = out.shape[0]
    rows = lax.broadcasted_iota(jnp.int32, (n, n), 0)
    columns = lax.broadcasted_iota(jnp.int32, (n, n), 1)
    out[...] = eliminate(symmetric(grams[:, :n]), (rows == columns).astype(jnp.float32))


VMEM = pl.BlockSpec(memory_space=pltpu.VMEM)
SMEM = pl.BlockSpec(memory_space=pltpu.SMEM)


def call(kernel, name, flops, outs, *args):
    shapes = [jax.ShapeDtypeStruct(shape, dtype) for shape, dtype in outs]
    moved = sum(a.size * a.dtype.itemsize for a in (*args, *shapes))
    return pl.pallas_call(
        kernel,
        out_shape=shapes,
        in_specs=[SMEM if a.ndim == 1 else VMEM for a in args],
        out_specs=[VMEM] * len(shapes),
        name=name,
        compiler_params=pltpu.CompilerParams(vmem_limit_bytes=32 * 1024 * 1024),
        cost_estimate=pl.CostEstimate(flops=flops, bytes_accessed=moved, transcendentals=0),
    )(*args)


def pairs(axis, first):
    count = lax.axis_size(axis)
    low = range(first, count - 1, 2)
    return [(i, i + 1) for i in low] + [(i + 1, i) for i in low]


def exchange(slots):
    return [
        lax.ppermute(slot, axis, pairs(axis, first))
        for slot, (axis, first) in zip(
            slots, (("sub", 0), ("sub", 1), ("group", 0), ("group", 1))
        )
    ]


def shards(
    schur, local_inverse, rhs_parts, basis, coarse_map, coarse_inverse, shared_rows, shared_counts
):
    schur, local_inverse, basis = schur[0, 0], local_inverse[0, 0], basis[0, 0]
    rhs = rhs_parts[0, 0]
    rows, columns = rhs.shape
    zone = shared_rows.shape[-1]
    modes = basis.shape[0]
    subs = lax.axis_size("sub")
    parity = jnp.stack([lax.axis_index("sub") % 2, lax.axis_index("group") % 2]).astype(jnp.int32)
    block = ((rows, columns), jnp.float32)
    part = ((zone, columns), jnp.float32)
    square = ((columns, columns), jnp.float32)
    double = ((columns, 2 * columns), jnp.float32)
    shares = ((subs, modes, columns), jnp.float32)
    solve_flops = 400_000_000
    product_flops = 4 * rows * rows * columns

    def rhs_zone(slot):
        return lax.dynamic_slice_in_dim(rhs, zone_of(parity, slot) * zone, zone, axis=0)

    rhs_slots = [rhs_zone(slot) for slot in range(4)]
    received = exchange(rhs_slots)
    tables, weight = call(
        tables_kernel,
        "shared_row_tables",
        16 * zone**3,
        [((4, zone, zone), jnp.bfloat16), block],
        parity,
        shared_rows[0, 0],
        shared_counts[0, 0],
    )
    chosen = selected_inverse(coarse_map[0, 0], coarse_inverse[0])

    def precondition(vector, pieces):
        gathered = lax.all_to_all(pieces, "sub", 0, 0)
        (local,) = call(
            local_kernel, "local_inverse", product_flops, [block], weight, local_inverse, vector
        )
        slots = call(
            finish_kernel,
            "coarse_part",
            product_flops // 8,
            [part] * 4,
            parity,
            weight,
            basis,
            chosen,
            gathered,
            local,
        )
        return slots, exchange(slots)

    def operator(slots, received):
        vector, *image = call(
            operator_kernel,
            "operator",
            product_flops,
            [block] + [part] * 4,
            parity,
            tables,
            schur,
            *slots,
            *received,
        )
        return vector, image, exchange(image)

    r, pieces = call(
        start_kernel,
        "start",
        product_flops // 8,
        [block, shares],
        parity,
        tables,
        weight,
        basis,
        *rhs_slots,
        *received,
    )
    z, image, received = operator(*precondition(r, pieces))
    w, pieces, local = call(
        gram_start_kernel,
        "start_grams",
        product_flops // 4,
        [block, shares, double],
        parity,
        tables,
        weight,
        basis,
        z,
        r,
        *image,
        *received,
    )
    for iteration in range(ITERS):
        grams = total(local)
        if iteration + 1 == ITERS:
            break
        (inverse,) = call(inverse_kernel, "inner_inverse", solve_flops, [square], grams)
        m, image, received = operator(*precondition(w, pieces))
        common = (parity, tables, weight, basis, grams)
        if iteration == 0:
            p, s, q, curvature = z, w, m, grams[:, columns:]
            x, r, z, w, t, local, pieces = call(
                first_update_kernel,
                "first_update",
                2 * solve_flops,
                [block] * 5 + [double, shares],
                *common,
                z,
                w,
                r,
                m,
                *image,
                *received,
            )
        else:
            x, r, z, w, p, s, q, t, curvature, local, pieces = call(
                next_update_kernel,
                "next_update",
                2 * solve_flops,
                [block] * 8 + [square, double, shares],
                *common,
                inner_inverse,
                curvature,
                z,
                w,
                r,
                m,
                p,
                s,
                q,
                t,
                x,
                *image,
                *received,
            )
        inner_inverse = inverse
    x, r = call(
        last_update_kernel,
        "last_update",
        2 * solve_flops,
        [block, block],
        grams,
        inner_inverse,
        curvature,
        z,
        w,
        r,
        p,
        s,
        x,
    )
    return x[None, None], r[None, None]


def solution(mesh):
    placed = (
        P("group", "sub", None, None),
        P("group", "sub", None, None),
        P("group", "sub", None, None),
        P("group", "sub", None, None),
        P("group", "sub", None),
        P("group", "sub", None),
        P("group", "sub", None, None, None),
        P("group", "sub", None),
    )
    return jax.shard_map(
        shards,
        mesh=mesh,
        in_specs=placed,
        out_specs=(P("group", "sub", None, None), P("group", "sub", None, None)),
        check_vma=False,
    )
```

```python
import jax
import jax.numpy as jnp
from jax import lax
from jax.experimental import pallas as pl
from jax.experimental.pallas import tpu as pltpu
from jax.sharding import PartitionSpec as P

ITERS = 3
HIGHEST = lax.Precision.HIGHEST


def swap(x, axis, bit):
    return lax.ppermute(x, axis, [(i, i ^ bit) for i in range(lax.axis_size(axis))])


def bits_of(axis):
    count = lax.axis_size(axis)
    if count & (count - 1):
        raise ValueError("axis size")
    return [1 << b for b in range(count.bit_length() - 1)]


def total(kept, sent):
    half = kept + swap(sent, "group", 1)
    rest = [("group", bit) for bit in bits_of("group")[1:]]
    subs = [("sub", bit) for bit in bits_of("sub")]
    for axis, bit in subs[:1] + rest + subs[1:]:
        half = half + swap(half, axis, bit)
    return half, swap(half, "group", 1)


def gather_sub(x):
    pieces = [x]
    for bit in bits_of("sub"):
        pieces.append(swap(jnp.concatenate(pieces, axis=0), "sub", bit))
    return pieces


def one_hot(rows, count):
    return rows[:, None] == jnp.arange(count, dtype=jnp.int32)[None, :]


def selected_inverse(coarse_map, inverse_rows):
    modes = coarse_map.shape[0]
    rows_here, coarse_total = inverse_rows.shape
    maps = jnp.concatenate(gather_sub(coarse_map))
    count = maps.shape[0] // modes
    columns = one_hot(maps, coarse_total).astype(jnp.bfloat16)
    picked_columns = lax.dot_general(
        inverse_rows, columns, (((1,), (1,)), ((), ())), preferred_element_type=jnp.float32
    ).astype(jnp.bfloat16)
    first = lax.axis_index("sub") * rows_here
    rows = one_hot(maps - first, rows_here).astype(jnp.bfloat16)
    table = jnp.dot(rows, picked_columns, preferred_element_type=jnp.float32).astype(jnp.bfloat16)
    table = table.reshape(count, modes, count, modes)
    pieces = jnp.stack(
        [
            jnp.concatenate([table[j, :, j ^ k] for k in range(count)], axis=-1)
            for j in range(count)
        ]
    )
    for bit in reversed(bits_of("sub")):
        pieces = pieces[:bit] + swap(pieces[bit:], "sub", bit)
    return pieces[0]


def eliminate(matrix, block, tile=8):
    n, width = matrix.shape[0], block.shape[1]
    sublane = lax.broadcasted_iota(jnp.int32, (tile, 1), 0)
    left = [matrix[i : i + tile] for i in range(0, n, tile)]
    right = [block[i : i + tile] for i in range(0, n, tile)]
    for k in range(n // tile):
        pivot_left, pivot_right = left[k], right[k]
        at = k * tile
        spread = [
            jnp.broadcast_to(pivot_left[:, at + j : at + j + 1], (tile, n)) for j in range(tile)
        ]
        for j in range(tile):
            inverse = 1.0 / spread[j][j : j + 1]
            here = sublane == j
            column = spread[j]

            def cleared(rows, column=column, inverse=inverse, here=here, j=j):
                pivot = rows[j : j + 1] * inverse
                return jnp.where(here, pivot, rows - column * pivot)

            for i in range(j + 1, tile):
                spread[i] = cleared(spread[i])
            pivot_left, pivot_right = cleared(pivot_left), cleared(pivot_right)
        for i in range(n // tile):
            if i == k:
                continue
            old = left[i]
            new_left, new_right = old, right[i]
            for j in range(tile):
                scale = jnp.broadcast_to(old[:, at + j : at + j + 1], (tile, n))
                new_left = new_left - scale * pivot_left[j : j + 1]
                new_right = new_right - scale * pivot_right[j : j + 1]
            left[i], right[i] = new_left, new_right
        left[k], right[k] = pivot_left, pivot_right
    return jnp.concatenate(right, axis=0)


def exact(a, b):
    return jnp.dot(a, b, precision=HIGHEST, preferred_element_type=jnp.float32)


def symmetric(a):
    return (a + a.T) * 0.5


def halves(x):
    high = x.astype(jnp.bfloat16)
    low = (x - high.astype(jnp.float32)).astype(jnp.bfloat16)
    return jnp.concatenate([high, low], axis=1)


def folded(both):
    n = both.shape[1] // 2
    return both[:, :n] + both[:, n:]


def times(matrix, x, contracting=1):
    dims = (((contracting,), (0,)), ((), ()))
    if x.dtype == jnp.bfloat16:
        return lax.dot_general(matrix, x, dims, preferred_element_type=jnp.float32)
    return folded(lax.dot_general(matrix, halves(x), dims, preferred_element_type=jnp.float32))


def mixer(mixing):
    both = halves(mixing)
    return jnp.concatenate([both, both], axis=0)


def mix(block, mixer_value):
    return folded(jnp.dot(halves(block), mixer_value, preferred_element_type=jnp.float32))


def local_gram(weighted, right):
    n = weighted.shape[1]
    both = lax.dot_general(
        halves(weighted),
        halves(right),
        (((0,), (0,)), ((), ())),
        preferred_element_type=jnp.float32,
    )
    both = both[:n] + both[n:]
    return both[:, :n] + both[:, n:]


def packed_halves(parity, inner, cross, kept, sent):
    n, half = inner.shape[0], kept.shape[0]
    rows = lax.broadcasted_iota(jnp.int32, (n, n), 0)
    columns = lax.broadcasted_iota(jnp.int32, (n, n), 1)
    body = jnp.where(rows > columns, inner, jnp.where(rows < columns, cross, 0.0))
    tail_rows = lax.broadcasted_iota(jnp.int32, (2 * half - n, n), 0)
    first = jnp.sum(jnp.where(rows == columns, inner, 0.0), axis=0, keepdims=True)
    second = jnp.sum(jnp.where(rows == columns, cross, 0.0), axis=0, keepdims=True)
    tail = jnp.where(tail_rows == 0, first, jnp.where(tail_rows == 1, second, 0.0))
    low, high = body[:half], jnp.concatenate([body[half:], tail], axis=0)
    kept[...] = jnp.where(parity[1] == 0, low, high)
    sent[...] = jnp.where(parity[1] == 0, high, low)


def unpacked(parity, half, other):
    low = jnp.where(parity[1] == 0, half[...], other[...])
    high = jnp.where(parity[1] == 0, other[...], half[...])
    n = low.shape[1]
    rows = lax.broadcasted_iota(jnp.int32, (n, n), 0)
    columns = lax.broadcasted_iota(jnp.int32, (n, n), 1)
    below = n - low.shape[0]
    body = jnp.concatenate([low, high[:below]], axis=0)
    lower = jnp.where(rows > columns, body, 0.0)
    upper = jnp.where(rows < columns, body, 0.0)
    inner = lower + lower.T + jnp.where(rows == columns, high[below : below + 1], 0.0)
    cross = upper + upper.T + jnp.where(rows == columns, high[below + 1 : below + 2], 0.0)
    return inner, cross


def zone_of(parity, slot):
    flip = parity[slot // 2]
    return 2 * (slot // 2) + (flip if slot % 2 == 0 else 1 - flip)


def assemble_into(parity, tables, slots, received, out):
    zone = slots[0].shape[0]
    for slot in range(4):
        start = pl.multiple_of(zone_of(parity, slot) * zone, zone)
        value = slots[slot][...].astype(jnp.float32) + times(tables[slot], received[slot][...])
        out[pl.ds(start, zone)] = value


def slots_from(parity, block, slots):
    zone = slots[0].shape[0]
    for slot in range(4):
        pair = 2 * (slot // 2)
        swapped = parity[slot // 2] == (1 if slot % 2 == 0 else 0)
        low, high = block[pair * zone : (pair + 1) * zone], block[(pair + 1) * zone : (pair + 2) * zone]
        slots[slot][...] = jnp.where(swapped, high, low)


def coarse_pieces(basis, scaled, pieces):
    pieces[...] = times(basis[...], scaled)


def tables_kernel(parity, rows, counts, tables, weight):
    capacity = rows.shape[2]
    place = lax.broadcasted_iota(jnp.int32, (capacity, capacity), 0)
    entry = lax.broadcasted_iota(jnp.int32, (1, capacity), 1)
    for slot in range(4):
        d = zone_of(parity, slot)
        partner_zone = zone_of(parity, slot ^ 1)
        own = rows[0, pl.ds(d, 1)] - d * capacity
        partner = rows[1, pl.ds(d, 1)] - partner_zone * capacity
        own = jnp.where(entry < counts[d], own, -1)
        to = (place == own).astype(jnp.float32).astype(jnp.bfloat16)
        source = (place == partner).astype(jnp.float32).astype(jnp.bfloat16)
        table = lax.dot_general(
            to, source, (((1,), (1,)), ((), ())), preferred_element_type=jnp.float32
        )
        tables[slot] = table.astype(jnp.bfloat16)
        ones = jnp.ones((capacity, weight.shape[1]), jnp.bfloat16)
        shared = jnp.dot(table.astype(jnp.bfloat16), ones, preferred_element_type=jnp.float32)
        weight[pl.ds(pl.multiple_of(d * capacity, capacity), capacity)] = 1.0 / (1.0 + shared)


def start_kernel(parity, tables, weight, basis, *refs):
    slots, received, (block, pieces) = refs[:4], refs[4:8], refs[8:]
    assemble_into(parity, tables, slots, received, block)
    coarse_pieces(basis, weight[...] * block[...], pieces)


def gram_start_kernel(parity, tables, weight, basis, z, r, *refs):
    slots, received, (block, pieces, kept, sent) = refs[:4], refs[4:8], refs[8:]
    assemble_into(parity, tables, slots, received, block)
    coarse_pieces(basis, weight[...] * block[...], pieces)
    weighted = weight[...] * z[...]
    packed_halves(
        parity, local_gram(weighted, r[...]), local_gram(weighted, block[...]), kept, sent
    )


def local_kernel(weight, matrix, block, out):
    out[...] = times(matrix[...], weight[...] * block[...])


def finish_kernel(parity, weight, basis, chosen, local, *refs):
    gathered, slots = refs[:-4], refs[-4:]
    pieces = jnp.concatenate([piece[...] for piece in gathered], axis=0)
    picked = times(chosen[...], pieces)
    smoothed = weight[...] * (local[...] + times(basis[...], picked, contracting=0))
    slots_from(parity, smoothed, slots)


def operator_kernel(parity, tables, matrix, *refs):
    slots, received, (block, out) = refs[:4], refs[4:8], (refs[8], refs[9:])
    assemble_into(parity, tables, slots, received, block)
    slots_from(parity, times(matrix[...], block[...]), out)


def first_update_kernel(parity, tables, weight, basis, half, other, z, w, r, m, *refs):
    slots, received = refs[:4], refs[4:8]
    x, r_out, z_out, w_out, image, curvature_out, kept, sent, pieces = refs[8:]
    assemble_into(parity, tables, slots, received, image)
    inner, cross = unpacked(parity, half, other)
    curvature_out[...] = cross
    alpha = mixer(eliminate(cross, inner))
    w_new = w[...] - mix(image[...], alpha)
    w_out[...] = w_new
    coarse_pieces(basis, weight[...] * w_new, pieces)
    x[...] = mix(z[...], alpha)
    r_new = r[...] - mix(w[...], alpha)
    r_out[...] = r_new
    z_new = z[...] - mix(m[...], alpha)
    z_out[...] = z_new
    weighted = weight[...] * z_new
    packed_halves(
        parity, local_gram(weighted, r_new), local_gram(weighted, w_new), kept, sent
    )


def step_sizes(parity, half, other, inner_inverse, curvature):
    inner, cross = unpacked(parity, half, other)
    beta = exact(inner_inverse[...], inner)
    bent = symmetric(cross - exact(beta.T, exact(curvature[...], beta)))
    return beta, bent, eliminate(bent, inner)


def next_update_kernel(
    parity, tables, weight, basis, half, other, inner_inverse, curvature,
    z, w, r, m, p, s, q, t, x, *refs
):
    slots, received = refs[:4], refs[4:8]
    (
        x_out, r_out, z_out, w_out, p_out, s_out, q_out, t_out, curvature_out, kept, sent, pieces
    ) = refs[8:]
    assemble_into(parity, tables, slots, received, t_out)
    beta, bent, alpha = step_sizes(parity, half, other, inner_inverse, curvature)
    curvature_out[...] = bent
    beta, alpha = mixer(beta), mixer(alpha)
    t_out[...] = t_out[...] + mix(t[...], beta)
    w_new = w[...] - mix(t_out[...], alpha)
    w_out[...] = w_new
    coarse_pieces(basis, weight[...] * w_new, pieces)
    p_out[...] = z[...] + mix(p[...], beta)
    s_out[...] = w[...] + mix(s[...], beta)
    q_out[...] = m[...] + mix(q[...], beta)
    x_out[...] = x[...] + mix(p_out[...], alpha)
    r_new = r[...] - mix(s_out[...], alpha)
    r_out[...] = r_new
    z_new = z[...] - mix(q_out[...], alpha)
    z_out[...] = z_new
    weighted = weight[...] * z_new
    packed_halves(
        parity, local_gram(weighted, r_new), local_gram(weighted, w_new), kept, sent
    )


def last_update_kernel(parity, half, other, inner_inverse, curvature, z, w, r, p, s, x, x_out, r_out):
    beta, _, alpha = step_sizes(parity, half, other, inner_inverse, curvature)
    beta, alpha = mixer(beta), mixer(alpha)
    x_out[...] = x[...] + mix(z[...] + mix(p[...], beta), alpha)
    r_out[...] = r[...] - mix(w[...] + mix(s[...], beta), alpha)


def inverse_kernel(parity, half, other, out):
    n = out.shape[0]
    rows = lax.broadcasted_iota(jnp.int32, (n, n), 0)
    columns = lax.broadcasted_iota(jnp.int32, (n, n), 1)
    inner, _ = unpacked(parity, half, other)
    out[...] = eliminate(inner, (rows == columns).astype(jnp.float32))


VMEM = pl.BlockSpec(memory_space=pltpu.VMEM)
SMEM = pl.BlockSpec(memory_space=pltpu.SMEM)


def call(kernel, name, flops, outs, *args):
    shapes = [jax.ShapeDtypeStruct(shape, dtype) for shape, dtype in outs]
    moved = sum(a.size * a.dtype.itemsize for a in (*args, *shapes))
    return pl.pallas_call(
        kernel,
        out_shape=shapes,
        in_specs=[SMEM if a.ndim == 1 else VMEM for a in args],
        out_specs=[VMEM] * len(shapes),
        name=name,
        compiler_params=pltpu.CompilerParams(vmem_limit_bytes=24 * 1024 * 1024),
        cost_estimate=pl.CostEstimate(flops=flops, bytes_accessed=moved, transcendentals=0),
    )(*args)


def pairs(axis, first):
    count = lax.axis_size(axis)
    low = range(first, count - 1, 2)
    return [(i, i + 1) for i in low] + [(i + 1, i) for i in low]


def exchange(slots):
    return [
        lax.ppermute(slot, axis, pairs(axis, first))
        for slot, (axis, first) in zip(
            slots, (("sub", 0), ("sub", 1), ("group", 0), ("group", 1))
        )
    ]


def shards(
    schur, local_inverse, rhs_parts, basis, coarse_map, coarse_inverse, shared_rows, shared_counts
):
    schur, local_inverse, basis = schur[0, 0], local_inverse[0, 0], basis[0, 0]
    rhs = rhs_parts[0, 0]
    rows, columns = rhs.shape
    zone = shared_rows.shape[-1]
    modes = basis.shape[0]
    parity = jnp.stack([lax.axis_index("sub") % 2, lax.axis_index("group") % 2]).astype(jnp.int32)
    block = ((rows, columns), jnp.float32)
    part = ((zone, columns), jnp.float32)
    square = ((columns, columns), jnp.float32)
    half_sum = ((columns // 2 + 8, columns), jnp.float32)
    share = ((modes, columns), jnp.float32)
    solve_flops = 400_000_000
    product_flops = 4 * rows * rows * columns

    def rhs_zone(slot):
        return lax.dynamic_slice_in_dim(rhs, zone_of(parity, slot) * zone, zone, axis=0)

    rhs_slots = [rhs_zone(slot) for slot in range(4)]
    received = exchange(rhs_slots)
    tables, weight = call(
        tables_kernel,
        "shared_row_tables",
        16 * zone**3,
        [((4, zone, zone), jnp.bfloat16), block],
        parity,
        shared_rows[0, 0],
        shared_counts[0, 0],
    )
    chosen = selected_inverse(coarse_map[0, 0], coarse_inverse[0])

    def precondition(vector, pieces):
        gathered = gather_sub(pieces)
        (local,) = call(
            local_kernel, "local_inverse", product_flops, [block], weight, local_inverse, vector
        )
        slots = call(
            finish_kernel,
            "coarse_part",
            product_flops // 8,
            [part] * 4,
            parity,
            weight,
            basis,
            chosen,
            local,
            *gathered,
        )
        return slots, exchange(slots)

    def operator(slots, received):
        vector, *image = call(
            operator_kernel,
            "operator",
            product_flops,
            [block] + [part] * 4,
            parity,
            tables,
            schur,
            *slots,
            *received,
        )
        return vector, image, exchange(image)

    r, pieces = call(
        start_kernel,
        "start",
        product_flops // 8,
        [block, share],
        parity,
        tables,
        weight,
        basis,
        *rhs_slots,
        *received,
    )
    z, image, received = operator(*precondition(r, pieces))
    w, pieces, *local = call(
        gram_start_kernel,
        "start_grams",
        product_flops // 4,
        [block, share, half_sum, half_sum],
        parity,
        tables,
        weight,
        basis,
        z,
        r,
        *image,
        *received,
    )
    for iteration in range(ITERS):
        grams = total(*local)
        if iteration + 1 == ITERS:
            break
        (inverse,) = call(inverse_kernel, "inner_inverse", solve_flops, [square], parity, *grams)
        m, image, received = operator(*precondition(w, pieces))
        common = (parity, tables, weight, basis, *grams)
        if iteration == 0:
            p, s, q = z, w, m
            x, r, z, w, t, curvature, *local, pieces = call(
                first_update_kernel,
                "first_update",
                2 * solve_flops,
                [block] * 5 + [square, half_sum, half_sum, share],
                *common,
                z,
                w,
                r,
                m,
                *image,
                *received,
            )
        else:
            x, r, z, w, p, s, q, t, curvature, *local, pieces = call(
                next_update_kernel,
                "next_update",
                2 * solve_flops,
                [block] * 8 + [square, half_sum, half_sum, share],
                *common,
                inner_inverse,
                curvature,
                z,
                w,
                r,
                m,
                p,
                s,
                q,
                t,
                x,
                *image,
                *received,
            )
        inner_inverse = inverse
    x, r = call(
        last_update_kernel,
        "last_update",
        2 * solve_flops,
        [block, block],
        parity,
        *grams,
        inner_inverse,
        curvature,
        z,
        w,
        r,
        p,
        s,
        x,
    )
    return x[None, None], r[None, None]


def solution(mesh):
    placed = (
        P("group", "sub", None, None),
        P("group", "sub", None, None),
        P("group", "sub", None, None),
        P("group", "sub", None, None),
        P("group", "sub", None),
        P("group", "sub", None),
        P("group", "sub", None, None, None),
        P("group", "sub", None),
    )
    return jax.shard_map(
        shards,
        mesh=mesh,
        in_specs=placed,
        out_specs=(P("group", "sub", None, None), P("group", "sub", None, None)),
        check_vma=False,
    )
```

```python
import functools

import jax
import jax.numpy as jnp
from jax import lax
from jax.experimental import pallas as pl
from jax.experimental.pallas import tpu as pltpu
from jax.sharding import PartitionSpec as P

ITERS = 3
TAIL = 16
HIGHEST = lax.Precision.HIGHEST


def swap(x, axis, bit):
    return lax.ppermute(x, axis, [(i, i ^ bit) for i in range(lax.axis_size(axis))])


def bits_of(axis):
    count = lax.axis_size(axis)
    if count & (count - 1):
        raise ValueError("axis size")
    return [1 << b for b in range(count.bit_length() - 1)]


def total(kept, sent):
    half = kept + swap(sent, "group", 1)
    rest = [("group", bit) for bit in bits_of("group")[1:]]
    subs = [("sub", bit) for bit in bits_of("sub")]
    for axis, bit in subs[:1] + rest + subs[1:]:
        half = half + swap(half, axis, bit)
    return half, swap(half, "group", 1)


def gather_sub(x):
    for bit in bits_of("sub"):
        x = jnp.concatenate([x, swap(x, "sub", bit)], axis=0)
    return x


def eliminate(matrix, block, tile=8):
    n, width = matrix.shape[0], block.shape[1]
    sublane = lax.broadcasted_iota(jnp.int32, (tile, 1), 0)
    left = [matrix[i : i + tile] for i in range(0, n, tile)]
    right = [block[i : i + tile] for i in range(0, n, tile)]
    for k in range(n // tile):
        pivot_left, pivot_right = left[k], right[k]
        at = k * tile
        spread = [
            jnp.broadcast_to(pivot_left[:, at + j : at + j + 1], (tile, n)) for j in range(tile)
        ]
        for j in range(tile):
            inverse = 1.0 / spread[j][j : j + 1]
            here = sublane == j
            column = spread[j]

            def cleared(rows, column=column, inverse=inverse, here=here, j=j):
                pivot = rows[j : j + 1] * inverse
                return jnp.where(here, pivot, rows - column * pivot)

            for i in range(j + 1, tile):
                spread[i] = cleared(spread[i])
            pivot_left, pivot_right = cleared(pivot_left), cleared(pivot_right)
        for i in range(n // tile):
            if i == k:
                continue
            old = left[i]
            new_left, new_right = old, right[i]
            for j in range(tile):
                scale = jnp.broadcast_to(old[:, at + j : at + j + 1], (tile, n))
                new_left = new_left - scale * pivot_left[j : j + 1]
                new_right = new_right - scale * pivot_right[j : j + 1]
            left[i], right[i] = new_left, new_right
        left[k], right[k] = pivot_left, pivot_right
    return jnp.concatenate(right, axis=0)


def exact(a, b):
    return jnp.dot(a, b, precision=HIGHEST, preferred_element_type=jnp.float32)


def symmetric(a):
    return (a + a.T) * 0.5


def halves(x):
    high = x.astype(jnp.bfloat16)
    low = (x - high.astype(jnp.float32)).astype(jnp.bfloat16)
    return jnp.concatenate([high, low], axis=1)


def folded(both):
    n = both.shape[1] // 2
    return both[:, :n] + both[:, n:]


def times(matrix, x, contracting=1):
    dims = (((contracting,), (0,)), ((), ()))
    if x.dtype == jnp.bfloat16:
        return lax.dot_general(matrix, x, dims, preferred_element_type=jnp.float32)
    return folded(lax.dot_general(matrix, halves(x), dims, preferred_element_type=jnp.float32))


def mixer(mixing):
    both = halves(mixing)
    return jnp.concatenate([both, both], axis=0)


def mix(block, mixer_value):
    return folded(jnp.dot(halves(block), mixer_value, preferred_element_type=jnp.float32))


def local_gram(weighted, right):
    n = weighted.shape[1]
    both = lax.dot_general(
        halves(weighted),
        halves(right),
        (((0,), (0,)), ((), ())),
        preferred_element_type=jnp.float32,
    )
    both = both[:n] + both[n:]
    return both[:, :n] + both[:, n:]


def packed(inner, cross):
    n = inner.shape[0]
    rows = lax.broadcasted_iota(jnp.int32, (n, n), 0)
    columns = lax.broadcasted_iota(jnp.int32, (n, n), 1)
    body = jnp.where(rows > columns, inner, jnp.where(rows < columns, cross, 0.0))
    tail_rows = lax.broadcasted_iota(jnp.int32, (TAIL, n), 0)
    first = jnp.sum(jnp.where(rows == columns, inner, 0.0), axis=0, keepdims=True)
    second = jnp.sum(jnp.where(rows == columns, cross, 0.0), axis=0, keepdims=True)
    tail = jnp.where(tail_rows == 0, first, jnp.where(tail_rows == 1, second, 0.0))
    return jnp.concatenate([body, tail], axis=0)


def unpacked(grams):
    n = grams.shape[1]
    rows = lax.broadcasted_iota(jnp.int32, (n, n), 0)
    columns = lax.broadcasted_iota(jnp.int32, (n, n), 1)
    body = grams[:n]
    lower = jnp.where(rows > columns, body, 0.0)
    upper = jnp.where(rows < columns, body, 0.0)
    inner = lower + lower.T + jnp.where(rows == columns, grams[n : n + 1], 0.0)
    cross = upper + upper.T + jnp.where(rows == columns, grams[n + 1 : n + 2], 0.0)
    return inner, cross


def zone_of(parity, slot):
    flip = parity[slot // 2]
    return 2 * (slot // 2) + (flip if slot % 2 == 0 else 1 - flip)


def assemble_into(parity, tables, slots, received, out):
    zone = slots[0].shape[0]
    for slot in range(4):
        start = pl.multiple_of(zone_of(parity, slot) * zone, zone)
        value = slots[slot][:zone].astype(jnp.float32) + times(tables[slot], received[slot][:zone])
        out[pl.ds(start, zone)] = value


def slots_from(parity, block, slots):
    zone = slots[0].shape[0]
    for slot in range(4):
        pair = 2 * (slot // 2)
        swapped = parity[slot // 2] == (1 if slot % 2 == 0 else 0)
        low, high = block[pair * zone : (pair + 1) * zone], block[(pair + 1) * zone : (pair + 2) * zone]
        slots[slot][:zone] = jnp.where(swapped, high, low)


def choice_kernel(first, maps, inverse_rows, out):
    count, modes, total_modes = out.shape
    rows_here, coarse_total = inverse_rows.shape
    unknown = lax.broadcasted_iota(jnp.int32, (coarse_total, total_modes), 0)
    columns = (unknown == maps[...]).astype(jnp.float32).astype(jnp.bfloat16)
    picked = jnp.dot(inverse_rows[...], columns, preferred_element_type=jnp.float32)
    here = lax.broadcasted_iota(jnp.int32, (rows_here, total_modes), 0) + first[0]
    rows = (here == maps[...]).astype(jnp.float32).astype(jnp.bfloat16)
    table = lax.dot_general(
        rows,
        picked.astype(jnp.bfloat16),
        (((0,), (0,)), ((), ())),
        preferred_element_type=jnp.float32,
    ).astype(jnp.bfloat16)
    source = lax.broadcasted_iota(jnp.int32, (total_modes, total_modes), 0)
    target = lax.broadcasted_iota(jnp.int32, (total_modes, total_modes), 1)
    for j in range(count):
        order = (source == (target ^ (j * modes))).astype(jnp.float32).astype(jnp.bfloat16)
        block = table[j * modes : (j + 1) * modes]
        out[j] = jnp.dot(block, order, preferred_element_type=jnp.float32).astype(jnp.bfloat16)


def fold_kernel(grams, own, received, out):
    count = own.shape[0] - grams
    if grams:
        out[:grams] = own[:grams] + received[:grams]
    out[grams : grams + count] = own[grams:]
    out[grams + count :] = received[grams:]


def tables_kernel(parity, rows, counts, tables, weight):
    capacity = rows.shape[2]
    place = lax.broadcasted_iota(jnp.int32, (capacity, capacity), 0)
    entry = lax.broadcasted_iota(jnp.int32, (1, capacity), 1)
    for slot in range(4):
        d = zone_of(parity, slot)
        partner_zone = zone_of(parity, slot ^ 1)
        own = rows[0, pl.ds(d, 1)] - d * capacity
        partner = rows[1, pl.ds(d, 1)] - partner_zone * capacity
        own = jnp.where(entry < counts[d], own, -1)
        to = (place == own).astype(jnp.float32).astype(jnp.bfloat16)
        source = (place == partner).astype(jnp.float32).astype(jnp.bfloat16)
        table = lax.dot_general(
            to, source, (((1,), (1,)), ((), ())), preferred_element_type=jnp.float32
        )
        tables[slot] = table.astype(jnp.bfloat16)
        ones = jnp.ones((capacity, weight.shape[1]), jnp.bfloat16)
        shared = jnp.dot(table.astype(jnp.bfloat16), ones, preferred_element_type=jnp.float32)
        weight[pl.ds(pl.multiple_of(d * capacity, capacity), capacity)] = 1.0 / (1.0 + shared)


def start_kernel(parity, tables, weight, basis, *refs):
    slots, received, (block, piece) = refs[:4], refs[4:8], refs[8:]
    assemble_into(parity, tables, slots, received, block)
    piece[...] = times(basis[...], weight[...] * block[...])


def gram_start_kernel(parity, tables, weight, basis, z, r, *refs):
    slots, received, (block, carried) = refs[:4], refs[4:8], refs[8:]
    n = z.shape[1]
    assemble_into(parity, tables, slots, received, block)
    carried[n + TAIL :] = times(basis[...], weight[...] * block[...])
    weighted = weight[...] * z[...]
    carried[: n + TAIL] = packed(local_gram(weighted, r[...]), local_gram(weighted, block[...]))


def local_kernel(weight, matrix, block, out):
    out[...] = times(matrix[...], weight[...] * block[...])


def finish_kernel(grams, parity, weight, basis, chosen, local, own, received, *slots):
    pieces = jnp.concatenate([own[grams:], received[grams:]], axis=0)
    picked = times(chosen[...], pieces)
    smoothed = weight[...] * (local[...] + times(basis[...], picked, contracting=0))
    slots_from(parity, smoothed, slots)
    if grams:
        slots[2][slots[0].shape[0] :] = own[:grams] + received[:grams]


def operator_kernel(parity, tables, matrix, *refs):
    slots, received, block, out = refs[:4], refs[4:8], refs[8], refs[9:13]
    zone = out[0].shape[0]
    assemble_into(parity, tables, slots, received, block)
    slots_from(parity, times(matrix[...], block[...]), out)
    for grams in refs[13:]:
        grams[...] = slots[2][zone:] + received[2][zone:]


def first_update_kernel(parity, tables, weight, basis, grams, z, w, r, m, *refs):
    slots, received = refs[:4], refs[4:8]
    x, r_out, z_out, w_out, image, curvature_out, carried = refs[8:]
    n = z.shape[1]
    assemble_into(parity, tables, slots, received, image)
    inner, cross = unpacked(grams[...])
    curvature_out[...] = cross
    alpha = mixer(eliminate(cross, inner))
    w_new = w[...] - mix(image[...], alpha)
    w_out[...] = w_new
    carried[n + TAIL :] = times(basis[...], weight[...] * w_new)
    x[...] = mix(z[...], alpha)
    r_new = r[...] - mix(w[...], alpha)
    r_out[...] = r_new
    z_new = z[...] - mix(m[...], alpha)
    z_out[...] = z_new
    weighted = weight[...] * z_new
    carried[: n + TAIL] = packed(local_gram(weighted, r_new), local_gram(weighted, w_new))


def step_sizes(grams, inner_inverse, curvature):
    inner, cross = unpacked(grams)
    beta = exact(inner_inverse[...], inner)
    bent = symmetric(cross - exact(beta.T, exact(curvature[...], beta)))
    return beta, bent, eliminate(bent, inner)


def next_update_kernel(
    parity, tables, weight, basis, grams, inner_inverse, curvature,
    z, w, r, m, p, s, q, t, x, *refs
):
    slots, received = refs[:4], refs[4:8]
    (
        x_out, r_out, z_out, w_out, p_out, s_out, q_out, t_out, curvature_out, *carried
    ) = refs[8:]
    assemble_into(parity, tables, slots, received, t_out)
    beta, bent, alpha = step_sizes(grams[...], inner_inverse, curvature)
    curvature_out[...] = bent
    beta, alpha = mixer(beta), mixer(alpha)
    t_out[...] = t_out[...] + mix(t[...], beta)
    w_new = w[...] - mix(t_out[...], alpha)
    w_out[...] = w_new
    p_out[...] = z[...] + mix(p[...], beta)
    s_out[...] = w[...] + mix(s[...], beta)
    q_out[...] = m[...] + mix(q[...], beta)
    x_out[...] = x[...] + mix(p_out[...], alpha)
    r_new = r[...] - mix(s_out[...], alpha)
    r_out[...] = r_new
    z_new = z[...] - mix(q_out[...], alpha)
    z_out[...] = z_new
    weighted = weight[...] * z_new
    sums = packed(local_gram(weighted, r_new), local_gram(weighted, w_new))
    if len(carried) == 1:
        rows = sums.shape[0]
        carried[0][:rows] = sums
        carried[0][rows:] = times(basis[...], weight[...] * w_new)
    else:
        kept, sent = carried
        low, high = sums[: kept.shape[0]], sums[kept.shape[0] :]
        kept[...] = jnp.where(parity[1] == 0, low, high)
        sent[...] = jnp.where(parity[1] == 0, high, low)


def last_update_kernel(parity, half, other, inner_inverse, curvature, z, w, r, p, s, x, x_out, r_out):
    low = jnp.where(parity[1] == 0, half[...], other[...])
    high = jnp.where(parity[1] == 0, other[...], half[...])
    sums = jnp.concatenate([low, high], axis=0)
    beta, _, alpha = step_sizes(sums, inner_inverse, curvature)
    beta, alpha = mixer(beta), mixer(alpha)
    x_out[...] = x[...] + mix(z[...] + mix(p[...], beta), alpha)
    r_out[...] = r[...] - mix(w[...] + mix(s[...], beta), alpha)


def inverse_kernel(grams, out):
    n = out.shape[0]
    rows = lax.broadcasted_iota(jnp.int32, (n, n), 0)
    columns = lax.broadcasted_iota(jnp.int32, (n, n), 1)
    inner, _ = unpacked(grams[...])
    out[...] = eliminate(inner, (rows == columns).astype(jnp.float32))


VMEM = pl.BlockSpec(memory_space=pltpu.VMEM)
SMEM = pl.BlockSpec(memory_space=pltpu.SMEM)


def call(kernel, name, flops, outs, *args):
    shapes = [jax.ShapeDtypeStruct(shape, dtype) for shape, dtype in outs]
    moved = sum(a.size * a.dtype.itemsize for a in (*args, *shapes))
    return pl.pallas_call(
        kernel,
        out_shape=shapes,
        in_specs=[SMEM if a.ndim == 1 else VMEM for a in args],
        out_specs=[VMEM] * len(shapes),
        name=name,
        compiler_params=pltpu.CompilerParams(vmem_limit_bytes=24 * 1024 * 1024),
        cost_estimate=pl.CostEstimate(flops=flops, bytes_accessed=moved, transcendentals=0),
    )(*args)


def pairs(axis, first):
    count = lax.axis_size(axis)
    low = range(first, count - 1, 2)
    return [(i, i + 1) for i in low] + [(i + 1, i) for i in low]


def exchange(slots):
    return [
        lax.ppermute(slot, axis, pairs(axis, first))
        for slot, (axis, first) in zip(
            slots, (("sub", 0), ("sub", 1), ("group", 0), ("group", 1))
        )
    ]


def shards(
    schur, local_inverse, rhs_parts, basis, coarse_map, coarse_inverse, shared_rows, shared_counts
):
    schur, local_inverse, basis = schur[0, 0], local_inverse[0, 0], basis[0, 0]
    rhs = rhs_parts[0, 0]
    rows, columns = rhs.shape
    zone = shared_rows.shape[-1]
    modes = basis.shape[0]
    parity = jnp.stack([lax.axis_index("sub") % 2, lax.axis_index("group") % 2]).astype(jnp.int32)
    block = ((rows, columns), jnp.float32)
    part = ((zone, columns), jnp.float32)
    square = ((columns, columns), jnp.float32)
    sums = columns + TAIL
    share = ((modes, columns), jnp.float32)
    carry = ((sums + modes, columns), jnp.float32)
    halves_out = [((sums // 2, columns), jnp.float32)] * 2
    solve_flops = 400_000_000
    product_flops = 4 * rows * rows * columns

    def rhs_zone(slot):
        return lax.dynamic_slice_in_dim(rhs, zone_of(parity, slot) * zone, zone, axis=0)

    rhs_slots = [rhs_zone(slot) for slot in range(4)]
    received = exchange(rhs_slots)
    tables, weight = call(
        tables_kernel,
        "shared_row_tables",
        16 * zone**3,
        [((4, zone, zone), jnp.bfloat16), block],
        parity,
        shared_rows[0, 0],
        shared_counts[0, 0],
    )
    subs = lax.axis_size("sub")
    inverse_rows = coarse_inverse[0]
    (chosen,) = call(
        choice_kernel,
        "selected_inverse",
        product_flops // 4,
        [((subs, modes, subs * modes), jnp.bfloat16)],
        (lax.axis_index("sub") * inverse_rows.shape[0]).astype(jnp.int32)[None],
        gather_sub(coarse_map[0, 0])[None],
        inverse_rows,
    )
    for bit in reversed(bits_of("sub")):
        chosen = chosen[:bit] + swap(chosen[bit:], "sub", bit)
    chosen = chosen[0]

    def precondition(vector, carried):
        grams = carried.shape[0] - modes
        (local,) = call(
            local_kernel, "local_inverse", product_flops, [block], weight, local_inverse, vector
        )
        bits = bits_of("sub")
        for bit in bits[:-1]:
            rows_out = 2 * carried.shape[0] - grams
            (carried,) = call(
                functools.partial(fold_kernel, grams),
                "fold",
                columns * rows_out,
                [((rows_out, columns), jnp.float32)],
                carried,
                swap(carried, "sub", bit),
            )
        slots = call(
            functools.partial(finish_kernel, grams),
            "coarse_part",
            product_flops // 8,
            [part, part, ((zone + grams, columns), jnp.float32), part],
            parity,
            weight,
            basis,
            chosen,
            local,
            carried,
            swap(carried, "sub", bits[-1]),
        )
        return slots, exchange(slots)

    def operator(slots, received):
        grams = slots[2].shape[0] - zone
        outs = [((grams, columns), jnp.float32)] if grams else []
        vector, *image = call(
            operator_kernel,
            "operator",
            product_flops,
            [block] + [part] * 4 + outs,
            parity,
            tables,
            schur,
            *slots,
            *received,
        )
        whole = image[4:]
        for bit in bits_of("group")[1:] if grams else ():
            whole = [whole[0] + swap(whole[0], "group", bit)]
        return vector, image[:4], exchange(image[:4]), *whole

    r, pieces = call(
        start_kernel,
        "start",
        product_flops // 8,
        [block, share],
        parity,
        tables,
        weight,
        basis,
        *rhs_slots,
        *received,
    )
    z, image, received = operator(*precondition(r, pieces))
    w, carried = call(
        gram_start_kernel,
        "start_grams",
        product_flops // 4,
        [block, carry],
        parity,
        tables,
        weight,
        basis,
        z,
        r,
        *image,
        *received,
    )
    for iteration in range(ITERS - 1):
        final = iteration + 2 == ITERS
        m, image, received, grams = operator(*precondition(w, carried))
        common = (parity, tables, weight, basis, grams)
        if iteration == 0:
            p, s, q = z, w, m
            x, r, z, w, t, curvature, carried = call(
                first_update_kernel,
                "first_update",
                2 * solve_flops,
                [block] * 5 + [square, carry],
                *common,
                z,
                w,
                r,
                m,
                *image,
                *received,
            )
        else:
            x, r, z, w, p, s, q, t, curvature, *carried = call(
                next_update_kernel,
                "next_update",
                2 * solve_flops,
                [block] * 8 + [square] + (halves_out if final else [carry]),
                *common,
                inner_inverse,
                curvature,
                z,
                w,
                r,
                m,
                p,
                s,
                q,
                t,
                x,
                *image,
                *received,
            )
            if not final:
                (carried,) = carried
        grams, curvature = lax.optimization_barrier((grams, curvature))
        (inner_inverse,) = call(inverse_kernel, "inner_inverse", solve_flops, [square], grams)
    grams = total(*carried)
    x, r = call(
        last_update_kernel,
        "last_update",
        2 * solve_flops,
        [block, block],
        parity,
        *grams,
        inner_inverse,
        curvature,
        z,
        w,
        r,
        p,
        s,
        x,
    )
    return x[None, None], r[None, None]


def solution(mesh):
    placed = (
        P("group", "sub", None, None),
        P("group", "sub", None, None),
        P("group", "sub", None, None),
        P("group", "sub", None, None),
        P("group", "sub", None),
        P("group", "sub", None),
        P("group", "sub", None, None, None),
        P("group", "sub", None),
    )
    return jax.shard_map(
        shards,
        mesh=mesh,
        in_specs=placed,
        out_specs=(P("group", "sub", None, None), P("group", "sub", None, None)),
        check_vma=False,
    )
```

```python
import functools

import jax
import jax.numpy as jnp
from jax import lax
from jax.experimental import pallas as pl
from jax.experimental.pallas import tpu as pltpu
from jax.sharding import PartitionSpec as P

ITERS = 3
TAIL = 16
HIGHEST = lax.Precision.HIGHEST


def swap(x, axis, bit):
    return lax.ppermute(x, axis, [(i, i ^ bit) for i in range(lax.axis_size(axis))])


def bits_of(axis):
    count = lax.axis_size(axis)
    if count & (count - 1):
        raise ValueError("axis size")
    return [1 << b for b in range(count.bit_length() - 1)]


def total(kept, sent, ride):
    half = kept + swap(sent, "group", 1)
    rest = [("group", bit) for bit in bits_of("group")[1:]]
    subs = [("sub", bit) for bit in bits_of("sub")]
    for number, (axis, bit) in enumerate(subs[:1] + rest + subs[1:]):
        arrived = swap(half, axis, bit)
        if number == 1:
            arrived, ride = lax.optimization_barrier((arrived, ride))
        half = half + arrived
    return half, swap(half, "group", 1), ride


def gather_sub(x):
    for bit in bits_of("sub"):
        x = jnp.concatenate([x, swap(x, "sub", bit)], axis=0)
    return x


def eliminate(matrix, block, tile=8):
    n, width = matrix.shape[0], block.shape[1]
    sublane = lax.broadcasted_iota(jnp.int32, (tile, 1), 0)
    left = [matrix[i : i + tile] for i in range(0, n, tile)]
    right = [block[i : i + tile] for i in range(0, n, tile)]
    for k in range(n // tile):
        pivot_left, pivot_right = left[k], right[k]
        at = k * tile
        spread = [
            jnp.broadcast_to(pivot_left[:, at + j : at + j + 1], (tile, n)) for j in range(tile)
        ]
        for j in range(tile):
            inverse = 1.0 / spread[j][j : j + 1]
            here = sublane == j
            column = spread[j]

            def cleared(rows, column=column, inverse=inverse, here=here, j=j):
                pivot = rows[j : j + 1] * inverse
                return jnp.where(here, pivot, rows - column * pivot)

            for i in range(j + 1, tile):
                spread[i] = cleared(spread[i])
            pivot_left, pivot_right = cleared(pivot_left), cleared(pivot_right)
        for i in range(n // tile):
            if i == k:
                continue
            old = left[i]
            new_left, new_right = old, right[i]
            for j in range(tile):
                scale = jnp.broadcast_to(old[:, at + j : at + j + 1], (tile, n))
                new_left = new_left - scale * pivot_left[j : j + 1]
                new_right = new_right - scale * pivot_right[j : j + 1]
            left[i], right[i] = new_left, new_right
        left[k], right[k] = pivot_left, pivot_right
    return jnp.concatenate(right, axis=0)


def exact(a, b):
    return jnp.dot(a, b, precision=HIGHEST, preferred_element_type=jnp.float32)


def symmetric(a):
    return (a + a.T) * 0.5


def halves(x):
    high = x.astype(jnp.bfloat16)
    low = (x - high.astype(jnp.float32)).astype(jnp.bfloat16)
    return jnp.concatenate([high, low], axis=1)


def folded(both):
    n = both.shape[1] // 2
    return both[:, :n] + both[:, n:]


def times(matrix, x, contracting=1):
    dims = (((contracting,), (0,)), ((), ()))
    if x.dtype == jnp.bfloat16:
        return lax.dot_general(matrix, x, dims, preferred_element_type=jnp.float32)
    return folded(lax.dot_general(matrix, halves(x), dims, preferred_element_type=jnp.float32))


def mixer(mixing):
    both = halves(mixing)
    return jnp.concatenate([both, both], axis=0)


def mix(block, mixer_value):
    return folded(jnp.dot(halves(block), mixer_value, preferred_element_type=jnp.float32))


def local_gram(weighted, right):
    n = weighted.shape[1]
    both = lax.dot_general(
        halves(weighted),
        halves(right),
        (((0,), (0,)), ((), ())),
        preferred_element_type=jnp.float32,
    )
    both = both[:n] + both[n:]
    return both[:, :n] + both[:, n:]


def packed(inner, cross):
    n = inner.shape[0]
    rows = lax.broadcasted_iota(jnp.int32, (n, n), 0)
    columns = lax.broadcasted_iota(jnp.int32, (n, n), 1)
    body = jnp.where(rows > columns, inner, jnp.where(rows < columns, cross, 0.0))
    tail_rows = lax.broadcasted_iota(jnp.int32, (TAIL, n), 0)
    first = jnp.sum(jnp.where(rows == columns, inner, 0.0), axis=0, keepdims=True)
    second = jnp.sum(jnp.where(rows == columns, cross, 0.0), axis=0, keepdims=True)
    tail = jnp.where(tail_rows == 0, first, jnp.where(tail_rows == 1, second, 0.0))
    return jnp.concatenate([body, tail], axis=0)


def unpacked(grams):
    n = grams.shape[1]
    rows = lax.broadcasted_iota(jnp.int32, (n, n), 0)
    columns = lax.broadcasted_iota(jnp.int32, (n, n), 1)
    body = grams[:n]
    lower = jnp.where(rows > columns, body, 0.0)
    upper = jnp.where(rows < columns, body, 0.0)
    inner = lower + lower.T + jnp.where(rows == columns, grams[n : n + 1], 0.0)
    cross = upper + upper.T + jnp.where(rows == columns, grams[n + 1 : n + 2], 0.0)
    return inner, cross


def zone_of(parity, slot):
    flip = parity[slot // 2]
    return 2 * (slot // 2) + (flip if slot % 2 == 0 else 1 - flip)


def assemble_into(parity, tables, slots, received, out):
    zone = tables.shape[1]
    for slot in range(4):
        start = pl.multiple_of(zone_of(parity, slot) * zone, zone)
        value = slots[slot][:zone].astype(jnp.float32) + times(tables[slot], received[slot][:zone])
        out[pl.ds(start, zone)] = value


def slots_from(parity, block, slots):
    zone = slots[3].shape[0]
    for slot in range(4):
        pair = 2 * (slot // 2)
        swapped = parity[slot // 2] == (1 if slot % 2 == 0 else 0)
        low, high = block[pair * zone : (pair + 1) * zone], block[(pair + 1) * zone : (pair + 2) * zone]
        slots[slot][:zone] = jnp.where(swapped, high, low)


def choice_kernel(first, maps, inverse_rows, out):
    count, modes, total_modes = out.shape
    rows_here, coarse_total = inverse_rows.shape
    unknown = lax.broadcasted_iota(jnp.int32, (coarse_total, total_modes), 0)
    columns = (unknown == maps[...]).astype(jnp.float32).astype(jnp.bfloat16)
    picked = jnp.dot(inverse_rows[...], columns, preferred_element_type=jnp.float32)
    here = lax.broadcasted_iota(jnp.int32, (rows_here, total_modes), 0) + first[0]
    rows = (here == maps[...]).astype(jnp.float32).astype(jnp.bfloat16)
    table = lax.dot_general(
        rows,
        picked.astype(jnp.bfloat16),
        (((0,), (0,)), ((), ())),
        preferred_element_type=jnp.float32,
    ).astype(jnp.bfloat16)
    source = lax.broadcasted_iota(jnp.int32, (total_modes, total_modes), 0)
    target = lax.broadcasted_iota(jnp.int32, (total_modes, total_modes), 1)
    for j in range(count):
        order = (source == (target ^ (j * modes))).astype(jnp.float32).astype(jnp.bfloat16)
        block = table[j * modes : (j + 1) * modes]
        out[j] = jnp.dot(block, order, preferred_element_type=jnp.float32).astype(jnp.bfloat16)


def fold_kernel(grams, own, received, out):
    count = own.shape[0] - grams
    if grams:
        out[:grams] = own[:grams] + received[:grams]
    out[grams : grams + count] = own[grams:]
    out[grams + count :] = received[grams:]


def tables_kernel(parity, rows, counts, tables, weight):
    capacity = rows.shape[2]
    place = lax.broadcasted_iota(jnp.int32, (capacity, capacity), 0)
    entry = lax.broadcasted_iota(jnp.int32, (1, capacity), 1)
    for slot in range(4):
        d = zone_of(parity, slot)
        partner_zone = zone_of(parity, slot ^ 1)
        own = rows[0, pl.ds(d, 1)] - d * capacity
        partner = rows[1, pl.ds(d, 1)] - partner_zone * capacity
        own = jnp.where(entry < counts[d], own, -1)
        to = (place == own).astype(jnp.float32).astype(jnp.bfloat16)
        source = (place == partner).astype(jnp.float32).astype(jnp.bfloat16)
        table = lax.dot_general(
            to, source, (((1,), (1,)), ((), ())), preferred_element_type=jnp.float32
        )
        tables[slot] = table.astype(jnp.bfloat16)
        ones = jnp.ones((capacity, weight.shape[1]), jnp.bfloat16)
        shared = jnp.dot(table.astype(jnp.bfloat16), ones, preferred_element_type=jnp.float32)
        weight[pl.ds(pl.multiple_of(d * capacity, capacity), capacity)] = 1.0 / (1.0 + shared)


def start_kernel(parity, tables, weight, basis, *refs):
    slots, received, (block, piece) = refs[:4], refs[4:8], refs[8:]
    assemble_into(parity, tables, slots, received, block)
    piece[...] = times(basis[...], weight[...] * block[...])


def gram_start_kernel(parity, tables, weight, basis, z, r, *refs):
    slots, received, (block, carried) = refs[:4], refs[4:8], refs[8:]
    n = z.shape[1]
    assemble_into(parity, tables, slots, received, block)
    carried[n + TAIL :] = times(basis[...], weight[...] * block[...])
    weighted = weight[...] * z[...]
    carried[: n + TAIL] = packed(local_gram(weighted, r[...]), local_gram(weighted, block[...]))


def send_kernel(parity, rhs, basis, *slots):
    zone, columns = slots[3].shape
    slots_from(parity, rhs[...], slots)
    modes = basis.shape[0]
    for slot in range(2):
        for part in range(zone // columns):
            at = part * columns
            low, high = basis[:, at : at + columns], basis[:, zone + at : zone + at + columns]
            chosen = jnp.where(parity[0] == slot, low, high)
            slots[slot][zone + part * modes : zone + (part + 1) * modes] = chosen


def neighbour_kernel(shift, tables, chosen, first, second, first_zone, second_zone, rows, columns):
    modes, total_modes = chosen.shape
    zone, width = tables.shape[1], first_zone.shape[1]
    source = lax.broadcasted_iota(jnp.int32, (total_modes, total_modes), 0)
    target = lax.broadcasted_iota(jnp.int32, (total_modes, total_modes), 1)
    rows[:modes] = chosen[...]
    for slot, (theirs, below) in enumerate(((first, first_zone), (second, second_zone))):
        order = (source == (target ^ shift[slot])).astype(jnp.float32).astype(jnp.bfloat16)
        ordered = jnp.dot(theirs[...], order, preferred_element_type=jnp.float32)
        rows[(slot + 1) * modes : (slot + 2) * modes] = ordered.astype(jnp.bfloat16)
        basis = jnp.concatenate(
            [
                below[zone + part * modes : zone + (part + 1) * modes]
                for part in range(zone // width)
            ],
            axis=1,
        )
        columns[slot] = lax.dot_general(
            basis, tables[slot], (((1,), (1,)), ((), ())), preferred_element_type=jnp.float32
        ).astype(jnp.bfloat16)


def local_kernel(parity, weight, matrix, block, out, *early):
    zone = early[0].shape[0]
    out[...] = weight[...] * times(matrix[...], weight[...] * block[...])
    low, high = out[:zone], out[zone : 2 * zone]
    early[0][...] = jnp.where(parity[0] == 0, low, high)
    early[1][...] = jnp.where(parity[0] == 0, high, low)


def finish_kernel(
    grams, parity, weight, basis, chosen, near, local, own, received, *slots
):
    modes, zone = basis.shape[0], slots[0].shape[0]
    pieces = jnp.concatenate([own[grams:], received[grams:]], axis=0)
    picked = times(chosen[...], pieces)
    smoothed = local[...] + weight[...] * times(basis[...], picked[:modes], contracting=0)
    slots_from(parity, smoothed, slots)
    for slot in range(2):
        start = pl.multiple_of(zone_of(parity, slot) * zone, zone)
        theirs = times(near[slot], picked[(slot + 1) * modes : (slot + 2) * modes], contracting=0)
        slots[slot][...] = slots[slot][...] + weight[pl.ds(start, zone)] * theirs
    if grams:
        slots[2][zone:] = own[:grams] + received[:grams]


def operator_kernel(parity, tables, matrix, *refs):
    slots, received, block, out = refs[:4], refs[4:8], refs[8], refs[9:13]
    zone = out[0].shape[0]
    assemble_into(parity, tables, slots, received, block)
    slots_from(parity, times(matrix[...], block[...]), out)
    for grams in refs[13:]:
        grams[...] = slots[2][zone:] + received[2][zone:]


def first_update_kernel(parity, tables, weight, basis, grams, z, w, r, m, *refs):
    slots, received = refs[:4], refs[4:8]
    x, r_out, z_out, w_out, image, curvature_out, carried = refs[8:]
    n = z.shape[1]
    assemble_into(parity, tables, slots, received, image)
    inner, cross = unpacked(grams[...])
    curvature_out[...] = cross
    alpha = mixer(eliminate(cross, inner))
    w_new = w[...] - mix(image[...], alpha)
    w_out[...] = w_new
    carried[n + TAIL :] = times(basis[...], weight[...] * w_new)
    x[...] = mix(z[...], alpha)
    r_new = r[...] - mix(w[...], alpha)
    r_out[...] = r_new
    z_new = z[...] - mix(m[...], alpha)
    z_out[...] = z_new
    weighted = weight[...] * z_new
    carried[: n + TAIL] = packed(local_gram(weighted, r_new), local_gram(weighted, w_new))


def step_sizes(grams, inner_inverse, curvature):
    inner, cross = unpacked(grams)
    beta = exact(inner_inverse[...], inner)
    bent = symmetric(cross - exact(beta.T, exact(curvature[...], beta)))
    return beta, bent, eliminate(bent, inner)


def next_update_kernel(
    parity, tables, weight, basis, grams, inner_inverse, curvature,
    z, w, r, m, p, s, q, t, x, *refs
):
    slots, received = refs[:4], refs[4:8]
    (
        x_out, r_out, z_out, w_out, p_out, s_out, q_out, t_out, curvature_out, *carried
    ) = refs[8:]
    assemble_into(parity, tables, slots, received, t_out)
    beta, bent, alpha = step_sizes(grams[...], inner_inverse, curvature)
    curvature_out[...] = bent
    beta, alpha = mixer(beta), mixer(alpha)
    t_out[...] = t_out[...] + mix(t[...], beta)
    w_new = w[...] - mix(t_out[...], alpha)
    w_out[...] = w_new
    p_out[...] = z[...] + mix(p[...], beta)
    s_out[...] = w[...] + mix(s[...], beta)
    q_out[...] = m[...] + mix(q[...], beta)
    x_out[...] = x[...] + mix(p_out[...], alpha)
    r_new = r[...] - mix(s_out[...], alpha)
    r_out[...] = r_new
    z_new = z[...] - mix(q_out[...], alpha)
    z_out[...] = z_new
    weighted = weight[...] * z_new
    sums = packed(local_gram(weighted, r_new), local_gram(weighted, w_new))
    if len(carried) == 1:
        rows = sums.shape[0]
        carried[0][:rows] = sums
        carried[0][rows:] = times(basis[...], weight[...] * w_new)
    else:
        kept, sent = carried
        low, high = sums[: kept.shape[0]], sums[kept.shape[0] :]
        kept[...] = jnp.where(parity[1] == 0, low, high)
        sent[...] = jnp.where(parity[1] == 0, high, low)


def last_update_kernel(parity, half, other, inner_inverse, curvature, z, w, r, p, s, x, x_out, r_out):
    low = jnp.where(parity[1] == 0, half[...], other[...])
    high = jnp.where(parity[1] == 0, other[...], half[...])
    sums = jnp.concatenate([low, high], axis=0)
    beta, _, alpha = step_sizes(sums, inner_inverse, curvature)
    beta, alpha = mixer(beta), mixer(alpha)
    x_out[...] = x[...] + mix(z[...] + mix(p[...], beta), alpha)
    r_out[...] = r[...] - mix(w[...] + mix(s[...], beta), alpha)


def inverse_kernel(grams, out):
    n = out.shape[0]
    rows = lax.broadcasted_iota(jnp.int32, (n, n), 0)
    columns = lax.broadcasted_iota(jnp.int32, (n, n), 1)
    inner, _ = unpacked(grams[...])
    out[...] = eliminate(inner, (rows == columns).astype(jnp.float32))


VMEM = pl.BlockSpec(memory_space=pltpu.VMEM)
SMEM = pl.BlockSpec(memory_space=pltpu.SMEM)


def call(kernel, name, flops, outs, *args):
    shapes = [jax.ShapeDtypeStruct(shape, dtype) for shape, dtype in outs]
    moved = sum(a.size * a.dtype.itemsize for a in (*args, *shapes))
    return pl.pallas_call(
        kernel,
        out_shape=shapes,
        in_specs=[SMEM if a.ndim == 1 else VMEM for a in args],
        out_specs=[VMEM] * len(shapes),
        name=name,
        compiler_params=pltpu.CompilerParams(vmem_limit_bytes=24 * 1024 * 1024),
        cost_estimate=pl.CostEstimate(flops=flops, bytes_accessed=moved, transcendentals=0),
    )(*args)


def pairs(axis, first):
    count = lax.axis_size(axis)
    low = range(first, count - 1, 2)
    return [(i, i + 1) for i in low] + [(i + 1, i) for i in low]


def exchange(slots, first=0):
    patterns = (("sub", 0), ("sub", 1), ("group", 0), ("group", 1))
    return [
        lax.ppermute(slot, axis, pairs(axis, low))
        for slot, (axis, low) in zip(slots, patterns[first:])
    ]


def shards(
    schur, local_inverse, rhs_parts, basis, coarse_map, coarse_inverse, shared_rows, shared_counts
):
    schur, local_inverse, basis = schur[0, 0], local_inverse[0, 0], basis[0, 0]
    rhs = rhs_parts[0, 0]
    rows, columns = rhs.shape
    zone = shared_rows.shape[-1]
    modes = basis.shape[0]
    parity = jnp.stack([lax.axis_index("sub") % 2, lax.axis_index("group") % 2]).astype(jnp.int32)
    block = ((rows, columns), jnp.float32)
    part = ((zone, columns), jnp.float32)
    square = ((columns, columns), jnp.float32)
    sums = columns + TAIL
    share = ((modes, columns), jnp.float32)
    carry = ((sums + modes, columns), jnp.float32)
    halves_out = [((sums // 2, columns), jnp.float32)] * 2
    solve_flops = 400_000_000
    product_flops = 4 * rows * rows * columns

    low_part = ((zone, columns), jnp.bfloat16)
    long_part = ((zone + modes * (zone // columns), columns), jnp.bfloat16)
    rhs_slots = call(
        send_kernel,
        "first_zones",
        rows * columns,
        [long_part, long_part, low_part, low_part],
        parity,
        rhs,
        basis,
    )
    received = exchange(rhs_slots)
    tables, weight = call(
        tables_kernel,
        "shared_row_tables",
        16 * zone**3,
        [((4, zone, zone), jnp.bfloat16), block],
        parity,
        shared_rows[0, 0],
        shared_counts[0, 0],
    )
    subs = lax.axis_size("sub")
    inverse_rows = coarse_inverse[0]
    (chosen,) = call(
        choice_kernel,
        "selected_inverse",
        product_flops // 4,
        [((subs, modes, subs * modes), jnp.bfloat16)],
        (lax.axis_index("sub") * inverse_rows.shape[0]).astype(jnp.int32)[None],
        gather_sub(coarse_map[0, 0])[None],
        inverse_rows,
    )
    for bit in reversed(bits_of("sub")):
        chosen = chosen[:bit] + swap(chosen[bit:], "sub", bit)
    chosen = chosen[0]
    me = lax.axis_index("sub")
    across = jnp.stack([me ^ (me ^ 1), me ^ (((me + 1) ^ 1) - 1)]) & (subs - 1)
    chosen, near = call(
        neighbour_kernel,
        "neighbours",
        product_flops // 16,
        [((3 * modes, subs * modes), jnp.bfloat16), ((2, modes, zone), jnp.bfloat16)],
        (across * modes).astype(jnp.int32),
        tables,
        chosen,
        *exchange([chosen, chosen]),
        *received[:2],
    )

    def precondition(vector, carried, ride=None):
        grams = carried.shape[0] - modes
        local, *early = call(
            local_kernel,
            "local_inverse",
            product_flops,
            [block, part, part],
            parity,
            weight,
            local_inverse,
            vector,
        )
        early = exchange(early)
        bits = bits_of("sub")
        for bit in bits[:-1]:
            rows_out = 2 * carried.shape[0] - grams
            arrived = swap(carried, "sub", bit)
            if ride is not None and bit == bits[0]:
                arrived, ride = lax.optimization_barrier((arrived, ride))
            (carried,) = call(
                functools.partial(fold_kernel, grams),
                "fold",
                columns * rows_out,
                [((rows_out, columns), jnp.float32)],
                carried,
                arrived,
            )
        slots = call(
            functools.partial(finish_kernel, grams),
            "coarse_part",
            product_flops // 8,
            [part, part, ((zone + grams, columns), jnp.float32), part],
            parity,
            weight,
            basis,
            chosen,
            near,
            local,
            carried,
            swap(carried, "sub", bits[-1]),
        )
        return slots, early + exchange(slots[2:], 2), ride

    def operator(slots, received):
        grams = slots[2].shape[0] - zone
        outs = [((grams, columns), jnp.float32)] if grams else []
        vector, *image = call(
            operator_kernel,
            "operator",
            product_flops,
            [block] + [part] * 4 + outs,
            parity,
            tables,
            schur,
            *slots,
            *received,
        )
        whole = image[4:]
        for bit in bits_of("group")[1:] if grams else ():
            whole = [whole[0] + swap(whole[0], "group", bit)]
        return vector, image[:4], exchange(image[:4]), *whole

    r, pieces = call(
        start_kernel,
        "start",
        product_flops // 8,
        [block, share],
        parity,
        tables,
        weight,
        basis,
        *rhs_slots,
        *received,
    )
    slots, received, _ = precondition(r, pieces)
    z, image, received = operator(slots, received)
    w, carried = call(
        gram_start_kernel,
        "start_grams",
        product_flops // 4,
        [block, carry],
        parity,
        tables,
        weight,
        basis,
        z,
        r,
        *image,
        *received,
    )
    ride = None
    for iteration in range(ITERS - 1):
        final = iteration + 2 == ITERS
        slots, received, inner_inverse = precondition(w, carried, ride)
        m, image, received, grams = operator(slots, received)
        common = (parity, tables, weight, basis, grams)
        if iteration == 0:
            p, s, q = z, w, m
            x, r, z, w, t, curvature, carried = call(
                first_update_kernel,
                "first_update",
                2 * solve_flops,
                [block] * 5 + [square, carry],
                *common,
                z,
                w,
                r,
                m,
                *image,
                *received,
            )
        else:
            x, r, z, w, p, s, q, t, curvature, *carried = call(
                next_update_kernel,
                "next_update",
                2 * solve_flops,
                [block] * 8 + [square] + (halves_out if final else [carry]),
                *common,
                inner_inverse,
                curvature,
                z,
                w,
                r,
                m,
                p,
                s,
                q,
                t,
                x,
                *image,
                *received,
            )
            if not final:
                (carried,) = carried
        grams, curvature = lax.optimization_barrier((grams, curvature))
        (ride,) = call(inverse_kernel, "inner_inverse", solve_flops, [square], grams)
    *grams, inner_inverse = total(*carried, ride)
    x, r = call(
        last_update_kernel,
        "last_update",
        2 * solve_flops,
        [block, block],
        parity,
        *grams,
        inner_inverse,
        curvature,
        z,
        w,
        r,
        p,
        s,
        x,
    )
    return x[None, None], r[None, None]


def solution(mesh):
    placed = (
        P("group", "sub", None, None),
        P("group", "sub", None, None),
        P("group", "sub", None, None),
        P("group", "sub", None, None),
        P("group", "sub", None),
        P("group", "sub", None),
        P("group", "sub", None, None, None),
        P("group", "sub", None),
    )
    return jax.shard_map(
        shards,
        mesh=mesh,
        in_specs=placed,
        out_specs=(P("group", "sub", None, None), P("group", "sub", None, None)),
        check_vma=False,
    )
```

```python
import functools

import jax
import jax.numpy as jnp
from jax import lax
from jax.experimental import pallas as pl
from jax.experimental.pallas import tpu as pltpu
from jax.sharding import PartitionSpec as P

ITERS = 3
TAIL = 16
HIGHEST = lax.Precision.HIGHEST


def swap(x, axis, bit):
    return lax.ppermute(x, axis, [(i, i ^ bit) for i in range(lax.axis_size(axis))])


def bits_of(axis):
    count = lax.axis_size(axis)
    if count & (count - 1):
        raise ValueError("axis size")
    return [1 << b for b in range(count.bit_length() - 1)]


def total(kept, sent, ride):
    half = kept + swap(sent, "group", 1)
    rest = [("group", bit) for bit in bits_of("group")[1:]]
    subs = [("sub", bit) for bit in bits_of("sub")]
    for number, (axis, bit) in enumerate(subs[:1] + rest + subs[1:]):
        arrived = swap(half, axis, bit)
        if number == 1:
            arrived, ride = lax.optimization_barrier((arrived, ride))
        half = half + arrived
    return half, swap(half, "group", 1), ride


def gather_sub(x, *rides):
    rides = list(rides)
    for number, bit in enumerate(bits_of("sub")):
        arrived = swap(x, "sub", bit)
        if number < len(rides):
            arrived, rides[number] = lax.optimization_barrier((arrived, rides[number]))
        x = jnp.concatenate([x, arrived], axis=0)
    return x, rides


def eliminate(matrix, block, tile=8):
    n, width = matrix.shape[0], block.shape[1]
    sublane = lax.broadcasted_iota(jnp.int32, (tile, 1), 0)
    left = [matrix[i : i + tile] for i in range(0, n, tile)]
    right = [block[i : i + tile] for i in range(0, n, tile)]
    for k in range(n // tile):
        pivot_left, pivot_right = left[k], right[k]
        at = k * tile
        spread = [
            jnp.broadcast_to(pivot_left[:, at + j : at + j + 1], (tile, n)) for j in range(tile)
        ]
        for j in range(tile):
            inverse = 1.0 / spread[j][j : j + 1]
            here = sublane == j
            column = spread[j]

            def cleared(rows, column=column, inverse=inverse, here=here, j=j):
                pivot = rows[j : j + 1] * inverse
                return jnp.where(here, pivot, rows - column * pivot)

            for i in range(j + 1, tile):
                spread[i] = cleared(spread[i])
            pivot_left, pivot_right = cleared(pivot_left), cleared(pivot_right)
        for i in range(n // tile):
            if i == k:
                continue
            old = left[i]
            new_left, new_right = old, right[i]
            for j in range(tile):
                scale = jnp.broadcast_to(old[:, at + j : at + j + 1], (tile, n))
                new_left = new_left - scale * pivot_left[j : j + 1]
                new_right = new_right - scale * pivot_right[j : j + 1]
            left[i], right[i] = new_left, new_right
        left[k], right[k] = pivot_left, pivot_right
    return jnp.concatenate(right, axis=0)


def exact(a, b):
    return jnp.dot(a, b, precision=HIGHEST, preferred_element_type=jnp.float32)


def symmetric(a):
    return (a + a.T) * 0.5


def halves(x):
    high = x.astype(jnp.bfloat16)
    low = (x - high.astype(jnp.float32)).astype(jnp.bfloat16)
    return jnp.concatenate([high, low], axis=1)


def folded(both):
    n = both.shape[1] // 2
    return both[:, :n] + both[:, n:]


def times(matrix, x, contracting=1):
    dims = (((contracting,), (0,)), ((), ()))
    if x.dtype == jnp.bfloat16:
        return lax.dot_general(matrix, x, dims, preferred_element_type=jnp.float32)
    return folded(lax.dot_general(matrix, halves(x), dims, preferred_element_type=jnp.float32))


def mixer(mixing):
    both = halves(mixing)
    return jnp.concatenate([both, both], axis=0)


def mix(block, mixer_value):
    return folded(jnp.dot(halves(block), mixer_value, preferred_element_type=jnp.float32))


def local_gram(weighted, right):
    n = weighted.shape[1]
    both = lax.dot_general(
        halves(weighted),
        halves(right),
        (((0,), (0,)), ((), ())),
        preferred_element_type=jnp.float32,
    )
    both = both[:n] + both[n:]
    return both[:, :n] + both[:, n:]


def packed(inner, cross):
    n = inner.shape[0]
    rows = lax.broadcasted_iota(jnp.int32, (n, n), 0)
    columns = lax.broadcasted_iota(jnp.int32, (n, n), 1)
    body = jnp.where(rows > columns, inner, jnp.where(rows < columns, cross, 0.0))
    tail_rows = lax.broadcasted_iota(jnp.int32, (TAIL, n), 0)
    first = jnp.sum(jnp.where(rows == columns, inner, 0.0), axis=0, keepdims=True)
    second = jnp.sum(jnp.where(rows == columns, cross, 0.0), axis=0, keepdims=True)
    tail = jnp.where(tail_rows == 0, first, jnp.where(tail_rows == 1, second, 0.0))
    return jnp.concatenate([body, tail], axis=0)


def unpacked(grams):
    n = grams.shape[1]
    rows = lax.broadcasted_iota(jnp.int32, (n, n), 0)
    columns = lax.broadcasted_iota(jnp.int32, (n, n), 1)
    body = grams[:n]
    lower = jnp.where(rows > columns, body, 0.0)
    upper = jnp.where(rows < columns, body, 0.0)
    inner = lower + lower.T + jnp.where(rows == columns, grams[n : n + 1], 0.0)
    cross = upper + upper.T + jnp.where(rows == columns, grams[n + 1 : n + 2], 0.0)
    return inner, cross


def zone_of(parity, slot):
    flip = parity[slot // 2]
    return 2 * (slot // 2) + (flip if slot % 2 == 0 else 1 - flip)


def assemble_into(parity, tables, slots, received, out):
    zone = tables.shape[1]
    for slot in range(4):
        start = pl.multiple_of(zone_of(parity, slot) * zone, zone)
        value = slots[slot][:zone].astype(jnp.float32) + times(tables[slot], received[slot][:zone])
        out[pl.ds(start, zone)] = value


def slots_from(parity, block, slots):
    zone = slots[3].shape[0]
    for slot in range(4):
        pair = 2 * (slot // 2)
        swapped = parity[slot // 2] == (1 if slot % 2 == 0 else 0)
        low, high = block[pair * zone : (pair + 1) * zone], block[(pair + 1) * zone : (pair + 2) * zone]
        slots[slot][:zone] = jnp.where(swapped, high, low)


def choice_kernel(first, maps, inverse_rows, out):
    count, modes, total_modes = out.shape
    rows_here, coarse_total = inverse_rows.shape
    unknown = lax.broadcasted_iota(jnp.int32, (coarse_total, total_modes), 0)
    columns = (unknown == maps[...]).astype(jnp.float32).astype(jnp.bfloat16)
    picked = jnp.dot(inverse_rows[...], columns, preferred_element_type=jnp.float32)
    here = lax.broadcasted_iota(jnp.int32, (rows_here, total_modes), 0) + first[0]
    rows = (here == maps[...]).astype(jnp.float32).astype(jnp.bfloat16)
    table = lax.dot_general(
        rows,
        picked.astype(jnp.bfloat16),
        (((0,), (0,)), ((), ())),
        preferred_element_type=jnp.float32,
    ).astype(jnp.bfloat16)
    source = lax.broadcasted_iota(jnp.int32, (total_modes, total_modes), 0)
    target = lax.broadcasted_iota(jnp.int32, (total_modes, total_modes), 1)
    for j in range(count):
        order = (source == (target ^ (j * modes))).astype(jnp.float32).astype(jnp.bfloat16)
        block = table[j * modes : (j + 1) * modes]
        out[j] = jnp.dot(block, order, preferred_element_type=jnp.float32).astype(jnp.bfloat16)


def fold_kernel(grams, own, received, out):
    count = own.shape[0] - grams
    if grams:
        out[:grams] = own[:grams] + received[:grams]
    out[grams : grams + count] = own[grams:]
    out[grams + count :] = received[grams:]


def tables_kernel(parity, rows, counts, tables, weight):
    capacity = rows.shape[2]
    place = lax.broadcasted_iota(jnp.int32, (capacity, capacity), 0)
    entry = lax.broadcasted_iota(jnp.int32, (1, capacity), 1)
    for slot in range(4):
        d = zone_of(parity, slot)
        partner_zone = zone_of(parity, slot ^ 1)
        own = rows[0, pl.ds(d, 1)] - d * capacity
        partner = rows[1, pl.ds(d, 1)] - partner_zone * capacity
        own = jnp.where(entry < counts[d], own, -1)
        to = (place == own).astype(jnp.float32).astype(jnp.bfloat16)
        source = (place == partner).astype(jnp.float32).astype(jnp.bfloat16)
        table = lax.dot_general(
            to, source, (((1,), (1,)), ((), ())), preferred_element_type=jnp.float32
        )
        tables[slot] = table.astype(jnp.bfloat16)
        ones = jnp.ones((capacity, weight.shape[1]), jnp.bfloat16)
        shared = jnp.dot(table.astype(jnp.bfloat16), ones, preferred_element_type=jnp.float32)
        weight[pl.ds(pl.multiple_of(d * capacity, capacity), capacity)] = 1.0 / (1.0 + shared)


def start_kernel(parity, tables, weight, basis, *refs):
    slots, received, (block, piece) = refs[:4], refs[4:8], refs[8:]
    assemble_into(parity, tables, slots, received, block)
    piece[...] = times(basis[...], weight[...] * block[...])


def gram_start_kernel(parity, tables, weight, basis, z, r, *refs):
    slots, received, (block, carried) = refs[:4], refs[4:8], refs[8:]
    n = z.shape[1]
    assemble_into(parity, tables, slots, received, block)
    carried[n + TAIL :] = times(basis[...], weight[...] * block[...])
    weighted = weight[...] * z[...]
    carried[: n + TAIL] = packed(local_gram(weighted, r[...]), local_gram(weighted, block[...]))


def send_kernel(parity, rhs, basis, *slots):
    zone, columns = slots[3].shape
    slots_from(parity, rhs[...], slots)
    modes = basis.shape[0]
    for slot in range(2):
        for part in range(zone // columns):
            at = part * columns
            low, high = basis[:, at : at + columns], basis[:, zone + at : zone + at + columns]
            chosen = jnp.where(parity[0] == slot, low, high)
            slots[slot][zone + part * modes : zone + (part + 1) * modes] = chosen


def neighbour_kernel(shift, tables, chosen, first, second, first_zone, second_zone, rows, columns):
    modes, total_modes = chosen.shape
    zone, width = tables.shape[1], first_zone.shape[1]
    source = lax.broadcasted_iota(jnp.int32, (total_modes, total_modes), 0)
    target = lax.broadcasted_iota(jnp.int32, (total_modes, total_modes), 1)
    rows[:modes] = chosen[...]
    for slot, (theirs, below) in enumerate(((first, first_zone), (second, second_zone))):
        order = (source == (target ^ shift[slot])).astype(jnp.float32).astype(jnp.bfloat16)
        ordered = jnp.dot(theirs[...], order, preferred_element_type=jnp.float32)
        rows[(slot + 1) * modes : (slot + 2) * modes] = ordered.astype(jnp.bfloat16)
        basis = jnp.concatenate(
            [
                below[zone + part * modes : zone + (part + 1) * modes]
                for part in range(zone // width)
            ],
            axis=1,
        )
        columns[slot] = lax.dot_general(
            basis, tables[slot], (((1,), (1,)), ((), ())), preferred_element_type=jnp.float32
        ).astype(jnp.bfloat16)


def local_kernel(parity, weight, matrix, block, out, *early):
    zone = early[0].shape[0]
    out[...] = weight[...] * times(matrix[...], weight[...] * block[...])
    low, high = out[:zone], out[zone : 2 * zone]
    early[0][...] = jnp.where(parity[0] == 0, low, high)
    early[1][...] = jnp.where(parity[0] == 0, high, low)


def finish_kernel(
    grams, parity, weight, basis, chosen, near, local, own, received, *slots
):
    modes, zone = basis.shape[0], slots[0].shape[0]
    pieces = jnp.concatenate([own[grams:], received[grams:]], axis=0)
    picked = times(chosen[...], pieces)
    smoothed = local[...] + weight[...] * times(basis[...], picked[:modes], contracting=0)
    slots_from(parity, smoothed, slots)
    for slot in range(2):
        start = pl.multiple_of(zone_of(parity, slot) * zone, zone)
        theirs = times(near[slot], picked[(slot + 1) * modes : (slot + 2) * modes], contracting=0)
        slots[slot][...] = slots[slot][...] + weight[pl.ds(start, zone)] * theirs
    if grams:
        slots[2][zone:] = own[:grams] + received[:grams]


def operator_kernel(parity, tables, matrix, *refs):
    slots, received, block, out = refs[:4], refs[4:8], refs[8], refs[9:13]
    zone = out[0].shape[0]
    assemble_into(parity, tables, slots, received, block)
    slots_from(parity, times(matrix[...], block[...]), out)
    for grams in refs[13:]:
        grams[...] = slots[2][zone:] + received[2][zone:]


def first_update_kernel(parity, tables, weight, basis, grams, z, w, r, m, *refs):
    slots, received = refs[:4], refs[4:8]
    x, r_out, z_out, w_out, image, curvature_out, carried = refs[8:]
    n = z.shape[1]
    assemble_into(parity, tables, slots, received, image)
    inner, cross = unpacked(grams[...])
    curvature_out[...] = cross
    alpha = mixer(eliminate(cross, inner))
    w_new = w[...] - mix(image[...], alpha)
    w_out[...] = w_new
    carried[n + TAIL :] = times(basis[...], weight[...] * w_new)
    x[...] = mix(z[...], alpha)
    r_new = r[...] - mix(w[...], alpha)
    r_out[...] = r_new
    z_new = z[...] - mix(m[...], alpha)
    z_out[...] = z_new
    weighted = weight[...] * z_new
    carried[: n + TAIL] = packed(local_gram(weighted, r_new), local_gram(weighted, w_new))


def step_sizes(grams, inner_inverse, curvature):
    inner, cross = unpacked(grams)
    beta = exact(inner_inverse[...], inner)
    bent = symmetric(cross - exact(beta.T, exact(curvature[...], beta)))
    return beta, bent, eliminate(bent, inner)


def next_update_kernel(
    parity, tables, weight, basis, grams, inner_inverse, curvature,
    z, w, r, m, p, s, q, t, x, *refs
):
    slots, received = refs[:4], refs[4:8]
    (
        x_out, r_out, z_out, w_out, p_out, s_out, q_out, t_out, curvature_out, *carried
    ) = refs[8:]
    assemble_into(parity, tables, slots, received, t_out)
    beta, bent, alpha = step_sizes(grams[...], inner_inverse, curvature)
    curvature_out[...] = bent
    beta, alpha = mixer(beta), mixer(alpha)
    t_out[...] = t_out[...] + mix(t[...], beta)
    w_new = w[...] - mix(t_out[...], alpha)
    w_out[...] = w_new
    p_out[...] = z[...] + mix(p[...], beta)
    s_out[...] = w[...] + mix(s[...], beta)
    q_out[...] = m[...] + mix(q[...], beta)
    x_out[...] = x[...] + mix(p_out[...], alpha)
    r_new = r[...] - mix(s_out[...], alpha)
    r_out[...] = r_new
    z_new = z[...] - mix(q_out[...], alpha)
    z_out[...] = z_new
    weighted = weight[...] * z_new
    sums = packed(local_gram(weighted, r_new), local_gram(weighted, w_new))
    if len(carried) == 1:
        rows = sums.shape[0]
        carried[0][:rows] = sums
        carried[0][rows:] = times(basis[...], weight[...] * w_new)
    else:
        kept, sent = carried
        low, high = sums[: kept.shape[0]], sums[kept.shape[0] :]
        kept[...] = jnp.where(parity[1] == 0, low, high)
        sent[...] = jnp.where(parity[1] == 0, high, low)


def last_update_kernel(parity, half, other, inner_inverse, curvature, z, w, r, p, s, x, x_out, r_out):
    low = jnp.where(parity[1] == 0, half[...], other[...])
    high = jnp.where(parity[1] == 0, other[...], half[...])
    sums = jnp.concatenate([low, high], axis=0)
    beta, _, alpha = step_sizes(sums, inner_inverse, curvature)
    beta, alpha = mixer(beta), mixer(alpha)
    x_out[...] = x[...] + mix(z[...] + mix(p[...], beta), alpha)
    r_out[...] = r[...] - mix(w[...] + mix(s[...], beta), alpha)


def inverse_kernel(grams, out):
    n = out.shape[0]
    rows = lax.broadcasted_iota(jnp.int32, (n, n), 0)
    columns = lax.broadcasted_iota(jnp.int32, (n, n), 1)
    inner, _ = unpacked(grams[...])
    out[...] = eliminate(inner, (rows == columns).astype(jnp.float32))


VMEM = pl.BlockSpec(memory_space=pltpu.VMEM)
SMEM = pl.BlockSpec(memory_space=pltpu.SMEM)


def call(kernel, name, flops, outs, *args):
    shapes = [jax.ShapeDtypeStruct(shape, dtype) for shape, dtype in outs]
    moved = sum(a.size * a.dtype.itemsize for a in (*args, *shapes))
    return pl.pallas_call(
        kernel,
        out_shape=shapes,
        in_specs=[SMEM if a.ndim == 1 else VMEM for a in args],
        out_specs=[VMEM] * len(shapes),
        name=name,
        compiler_params=pltpu.CompilerParams(vmem_limit_bytes=24 * 1024 * 1024),
        cost_estimate=pl.CostEstimate(flops=flops, bytes_accessed=moved, transcendentals=0),
    )(*args)


def pairs(axis, first):
    count = lax.axis_size(axis)
    low = range(first, count - 1, 2)
    return [(i, i + 1) for i in low] + [(i + 1, i) for i in low]


def exchange(slots, first=0):
    patterns = (("sub", 0), ("sub", 1), ("group", 0), ("group", 1))
    return [
        lax.ppermute(slot, axis, pairs(axis, low))
        for slot, (axis, low) in zip(slots, patterns[first:])
    ]


def shards(
    schur, local_inverse, rhs_parts, basis, coarse_map, coarse_inverse, shared_rows, shared_counts
):
    schur, local_inverse, basis = schur[0, 0], local_inverse[0, 0], basis[0, 0]
    rhs = rhs_parts[0, 0]
    rows, columns = rhs.shape
    zone = shared_rows.shape[-1]
    modes = basis.shape[0]
    parity = jnp.stack([lax.axis_index("sub") % 2, lax.axis_index("group") % 2]).astype(jnp.int32)
    block = ((rows, columns), jnp.float32)
    part = ((zone, columns), jnp.float32)
    square = ((columns, columns), jnp.float32)
    sums = columns + TAIL
    share = ((modes, columns), jnp.float32)
    carry = ((sums + modes, columns), jnp.float32)
    halves_out = [((sums // 2, columns), jnp.float32)] * 2
    solve_flops = 400_000_000
    product_flops = 4 * rows * rows * columns

    low_part = ((zone, columns), jnp.bfloat16)
    long_part = ((zone + modes * (zone // columns), columns), jnp.bfloat16)
    rhs_slots = call(
        send_kernel,
        "first_zones",
        rows * columns,
        [long_part, long_part, low_part, low_part],
        parity,
        rhs,
        basis,
    )
    received = exchange(rhs_slots)
    tables, weight = call(
        tables_kernel,
        "shared_row_tables",
        16 * zone**3,
        [((4, zone, zone), jnp.bfloat16), block],
        parity,
        shared_rows[0, 0],
        shared_counts[0, 0],
    )
    subs = lax.axis_size("sub")
    inverse_rows = coarse_inverse[0]
    maps, (rhs_slots, (received[0], received[2]), (received[1], received[3], weight)) = gather_sub(
        coarse_map[0, 0],
        rhs_slots,
        (received[0], received[2]),
        (received[1], received[3], weight),
    )
    (chosen,) = call(
        choice_kernel,
        "selected_inverse",
        product_flops // 4,
        [((subs, modes, subs * modes), jnp.bfloat16)],
        (lax.axis_index("sub") * inverse_rows.shape[0]).astype(jnp.int32)[None],
        maps[None],
        inverse_rows,
    )
    for bit in reversed(bits_of("sub")):
        chosen = chosen[:bit] + swap(chosen[bit:], "sub", bit)
    chosen = chosen[0]
    me = lax.axis_index("sub")
    across = jnp.stack([me ^ (me ^ 1), me ^ (((me + 1) ^ 1) - 1)]) & (subs - 1)
    chosen, near = call(
        neighbour_kernel,
        "neighbours",
        product_flops // 16,
        [((3 * modes, subs * modes), jnp.bfloat16), ((2, modes, zone), jnp.bfloat16)],
        (across * modes).astype(jnp.int32),
        tables,
        chosen,
        *exchange([chosen, chosen]),
        *received[:2],
    )

    def precondition(vector, carried, ride=None):
        grams = carried.shape[0] - modes
        local, *early = call(
            local_kernel,
            "local_inverse",
            product_flops,
            [block, part, part],
            parity,
            weight,
            local_inverse,
            vector,
        )
        early = exchange(early)
        bits = bits_of("sub")
        for number, bit in enumerate(bits[:-1]):
            rows_out = 2 * carried.shape[0] - grams
            arrived = swap(carried, "sub", bit)
            if ride is not None and number == 0:
                arrived, ride = lax.optimization_barrier((arrived, ride))
            if number == 1:
                arrived, early[0] = lax.optimization_barrier((arrived, early[0]))
            (carried,) = call(
                functools.partial(fold_kernel, grams),
                "fold",
                columns * rows_out,
                [((rows_out, columns), jnp.float32)],
                carried,
                arrived,
            )
        arrived, early = lax.optimization_barrier((swap(carried, "sub", bits[-1]), early))
        slots = call(
            functools.partial(finish_kernel, grams),
            "coarse_part",
            product_flops // 8,
            [part, part, ((zone + grams, columns), jnp.float32), part],
            parity,
            weight,
            basis,
            chosen,
            near,
            local,
            carried,
            arrived,
        )
        return slots, early + exchange(slots[2:], 2), ride

    def operator(slots, received):
        grams = slots[2].shape[0] - zone
        outs = [((grams, columns), jnp.float32)] if grams else []
        vector, *image = call(
            operator_kernel,
            "operator",
            product_flops,
            [block] + [part] * 4 + outs,
            parity,
            tables,
            schur,
            *slots,
            *received,
        )
        whole = image[4:]
        for bit in bits_of("group")[1:] if grams else ():
            whole = [whole[0] + swap(whole[0], "group", bit)]
        return vector, image[:4], exchange(image[:4]), *whole

    r, pieces = call(
        start_kernel,
        "start",
        product_flops // 8,
        [block, share],
        parity,
        tables,
        weight,
        basis,
        *rhs_slots,
        *received,
    )
    slots, received, _ = precondition(r, pieces)
    z, image, received = operator(slots, received)
    w, carried = call(
        gram_start_kernel,
        "start_grams",
        product_flops // 4,
        [block, carry],
        parity,
        tables,
        weight,
        basis,
        z,
        r,
        *image,
        *received,
    )
    ride = None
    for iteration in range(ITERS - 1):
        final = iteration + 2 == ITERS
        slots, received, inner_inverse = precondition(w, carried, ride)
        m, image, received, grams = operator(slots, received)
        common = (parity, tables, weight, basis, grams)
        if iteration == 0:
            p, s, q = z, w, m
            x, r, z, w, t, curvature, carried = call(
                first_update_kernel,
                "first_update",
                2 * solve_flops,
                [block] * 5 + [square, carry],
                *common,
                z,
                w,
                r,
                m,
                *image,
                *received,
            )
        else:
            x, r, z, w, p, s, q, t, curvature, *carried = call(
                next_update_kernel,
                "next_update",
                2 * solve_flops,
                [block] * 8 + [square] + (halves_out if final else [carry]),
                *common,
                inner_inverse,
                curvature,
                z,
                w,
                r,
                m,
                p,
                s,
                q,
                t,
                x,
                *image,
                *received,
            )
            if not final:
                (carried,) = carried
        grams, curvature = lax.optimization_barrier((grams, curvature))
        (ride,) = call(inverse_kernel, "inner_inverse", solve_flops, [square], grams)
    *grams, inner_inverse = total(*carried, ride)
    x, r = call(
        last_update_kernel,
        "last_update",
        2 * solve_flops,
        [block, block],
        parity,
        *grams,
        inner_inverse,
        curvature,
        z,
        w,
        r,
        p,
        s,
        x,
    )
    return x[None, None], r[None, None]


def solution(mesh):
    placed = (
        P("group", "sub", None, None),
        P("group", "sub", None, None),
        P("group", "sub", None, None),
        P("group", "sub", None, None),
        P("group", "sub", None),
        P("group", "sub", None),
        P("group", "sub", None, None, None),
        P("group", "sub", None),
    )
    return jax.shard_map(
        shards,
        mesh=mesh,
        in_specs=placed,
        out_specs=(P("group", "sub", None, None), P("group", "sub", None, None)),
        check_vma=False,
    )
```

```python
import functools

import jax
import jax.numpy as jnp
from jax import lax
from jax.experimental import pallas as pl
from jax.experimental.pallas import tpu as pltpu
from jax.sharding import PartitionSpec as P

ITERS = 3
TAIL = 16
HIGHEST = lax.Precision.HIGHEST


def swap(x, axis, bit):
    return lax.ppermute(x, axis, [(i, i ^ bit) for i in range(lax.axis_size(axis))])


def bits_of(axis):
    count = lax.axis_size(axis)
    if count & (count - 1):
        raise ValueError("axis size")
    return [1 << b for b in range(count.bit_length() - 1)]


def total(kept, sent, ride):
    half = kept + swap(sent, "group", 1)
    rest = [("group", bit) for bit in bits_of("group")[1:]]
    subs = [("sub", bit) for bit in bits_of("sub")]
    for number, (axis, bit) in enumerate(subs[:1] + rest + subs[1:]):
        arrived = swap(half, axis, bit)
        if number == 1:
            arrived, ride = lax.optimization_barrier((arrived, ride))
        half = half + arrived
    return half, swap(half, "group", 1), ride


def gather_sub(x, *rides):
    rides = list(rides)
    for number, bit in enumerate(bits_of("sub")):
        arrived = swap(x, "sub", bit)
        if number < len(rides):
            arrived, rides[number] = lax.optimization_barrier((arrived, rides[number]))
        x = jnp.concatenate([x, arrived], axis=0)
    return x, rides


def eliminate(matrix, block, tile=8):
    n, width = matrix.shape[0], block.shape[1]
    sublane = lax.broadcasted_iota(jnp.int32, (tile, 1), 0)
    left = [matrix[i : i + tile] for i in range(0, n, tile)]
    right = [block[i : i + tile] for i in range(0, n, tile)]
    for k in range(n // tile):
        pivot_left, pivot_right = left[k], right[k]
        at = k * tile
        spread = [
            jnp.broadcast_to(pivot_left[:, at + j : at + j + 1], (tile, n)) for j in range(tile)
        ]
        for j in range(tile):
            inverse = 1.0 / spread[j][j : j + 1]
            here = sublane == j
            column = spread[j]

            def cleared(rows, column=column, inverse=inverse, here=here, j=j):
                pivot = rows[j : j + 1] * inverse
                return jnp.where(here, pivot, rows - column * pivot)

            for i in range(j + 1, tile):
                spread[i] = cleared(spread[i])
            pivot_left, pivot_right = cleared(pivot_left), cleared(pivot_right)
        for i in range(n // tile):
            if i == k:
                continue
            old = left[i]
            new_left, new_right = old, right[i]
            for j in range(tile):
                scale = jnp.broadcast_to(old[:, at + j : at + j + 1], (tile, n))
                new_left = new_left - scale * pivot_left[j : j + 1]
                new_right = new_right - scale * pivot_right[j : j + 1]
            left[i], right[i] = new_left, new_right
        left[k], right[k] = pivot_left, pivot_right
    return jnp.concatenate(right, axis=0)


def exact(a, b):
    return jnp.dot(a, b, precision=HIGHEST, preferred_element_type=jnp.float32)


def symmetric(a):
    return (a + a.T) * 0.5


def halves(x):
    high = x.astype(jnp.bfloat16)
    low = (x - high.astype(jnp.float32)).astype(jnp.bfloat16)
    return jnp.concatenate([high, low], axis=1)


def folded(both):
    n = both.shape[1] // 2
    return both[:, :n] + both[:, n:]


def times(matrix, x, contracting=1):
    dims = (((contracting,), (0,)), ((), ()))
    if x.dtype == jnp.bfloat16:
        return lax.dot_general(matrix, x, dims, preferred_element_type=jnp.float32)
    return folded(lax.dot_general(matrix, halves(x), dims, preferred_element_type=jnp.float32))


def mixer(mixing):
    both = halves(mixing)
    return jnp.concatenate([both, both], axis=0)


def mix(block, mixer_value):
    return folded(jnp.dot(halves(block), mixer_value, preferred_element_type=jnp.float32))


def local_gram(weighted, right):
    n = weighted.shape[1]
    both = lax.dot_general(
        halves(weighted),
        halves(right),
        (((0,), (0,)), ((), ())),
        preferred_element_type=jnp.float32,
    )
    both = both[:n] + both[n:]
    return both[:, :n] + both[:, n:]


def packed(inner, cross):
    n = inner.shape[0]
    rows = lax.broadcasted_iota(jnp.int32, (n, n), 0)
    columns = lax.broadcasted_iota(jnp.int32, (n, n), 1)
    body = jnp.where(rows > columns, inner, jnp.where(rows < columns, cross, 0.0))
    tail_rows = lax.broadcasted_iota(jnp.int32, (TAIL, n), 0)
    first = jnp.sum(jnp.where(rows == columns, inner, 0.0), axis=0, keepdims=True)
    second = jnp.sum(jnp.where(rows == columns, cross, 0.0), axis=0, keepdims=True)
    tail = jnp.where(tail_rows == 0, first, jnp.where(tail_rows == 1, second, 0.0))
    return jnp.concatenate([body, tail], axis=0)


def unpacked(grams):
    n = grams.shape[1]
    rows = lax.broadcasted_iota(jnp.int32, (n, n), 0)
    columns = lax.broadcasted_iota(jnp.int32, (n, n), 1)
    body = grams[:n]
    lower = jnp.where(rows > columns, body, 0.0)
    upper = jnp.where(rows < columns, body, 0.0)
    inner = lower + lower.T + jnp.where(rows == columns, grams[n : n + 1], 0.0)
    cross = upper + upper.T + jnp.where(rows == columns, grams[n + 1 : n + 2], 0.0)
    return inner, cross


def zone_of(parity, slot):
    flip = parity[slot // 2]
    return 2 * (slot // 2) + (flip if slot % 2 == 0 else 1 - flip)


def assemble_into(parity, tables, slots, received, out):
    zone = tables.shape[1]
    for slot in range(4):
        start = pl.multiple_of(zone_of(parity, slot) * zone, zone)
        value = slots[slot][:zone].astype(jnp.float32) + times(tables[slot], received[slot][:zone])
        out[pl.ds(start, zone)] = value


def slots_from(parity, block, slots):
    zone = block.shape[0] // 4
    for slot in range(4):
        pair = 2 * (slot // 2)
        swapped = parity[slot // 2] == (1 if slot % 2 == 0 else 0)
        low, high = block[pair * zone : (pair + 1) * zone], block[(pair + 1) * zone : (pair + 2) * zone]
        slots[slot][:zone] = jnp.where(swapped, high, low)


def choice_kernel(first, maps, inverse_rows, out):
    count, modes, total_modes = out.shape
    rows_here, coarse_total = inverse_rows.shape
    unknown = lax.broadcasted_iota(jnp.int32, (coarse_total, total_modes), 0)
    columns = (unknown == maps[...]).astype(jnp.float32).astype(jnp.bfloat16)
    picked = jnp.dot(inverse_rows[...], columns, preferred_element_type=jnp.float32)
    here = lax.broadcasted_iota(jnp.int32, (rows_here, total_modes), 0) + first[0]
    rows = (here == maps[...]).astype(jnp.float32).astype(jnp.bfloat16)
    table = lax.dot_general(
        rows,
        picked.astype(jnp.bfloat16),
        (((0,), (0,)), ((), ())),
        preferred_element_type=jnp.float32,
    ).astype(jnp.bfloat16)
    source = lax.broadcasted_iota(jnp.int32, (total_modes, total_modes), 0)
    target = lax.broadcasted_iota(jnp.int32, (total_modes, total_modes), 1)
    for j in range(count):
        order = (source == (target ^ (j * modes))).astype(jnp.float32).astype(jnp.bfloat16)
        block = table[j * modes : (j + 1) * modes]
        out[j] = jnp.dot(block, order, preferred_element_type=jnp.float32).astype(jnp.bfloat16)


def fold_kernel(grams, own, received, out):
    count = own.shape[0] - grams
    if grams:
        out[:grams] = own[:grams] + received[:grams]
    out[grams : grams + count] = own[grams:]
    out[grams + count :] = received[grams:]


def tables_kernel(parity, rows, counts, tables, weight):
    capacity = rows.shape[2]
    place = lax.broadcasted_iota(jnp.int32, (capacity, capacity), 0)
    entry = lax.broadcasted_iota(jnp.int32, (1, capacity), 1)
    for slot in range(4):
        d = zone_of(parity, slot)
        partner_zone = zone_of(parity, slot ^ 1)
        own = rows[0, pl.ds(d, 1)] - d * capacity
        partner = rows[1, pl.ds(d, 1)] - partner_zone * capacity
        own = jnp.where(entry < counts[d], own, -1)
        to = (place == own).astype(jnp.float32).astype(jnp.bfloat16)
        source = (place == partner).astype(jnp.float32).astype(jnp.bfloat16)
        table = lax.dot_general(
            to, source, (((1,), (1,)), ((), ())), preferred_element_type=jnp.float32
        )
        tables[slot] = table.astype(jnp.bfloat16)
        ones = jnp.ones((capacity, weight.shape[1]), jnp.bfloat16)
        shared = jnp.dot(table.astype(jnp.bfloat16), ones, preferred_element_type=jnp.float32)
        weight[pl.ds(pl.multiple_of(d * capacity, capacity), capacity)] = 1.0 / (1.0 + shared)


def start_kernel(parity, tables, weight, basis, *refs):
    slots, received, (block, piece) = refs[:4], refs[4:8], refs[8:]
    assemble_into(parity, tables, slots, received, block)
    piece[...] = times(basis[...], weight[...] * block[...])


def gram_start_kernel(parity, tables, weight, basis, z, r, *refs):
    slots, received, (block, carried) = refs[:4], refs[4:8], refs[8:]
    n = z.shape[1]
    assemble_into(parity, tables, slots, received, block)
    carried[n + TAIL :] = times(basis[...], weight[...] * block[...])
    weighted = weight[...] * z[...]
    carried[: n + TAIL] = packed(local_gram(weighted, r[...]), local_gram(weighted, block[...]))


def send_kernel(parity, rhs, basis, *slots):
    zone, columns = rhs.shape[0] // 4, rhs.shape[1]
    slots_from(parity, rhs[...], slots)
    modes = basis.shape[0]
    for slot in range(4):
        pair = 2 * (slot // 2)
        for part in range(zone // columns):
            at = pair * zone + part * columns
            low, high = basis[:, at : at + columns], basis[:, at + zone : at + zone + columns]
            chosen = jnp.where(parity[slot // 2] == slot % 2, low, high)
            slots[slot][zone + part * modes : zone + (part + 1) * modes] = chosen


def neighbour_kernel(shift, tables, chosen, first, second, *refs):
    zones, (rows, columns) = refs[:4], refs[4:]
    modes, total_modes = chosen.shape
    zone, width = tables.shape[1], zones[0].shape[1]
    source = lax.broadcasted_iota(jnp.int32, (total_modes, total_modes), 0)
    target = lax.broadcasted_iota(jnp.int32, (total_modes, total_modes), 1)
    rows[:modes] = chosen[...]
    for slot, theirs in enumerate((first, second)):
        order = (source == (target ^ shift[slot])).astype(jnp.float32).astype(jnp.bfloat16)
        ordered = jnp.dot(theirs[...], order, preferred_element_type=jnp.float32)
        rows[(slot + 1) * modes : (slot + 2) * modes] = ordered.astype(jnp.bfloat16)
    for slot, below in enumerate(zones):
        basis = jnp.concatenate(
            [
                below[zone + part * modes : zone + (part + 1) * modes]
                for part in range(zone // width)
            ],
            axis=1,
        )
        columns[slot] = lax.dot_general(
            basis, tables[slot], (((1,), (1,)), ((), ())), preferred_element_type=jnp.float32
        ).astype(jnp.bfloat16)


def local_kernel(parity, weight, matrix, block, out, *early):
    out[...] = weight[...] * times(matrix[...], weight[...] * block[...])
    slots_from(parity, out[...], early)


def pick_kernel(grams, chosen, own, received, picked, mine, carried):
    modes = mine.shape[0]
    pieces = jnp.concatenate([own[grams:], received[grams:]], axis=0)
    values = times(chosen[...], pieces)
    picked[...] = values
    mine[...] = values[:modes]
    carried[grams:] = values[:modes]
    if grams:
        carried[:grams] = own[:grams] + received[:grams]


def operator_kernel(
    parity, tables, weight, basis, near, matrix, local, picked, carried, across, beyond, *refs
):
    received, block, out = refs[:4], refs[4], refs[5:9]
    modes, zone = basis.shape[0], tables.shape[1]
    grams = carried.shape[0] - modes
    block[...] = local[...] + weight[...] * times(basis[...], picked[:modes], contracting=0)
    coarse = (picked[modes : 2 * modes], picked[2 * modes :], across[grams:], beyond[...])
    for slot in range(4):
        place = pl.ds(pl.multiple_of(zone_of(parity, slot) * zone, zone), zone)
        theirs = weight[place] * times(near[slot], coarse[slot], contracting=0)
        block[place] = block[place] + theirs + times(tables[slot], received[slot][...])
    slots_from(parity, times(matrix[...], block[...]), out)
    for total_out in refs[9:]:
        total_out[...] = carried[:grams] + across[:grams]


def first_update_kernel(parity, tables, weight, basis, grams, z, w, r, m, *refs):
    slots, received = refs[:4], refs[4:8]
    x, r_out, z_out, w_out, image, curvature_out, carried = refs[8:]
    n = z.shape[1]
    assemble_into(parity, tables, slots, received, image)
    inner, cross = unpacked(grams[...])
    curvature_out[...] = cross
    alpha = mixer(eliminate(cross, inner))
    w_new = w[...] - mix(image[...], alpha)
    w_out[...] = w_new
    carried[n + TAIL :] = times(basis[...], weight[...] * w_new)
    x[...] = mix(z[...], alpha)
    r_new = r[...] - mix(w[...], alpha)
    r_out[...] = r_new
    z_new = z[...] - mix(m[...], alpha)
    z_out[...] = z_new
    weighted = weight[...] * z_new
    carried[: n + TAIL] = packed(local_gram(weighted, r_new), local_gram(weighted, w_new))


def step_sizes(grams, inner_inverse, curvature):
    inner, cross = unpacked(grams)
    beta = exact(inner_inverse[...], inner)
    bent = symmetric(cross - exact(beta.T, exact(curvature[...], beta)))
    return beta, bent, eliminate(bent, inner)


def next_update_kernel(
    parity, tables, weight, basis, grams, inner_inverse, curvature,
    z, w, r, m, p, s, q, t, x, *refs
):
    slots, received = refs[:4], refs[4:8]
    (
        x_out, r_out, z_out, w_out, p_out, s_out, q_out, t_out, curvature_out, *carried
    ) = refs[8:]
    assemble_into(parity, tables, slots, received, t_out)
    beta, bent, alpha = step_sizes(grams[...], inner_inverse, curvature)
    curvature_out[...] = bent
    beta, alpha = mixer(beta), mixer(alpha)
    t_out[...] = t_out[...] + mix(t[...], beta)
    w_new = w[...] - mix(t_out[...], alpha)
    w_out[...] = w_new
    p_out[...] = z[...] + mix(p[...], beta)
    s_out[...] = w[...] + mix(s[...], beta)
    q_out[...] = m[...] + mix(q[...], beta)
    x_out[...] = x[...] + mix(p_out[...], alpha)
    r_new = r[...] - mix(s_out[...], alpha)
    r_out[...] = r_new
    z_new = z[...] - mix(q_out[...], alpha)
    z_out[...] = z_new
    weighted = weight[...] * z_new
    sums = packed(local_gram(weighted, r_new), local_gram(weighted, w_new))
    if len(carried) == 1:
        rows = sums.shape[0]
        carried[0][:rows] = sums
        carried[0][rows:] = times(basis[...], weight[...] * w_new)
    else:
        kept, sent = carried
        low, high = sums[: kept.shape[0]], sums[kept.shape[0] :]
        kept[...] = jnp.where(parity[1] == 0, low, high)
        sent[...] = jnp.where(parity[1] == 0, high, low)


def last_update_kernel(parity, half, other, inner_inverse, curvature, z, w, r, p, s, x, x_out, r_out):
    low = jnp.where(parity[1] == 0, half[...], other[...])
    high = jnp.where(parity[1] == 0, other[...], half[...])
    sums = jnp.concatenate([low, high], axis=0)
    beta, _, alpha = step_sizes(sums, inner_inverse, curvature)
    beta, alpha = mixer(beta), mixer(alpha)
    x_out[...] = x[...] + mix(z[...] + mix(p[...], beta), alpha)
    r_out[...] = r[...] - mix(w[...] + mix(s[...], beta), alpha)


def inverse_kernel(grams, out):
    n = out.shape[0]
    rows = lax.broadcasted_iota(jnp.int32, (n, n), 0)
    columns = lax.broadcasted_iota(jnp.int32, (n, n), 1)
    inner, _ = unpacked(grams[...])
    out[...] = eliminate(inner, (rows == columns).astype(jnp.float32))


VMEM = pl.BlockSpec(memory_space=pltpu.VMEM)
SMEM = pl.BlockSpec(memory_space=pltpu.SMEM)


def call(kernel, name, flops, outs, *args):
    shapes = [jax.ShapeDtypeStruct(shape, dtype) for shape, dtype in outs]
    moved = sum(a.size * a.dtype.itemsize for a in (*args, *shapes))
    return pl.pallas_call(
        kernel,
        out_shape=shapes,
        in_specs=[SMEM if a.ndim == 1 else VMEM for a in args],
        out_specs=[VMEM] * len(shapes),
        name=name,
        compiler_params=pltpu.CompilerParams(vmem_limit_bytes=24 * 1024 * 1024),
        cost_estimate=pl.CostEstimate(flops=flops, bytes_accessed=moved, transcendentals=0),
    )(*args)


def pairs(axis, first):
    count = lax.axis_size(axis)
    low = range(first, count - 1, 2)
    return [(i, i + 1) for i in low] + [(i + 1, i) for i in low]


def exchange(slots, first=0):
    patterns = (("sub", 0), ("sub", 1), ("group", 0), ("group", 1))
    return [
        lax.ppermute(slot, axis, pairs(axis, low))
        for slot, (axis, low) in zip(slots, patterns[first:])
    ]


def shards(
    schur, local_inverse, rhs_parts, basis, coarse_map, coarse_inverse, shared_rows, shared_counts
):
    schur, local_inverse, basis = schur[0, 0], local_inverse[0, 0], basis[0, 0]
    rhs = rhs_parts[0, 0]
    rows, columns = rhs.shape
    zone = shared_rows.shape[-1]
    modes = basis.shape[0]
    parity = jnp.stack([lax.axis_index("sub") % 2, lax.axis_index("group") % 2]).astype(jnp.int32)
    block = ((rows, columns), jnp.float32)
    part = ((zone, columns), jnp.float32)
    square = ((columns, columns), jnp.float32)
    sums = columns + TAIL
    share = ((modes, columns), jnp.float32)
    carry = ((sums + modes, columns), jnp.float32)
    halves_out = [((sums // 2, columns), jnp.float32)] * 2
    solve_flops = 400_000_000
    product_flops = 4 * rows * rows * columns

    long_part = ((zone + modes * (zone // columns), columns), jnp.bfloat16)
    rhs_slots = call(
        send_kernel,
        "first_zones",
        rows * columns,
        [long_part] * 4,
        parity,
        rhs,
        basis,
    )
    received = exchange(rhs_slots)
    tables, weight = call(
        tables_kernel,
        "shared_row_tables",
        16 * zone**3,
        [((4, zone, zone), jnp.bfloat16), block],
        parity,
        shared_rows[0, 0],
        shared_counts[0, 0],
    )
    subs = lax.axis_size("sub")
    inverse_rows = coarse_inverse[0]
    maps, (rhs_slots, (received[0], received[2]), (received[1], received[3], weight)) = gather_sub(
        coarse_map[0, 0],
        rhs_slots,
        (received[0], received[2]),
        (received[1], received[3], weight),
    )
    (chosen,) = call(
        choice_kernel,
        "selected_inverse",
        product_flops // 4,
        [((subs, modes, subs * modes), jnp.bfloat16)],
        (lax.axis_index("sub") * inverse_rows.shape[0]).astype(jnp.int32)[None],
        maps[None],
        inverse_rows,
    )
    for bit in reversed(bits_of("sub")):
        chosen = chosen[:bit] + swap(chosen[bit:], "sub", bit)
    chosen = chosen[0]
    me = lax.axis_index("sub")
    across = jnp.stack([me ^ (me ^ 1), me ^ (((me + 1) ^ 1) - 1)]) & (subs - 1)
    chosen, near = call(
        neighbour_kernel,
        "neighbours",
        product_flops // 16,
        [((3 * modes, subs * modes), jnp.bfloat16), ((4, modes, zone), jnp.bfloat16)],
        (across * modes).astype(jnp.int32),
        tables,
        chosen,
        *exchange([chosen, chosen]),
        *received,
    )

    def precondition(vector, carried, ride=None):
        grams = carried.shape[0] - modes
        local, *early = call(
            local_kernel,
            "local_inverse",
            product_flops,
            [block] + [part] * 4,
            parity,
            weight,
            local_inverse,
            vector,
        )
        early = exchange(early)
        bits = bits_of("sub")
        for number, bit in enumerate(bits[:-1]):
            rows_out = 2 * carried.shape[0] - grams
            arrived = swap(carried, "sub", bit)
            if ride is not None and number == 0:
                arrived, ride = lax.optimization_barrier((arrived, ride))
            if number == 1:
                arrived, *early[:2] = lax.optimization_barrier((arrived, *early[:2]))
            (carried,) = call(
                functools.partial(fold_kernel, grams),
                "fold",
                columns * rows_out,
                [((rows_out, columns), jnp.float32)],
                carried,
                arrived,
            )
        arrived, early = lax.optimization_barrier((swap(carried, "sub", bits[-1]), early))
        picked, mine, carried = call(
            functools.partial(pick_kernel, grams),
            "coarse_values",
            product_flops // 64,
            [((3 * modes, columns), jnp.float32), share, ((grams + modes, columns), jnp.float32)],
            chosen,
            carried,
            arrived,
        )
        across = lax.ppermute(carried, "group", pairs("group", 0))
        beyond = lax.ppermute(mine, "group", pairs("group", 1))
        return (local, picked, carried, across, beyond, *early), ride

    def operator(parts):
        grams = parts[2].shape[0] - modes
        outs = [((grams, columns), jnp.float32)] if grams else []
        vector, *image = call(
            operator_kernel,
            "operator",
            product_flops,
            [block] + [part] * 4 + outs,
            parity,
            tables,
            weight,
            basis,
            near,
            schur,
            *parts,
        )
        whole = image[4:]
        for bit in bits_of("group")[1:] if grams else ():
            whole = [whole[0] + swap(whole[0], "group", bit)]
        return vector, image[:4], exchange(image[:4]), *whole

    r, pieces = call(
        start_kernel,
        "start",
        product_flops // 8,
        [block, share],
        parity,
        tables,
        weight,
        basis,
        *rhs_slots,
        *received,
    )
    parts, _ = precondition(r, pieces)
    z, image, received = operator(parts)
    w, carried = call(
        gram_start_kernel,
        "start_grams",
        product_flops // 4,
        [block, carry],
        parity,
        tables,
        weight,
        basis,
        z,
        r,
        *image,
        *received,
    )
    ride = None
    for iteration in range(ITERS - 1):
        final = iteration + 2 == ITERS
        parts, inner_inverse = precondition(w, carried, ride)
        m, image, received, grams = operator(parts)
        common = (parity, tables, weight, basis, grams)
        if iteration == 0:
            p, s, q = z, w, m
            x, r, z, w, t, curvature, carried = call(
                first_update_kernel,
                "first_update",
                2 * solve_flops,
                [block] * 5 + [square, carry],
                *common,
                z,
                w,
                r,
                m,
                *image,
                *received,
            )
        else:
            x, r, z, w, p, s, q, t, curvature, *carried = call(
                next_update_kernel,
                "next_update",
                2 * solve_flops,
                [block] * 8 + [square] + (halves_out if final else [carry]),
                *common,
                inner_inverse,
                curvature,
                z,
                w,
                r,
                m,
                p,
                s,
                q,
                t,
                x,
                *image,
                *received,
            )
            if not final:
                (carried,) = carried
        grams, curvature = lax.optimization_barrier((grams, curvature))
        (ride,) = call(inverse_kernel, "inner_inverse", solve_flops, [square], grams)
    *grams, inner_inverse = total(*carried, ride)
    x, r = call(
        last_update_kernel,
        "last_update",
        2 * solve_flops,
        [block, block],
        parity,
        *grams,
        inner_inverse,
        curvature,
        z,
        w,
        r,
        p,
        s,
        x,
    )
    return x[None, None], r[None, None]


def solution(mesh):
    placed = (
        P("group", "sub", None, None),
        P("group", "sub", None, None),
        P("group", "sub", None, None),
        P("group", "sub", None, None),
        P("group", "sub", None),
        P("group", "sub", None),
        P("group", "sub", None, None, None),
        P("group", "sub", None),
    )
    return jax.shard_map(
        shards,
        mesh=mesh,
        in_specs=placed,
        out_specs=(P("group", "sub", None, None), P("group", "sub", None, None)),
        check_vma=False,
    )
```

```python
import functools

import jax
import jax.numpy as jnp
from jax import lax
from jax.experimental import pallas as pl
from jax.experimental.pallas import tpu as pltpu
from jax.sharding import PartitionSpec as P

ITERS = 3
TAIL = 16
HIGHEST = lax.Precision.HIGHEST


def swap(x, axis, bit):
    return lax.ppermute(x, axis, [(i, i ^ bit) for i in range(lax.axis_size(axis))])


def bits_of(axis):
    count = lax.axis_size(axis)
    if count & (count - 1):
        raise ValueError("axis size")
    return [1 << b for b in range(count.bit_length() - 1)]


def total(kept, sent, ride):
    half = kept + swap(sent, "group", 1)
    rest = [("group", bit) for bit in bits_of("group")[1:]]
    subs = [("sub", bit) for bit in bits_of("sub")]
    for number, (axis, bit) in enumerate(subs[:1] + rest + subs[1:]):
        arrived = swap(half, axis, bit)
        if number == 1:
            arrived, ride = lax.optimization_barrier((arrived, ride))
        half = half + arrived
    return half, swap(half, "group", 1), ride


def gather_sub(x, *rides):
    rides = list(rides)
    for number, bit in enumerate(bits_of("sub")):
        arrived = swap(x, "sub", bit)
        if number < len(rides):
            arrived, rides[number] = lax.optimization_barrier((arrived, rides[number]))
        x = jnp.concatenate([x, arrived], axis=0)
    return x, rides


def eliminate(matrix, block, tile=8):
    n, width = matrix.shape[0], block.shape[1]
    sublane = lax.broadcasted_iota(jnp.int32, (tile, 1), 0)
    left = [matrix[i : i + tile] for i in range(0, n, tile)]
    right = [block[i : i + tile] for i in range(0, n, tile)]
    for k in range(n // tile):
        pivot_left, pivot_right = left[k], right[k]
        at = k * tile
        spread = [
            jnp.broadcast_to(pivot_left[:, at + j : at + j + 1], (tile, n)) for j in range(tile)
        ]
        for j in range(tile):
            inverse = 1.0 / spread[j][j : j + 1]
            here = sublane == j
            column = spread[j]

            def cleared(rows, column=column, inverse=inverse, here=here, j=j):
                pivot = rows[j : j + 1] * inverse
                return jnp.where(here, pivot, rows - column * pivot)

            for i in range(j + 1, tile):
                spread[i] = cleared(spread[i])
            pivot_left, pivot_right = cleared(pivot_left), cleared(pivot_right)
        for i in range(n // tile):
            if i == k:
                continue
            old = left[i]
            new_left, new_right = old, right[i]
            for j in range(tile):
                scale = jnp.broadcast_to(old[:, at + j : at + j + 1], (tile, n))
                new_left = new_left - scale * pivot_left[j : j + 1]
                new_right = new_right - scale * pivot_right[j : j + 1]
            left[i], right[i] = new_left, new_right
        left[k], right[k] = pivot_left, pivot_right
    return jnp.concatenate(right, axis=0)


def exact(a, b):
    return jnp.dot(a, b, precision=HIGHEST, preferred_element_type=jnp.float32)


def symmetric(a):
    return (a + a.T) * 0.5


def halves(x):
    high = x.astype(jnp.bfloat16)
    low = (x - high.astype(jnp.float32)).astype(jnp.bfloat16)
    return jnp.concatenate([high, low], axis=1)


def folded(both):
    n = both.shape[1] // 2
    return both[:, :n] + both[:, n:]


def times(matrix, x, contracting=1):
    dims = (((contracting,), (0,)), ((), ()))
    if x.dtype == jnp.bfloat16:
        return lax.dot_general(matrix, x, dims, preferred_element_type=jnp.float32)
    return folded(lax.dot_general(matrix, halves(x), dims, preferred_element_type=jnp.float32))


def mixer(mixing):
    both = halves(mixing)
    return jnp.concatenate([both, both], axis=0)


def mix(block, mixer_value):
    return folded(jnp.dot(halves(block), mixer_value, preferred_element_type=jnp.float32))


def local_gram(weighted, right):
    n = weighted.shape[1]
    both = lax.dot_general(
        halves(weighted),
        halves(right),
        (((0,), (0,)), ((), ())),
        preferred_element_type=jnp.float32,
    )
    both = both[:n] + both[n:]
    return both[:, :n] + both[:, n:]


def packed(inner, cross):
    n = inner.shape[0]
    rows = lax.broadcasted_iota(jnp.int32, (n, n), 0)
    columns = lax.broadcasted_iota(jnp.int32, (n, n), 1)
    body = jnp.where(rows > columns, inner, jnp.where(rows < columns, cross, 0.0))
    tail_rows = lax.broadcasted_iota(jnp.int32, (TAIL, n), 0)
    first = jnp.sum(jnp.where(rows == columns, inner, 0.0), axis=0, keepdims=True)
    second = jnp.sum(jnp.where(rows == columns, cross, 0.0), axis=0, keepdims=True)
    tail = jnp.where(tail_rows == 0, first, jnp.where(tail_rows == 1, second, 0.0))
    return jnp.concatenate([body, tail], axis=0)


def unpacked(grams):
    n = grams.shape[1]
    rows = lax.broadcasted_iota(jnp.int32, (n, n), 0)
    columns = lax.broadcasted_iota(jnp.int32, (n, n), 1)
    body = grams[:n]
    lower = jnp.where(rows > columns, body, 0.0)
    upper = jnp.where(rows < columns, body, 0.0)
    inner = lower + lower.T + jnp.where(rows == columns, grams[n : n + 1], 0.0)
    cross = upper + upper.T + jnp.where(rows == columns, grams[n + 1 : n + 2], 0.0)
    return inner, cross


def zone_of(parity, slot):
    flip = parity[slot // 2]
    return 2 * (slot // 2) + (flip if slot % 2 == 0 else 1 - flip)


def assemble_into(parity, tables, slots, received, out):
    zone = slots[0].shape[0]
    for slot in range(4):
        start = pl.multiple_of(zone_of(parity, slot) * zone, zone)
        value = slots[slot][:zone].astype(jnp.float32) + times(tables[slot], received[slot][:zone])
        out[pl.ds(start, zone)] = value


def slots_from(parity, block, slots):
    zone = slots[0].shape[0]
    for slot in range(4):
        pair = 2 * (slot // 2)
        swapped = parity[slot // 2] == (1 if slot % 2 == 0 else 0)
        low, high = block[pair * zone : (pair + 1) * zone], block[(pair + 1) * zone : (pair + 2) * zone]
        slots[slot][:zone] = jnp.where(swapped, high, low)


def choice_kernel(first, maps, inverse_rows, out):
    count, modes, total_modes = out.shape
    rows_here, coarse_total = inverse_rows.shape
    unknown = lax.broadcasted_iota(jnp.int32, (coarse_total, total_modes), 0)
    columns = (unknown == maps[...]).astype(jnp.float32).astype(jnp.bfloat16)
    picked = jnp.dot(inverse_rows[...], columns, preferred_element_type=jnp.float32)
    here = lax.broadcasted_iota(jnp.int32, (rows_here, total_modes), 0) + first[0]
    rows = (here == maps[...]).astype(jnp.float32).astype(jnp.bfloat16)
    table = lax.dot_general(
        rows,
        picked.astype(jnp.bfloat16),
        (((0,), (0,)), ((), ())),
        preferred_element_type=jnp.float32,
    ).astype(jnp.bfloat16)
    source = lax.broadcasted_iota(jnp.int32, (total_modes, total_modes), 0)
    target = lax.broadcasted_iota(jnp.int32, (total_modes, total_modes), 1)
    for j in range(count):
        order = (source == (target ^ (j * modes))).astype(jnp.float32).astype(jnp.bfloat16)
        block = table[j * modes : (j + 1) * modes]
        out[j] = jnp.dot(block, order, preferred_element_type=jnp.float32).astype(jnp.bfloat16)


def fold_kernel(grams, own, received, out):
    count = own.shape[0] - grams
    if grams:
        out[:grams] = own[:grams] + received[:grams]
    out[grams : grams + count] = own[grams:]
    out[grams + count :] = received[grams:]


def tables_kernel(parity, rows, counts, tables, weight):
    capacity = rows.shape[2]
    place = lax.broadcasted_iota(jnp.int32, (capacity, capacity), 0)
    entry = lax.broadcasted_iota(jnp.int32, (1, capacity), 1)
    for slot in range(4):
        d = zone_of(parity, slot)
        partner_zone = zone_of(parity, slot ^ 1)
        own = rows[0, pl.ds(d, 1)] - d * capacity
        partner = rows[1, pl.ds(d, 1)] - partner_zone * capacity
        own = jnp.where(entry < counts[d], own, -1)
        to = (place == own).astype(jnp.float32).astype(jnp.bfloat16)
        source = (place == partner).astype(jnp.float32).astype(jnp.bfloat16)
        table = lax.dot_general(
            to, source, (((1,), (1,)), ((), ())), preferred_element_type=jnp.float32
        )
        tables[slot] = table.astype(jnp.bfloat16)
        ones = jnp.ones((capacity, weight.shape[1]), jnp.bfloat16)
        shared = jnp.dot(table.astype(jnp.bfloat16), ones, preferred_element_type=jnp.float32)
        weight[pl.ds(pl.multiple_of(d * capacity, capacity), capacity)] = 1.0 / (1.0 + shared)


def start_kernel(parity, tables, weight, basis, *refs):
    slots, received, (block, piece) = refs[:4], refs[4:8], refs[8:]
    assemble_into(parity, tables, slots, received, block)
    piece[...] = times(basis[...], weight[...] * block[...])


def gram_start_kernel(parity, tables, weight, basis, z, r, *refs):
    slots, received, (block, carried) = refs[:4], refs[4:8], refs[8:]
    n = z.shape[1]
    assemble_into(parity, tables, slots, received, block)
    carried[n + TAIL :] = times(basis[...], weight[...] * block[...])
    weighted = weight[...] * z[...]
    carried[: n + TAIL] = packed(local_gram(weighted, r[...]), local_gram(weighted, block[...]))


def local_kernel(weight, matrix, block, out):
    out[...] = times(matrix[...], weight[...] * block[...])


def finish_kernel(grams, parity, weight, basis, chosen, local, own, received, *slots):
    pieces = jnp.concatenate([own[grams:], received[grams:]], axis=0)
    picked = times(chosen[...], pieces)
    smoothed = weight[...] * (local[...] + times(basis[...], picked, contracting=0))
    slots_from(parity, smoothed, slots)
    if grams:
        slots[2][slots[0].shape[0] :] = own[:grams] + received[:grams]


def operator_kernel(parity, tables, matrix, *refs):
    slots, received, block, out = refs[:4], refs[4:8], refs[8], refs[9:13]
    zone = out[0].shape[0]
    assemble_into(parity, tables, slots, received, block)
    slots_from(parity, times(matrix[...], block[...]), out)
    for grams in refs[13:]:
        grams[...] = slots[2][zone:] + received[2][zone:]


def first_update_kernel(parity, tables, weight, basis, grams, z, w, r, m, *refs):
    slots, received = refs[:4], refs[4:8]
    x, r_out, z_out, w_out, image, curvature_out, carried = refs[8:]
    n = z.shape[1]
    assemble_into(parity, tables, slots, received, image)
    inner, cross = unpacked(grams[...])
    curvature_out[...] = cross
    alpha = mixer(eliminate(cross, inner))
    w_new = w[...] - mix(image[...], alpha)
    w_out[...] = w_new
    carried[n + TAIL :] = times(basis[...], weight[...] * w_new)
    x[...] = mix(z[...], alpha)
    r_new = r[...] - mix(w[...], alpha)
    r_out[...] = r_new
    z_new = z[...] - mix(m[...], alpha)
    z_out[...] = z_new
    weighted = weight[...] * z_new
    carried[: n + TAIL] = packed(local_gram(weighted, r_new), local_gram(weighted, w_new))


def step_sizes(grams, inner_inverse, curvature):
    inner, cross = unpacked(grams)
    beta = exact(inner_inverse[...], inner)
    bent = symmetric(cross - exact(beta.T, exact(curvature[...], beta)))
    return beta, bent, eliminate(bent, inner)


def next_update_kernel(
    parity, tables, weight, basis, grams, inner_inverse, curvature,
    z, w, r, m, p, s, q, t, x, *refs
):
    slots, received = refs[:4], refs[4:8]
    (
        x_out, r_out, z_out, w_out, p_out, s_out, q_out, t_out, curvature_out, *carried
    ) = refs[8:]
    assemble_into(parity, tables, slots, received, t_out)
    beta, bent, alpha = step_sizes(grams[...], inner_inverse, curvature)
    curvature_out[...] = bent
    beta, alpha = mixer(beta), mixer(alpha)
    t_out[...] = t_out[...] + mix(t[...], beta)
    w_new = w[...] - mix(t_out[...], alpha)
    w_out[...] = w_new
    p_out[...] = z[...] + mix(p[...], beta)
    s_out[...] = w[...] + mix(s[...], beta)
    q_out[...] = m[...] + mix(q[...], beta)
    x_out[...] = x[...] + mix(p_out[...], alpha)
    r_new = r[...] - mix(s_out[...], alpha)
    r_out[...] = r_new
    z_new = z[...] - mix(q_out[...], alpha)
    z_out[...] = z_new
    weighted = weight[...] * z_new
    sums = packed(local_gram(weighted, r_new), local_gram(weighted, w_new))
    if len(carried) == 1:
        rows = sums.shape[0]
        carried[0][:rows] = sums
        carried[0][rows:] = times(basis[...], weight[...] * w_new)
    else:
        kept, sent = carried
        low, high = sums[: kept.shape[0]], sums[kept.shape[0] :]
        kept[...] = jnp.where(parity[1] == 0, low, high)
        sent[...] = jnp.where(parity[1] == 0, high, low)


def last_update_kernel(parity, half, other, inner_inverse, curvature, z, w, r, p, s, x, x_out, r_out):
    low = jnp.where(parity[1] == 0, half[...], other[...])
    high = jnp.where(parity[1] == 0, other[...], half[...])
    sums = jnp.concatenate([low, high], axis=0)
    beta, _, alpha = step_sizes(sums, inner_inverse, curvature)
    beta, alpha = mixer(beta), mixer(alpha)
    x_out[...] = x[...] + mix(z[...] + mix(p[...], beta), alpha)
    r_out[...] = r[...] - mix(w[...] + mix(s[...], beta), alpha)


def inverse_kernel(grams, out):
    n = out.shape[0]
    rows = lax.broadcasted_iota(jnp.int32, (n, n), 0)
    columns = lax.broadcasted_iota(jnp.int32, (n, n), 1)
    inner, _ = unpacked(grams[...])
    out[...] = eliminate(inner, (rows == columns).astype(jnp.float32))


VMEM = pl.BlockSpec(memory_space=pltpu.VMEM)
SMEM = pl.BlockSpec(memory_space=pltpu.SMEM)


def call(kernel, name, flops, outs, *args):
    shapes = [jax.ShapeDtypeStruct(shape, dtype) for shape, dtype in outs]
    moved = sum(a.size * a.dtype.itemsize for a in (*args, *shapes))
    return pl.pallas_call(
        kernel,
        out_shape=shapes,
        in_specs=[SMEM if a.ndim == 1 else VMEM for a in args],
        out_specs=[VMEM] * len(shapes),
        name=name,
        compiler_params=pltpu.CompilerParams(vmem_limit_bytes=24 * 1024 * 1024),
        cost_estimate=pl.CostEstimate(flops=flops, bytes_accessed=moved, transcendentals=0),
    )(*args)


def pairs(axis, first):
    count = lax.axis_size(axis)
    low = range(first, count - 1, 2)
    return [(i, i + 1) for i in low] + [(i + 1, i) for i in low]


def exchange(slots):
    return [
        lax.ppermute(slot, axis, pairs(axis, first))
        for slot, (axis, first) in zip(
            slots, (("sub", 0), ("sub", 1), ("group", 0), ("group", 1))
        )
    ]


def shards(
    schur, local_inverse, rhs_parts, basis, coarse_map, coarse_inverse, shared_rows, shared_counts
):
    schur, local_inverse, basis = schur[0, 0], local_inverse[0, 0], basis[0, 0]
    rhs = rhs_parts[0, 0]
    rows, columns = rhs.shape
    zone = shared_rows.shape[-1]
    modes = basis.shape[0]
    parity = jnp.stack([lax.axis_index("sub") % 2, lax.axis_index("group") % 2]).astype(jnp.int32)
    block = ((rows, columns), jnp.float32)
    part = ((zone, columns), jnp.float32)
    square = ((columns, columns), jnp.float32)
    sums = columns + TAIL
    share = ((modes, columns), jnp.float32)
    carry = ((sums + modes, columns), jnp.float32)
    halves_out = [((sums // 2, columns), jnp.float32)] * 2
    solve_flops = 400_000_000
    product_flops = 4 * rows * rows * columns

    def rhs_zone(slot):
        return lax.dynamic_slice_in_dim(rhs, zone_of(parity, slot) * zone, zone, axis=0)

    rhs_slots = [rhs_zone(slot) for slot in range(4)]
    received = exchange(rhs_slots)
    tables, weight = call(
        tables_kernel,
        "shared_row_tables",
        16 * zone**3,
        [((4, zone, zone), jnp.bfloat16), block],
        parity,
        shared_rows[0, 0],
        shared_counts[0, 0],
    )
    subs = lax.axis_size("sub")
    inverse_rows = coarse_inverse[0]
    maps, (rhs_slots, (received[0], received[2]), (received[1], received[3], weight)) = gather_sub(
        coarse_map[0, 0],
        rhs_slots,
        (received[0], received[2]),
        (received[1], received[3], weight),
    )
    (chosen,) = call(
        choice_kernel,
        "selected_inverse",
        product_flops // 4,
        [((subs, modes, subs * modes), jnp.bfloat16)],
        (lax.axis_index("sub") * inverse_rows.shape[0]).astype(jnp.int32)[None],
        maps[None],
        inverse_rows,
    )
    r, pieces = call(
        start_kernel,
        "start",
        product_flops // 8,
        [block, share],
        parity,
        tables,
        weight,
        basis,
        *rhs_slots,
        *received,
    )
    for bit in reversed(bits_of("sub")):
        arrived = swap(chosen[bit:], "sub", bit)
        if bit == bits_of("sub")[-1]:
            arrived, r, pieces = lax.optimization_barrier((arrived, r, pieces))
        chosen = chosen[:bit] + arrived
    chosen = chosen[0]

    def precondition(vector, carried):
        grams = carried.shape[0] - modes
        (local,) = call(
            local_kernel, "local_inverse", product_flops, [block], weight, local_inverse, vector
        )
        bits = bits_of("sub")
        for bit in bits[:-1]:
            rows_out = 2 * carried.shape[0] - grams
            (carried,) = call(
                functools.partial(fold_kernel, grams),
                "fold",
                columns * rows_out,
                [((rows_out, columns), jnp.float32)],
                carried,
                swap(carried, "sub", bit),
            )
        slots = call(
            functools.partial(finish_kernel, grams),
            "coarse_part",
            product_flops // 8,
            [part, part, ((zone + grams, columns), jnp.float32), part],
            parity,
            weight,
            basis,
            chosen,
            local,
            carried,
            swap(carried, "sub", bits[-1]),
        )
        return slots, exchange(slots)

    def operator(slots, received):
        grams = slots[2].shape[0] - zone
        outs = [((grams, columns), jnp.float32)] if grams else []
        vector, *image = call(
            operator_kernel,
            "operator",
            product_flops,
            [block] + [part] * 4 + outs,
            parity,
            tables,
            schur,
            *slots,
            *received,
        )
        whole = image[4:]
        for bit in bits_of("group")[1:] if grams else ():
            whole = [whole[0] + swap(whole[0], "group", bit)]
        return vector, image[:4], exchange(image[:4]), *whole

    z, image, received = operator(*precondition(r, pieces))
    w, carried = call(
        gram_start_kernel,
        "start_grams",
        product_flops // 4,
        [block, carry],
        parity,
        tables,
        weight,
        basis,
        z,
        r,
        *image,
        *received,
    )
    for iteration in range(ITERS - 1):
        final = iteration + 2 == ITERS
        m, image, received, grams = operator(*precondition(w, carried))
        common = (parity, tables, weight, basis, grams)
        if iteration == 0:
            p, s, q = z, w, m
            x, r, z, w, t, curvature, carried = call(
                first_update_kernel,
                "first_update",
                2 * solve_flops,
                [block] * 5 + [square, carry],
                *common,
                z,
                w,
                r,
                m,
                *image,
                *received,
            )
        else:
            x, r, z, w, p, s, q, t, curvature, *carried = call(
                next_update_kernel,
                "next_update",
                2 * solve_flops,
                [block] * 8 + [square] + (halves_out if final else [carry]),
                *common,
                inner_inverse,
                curvature,
                z,
                w,
                r,
                m,
                p,
                s,
                q,
                t,
                x,
                *image,
                *received,
            )
            if not final:
                (carried,) = carried
        grams, curvature = lax.optimization_barrier((grams, curvature))
        (inner_inverse,) = call(inverse_kernel, "inner_inverse", solve_flops, [square], grams)
    *grams, inner_inverse = total(*carried, inner_inverse)
    x, r = call(
        last_update_kernel,
        "last_update",
        2 * solve_flops,
        [block, block],
        parity,
        *grams,
        inner_inverse,
        curvature,
        z,
        w,
        r,
        p,
        s,
        x,
    )
    return x[None, None], r[None, None]


def solution(mesh):
    placed = (
        P("group", "sub", None, None),
        P("group", "sub", None, None),
        P("group", "sub", None, None),
        P("group", "sub", None, None),
        P("group", "sub", None),
        P("group", "sub", None),
        P("group", "sub", None, None, None),
        P("group", "sub", None),
    )
    return jax.shard_map(
        shards,
        mesh=mesh,
        in_specs=placed,
        out_specs=(P("group", "sub", None, None), P("group", "sub", None, None)),
        check_vma=False,
    )
```

```python
import functools

import jax
import jax.numpy as jnp
from jax import lax
from jax.experimental import pallas as pl
from jax.experimental.pallas import tpu as pltpu
from jax.sharding import PartitionSpec as P

ITERS = 3
TAIL = 16
HIGHEST = lax.Precision.HIGHEST


def swap(x, axis, bit):
    return lax.ppermute(x, axis, [(i, i ^ bit) for i in range(lax.axis_size(axis))])


def bits_of(axis):
    count = lax.axis_size(axis)
    if count & (count - 1):
        raise ValueError("axis size")
    return [1 << b for b in range(count.bit_length() - 1)]


def total(kept, sent, ride):
    half = kept + swap(sent, "group", 1)
    rest = [("group", bit) for bit in bits_of("group")[1:]]
    subs = [("sub", bit) for bit in bits_of("sub")]
    for number, (axis, bit) in enumerate(subs[:1] + rest + subs[1:]):
        arrived = swap(half, axis, bit)
        if number == 1:
            arrived, ride = lax.optimization_barrier((arrived, ride))
        half = half + arrived
    return half, swap(half, "group", 1), ride


def gather_sub(x, *rides):
    rides = list(rides)
    for number, bit in enumerate(bits_of("sub")):
        arrived = swap(x, "sub", bit)
        if number < len(rides):
            arrived, rides[number] = lax.optimization_barrier((arrived, rides[number]))
        x = jnp.concatenate([x, arrived], axis=0)
    return x, rides


def eliminate(matrix, block, tile=8):
    n, width = matrix.shape[0], block.shape[1]
    sublane = lax.broadcasted_iota(jnp.int32, (tile, 1), 0)
    left = [matrix[i : i + tile] for i in range(0, n, tile)]
    right = [block[i : i + tile] for i in range(0, n, tile)]
    for k in range(n // tile):
        pivot_left, pivot_right = left[k], right[k]
        at = k * tile
        spread = [
            jnp.broadcast_to(pivot_left[:, at + j : at + j + 1], (tile, n)) for j in range(tile)
        ]
        for j in range(tile):
            inverse = 1.0 / spread[j][j : j + 1]
            here = sublane == j
            column = spread[j]

            def cleared(rows, column=column, inverse=inverse, here=here, j=j):
                pivot = rows[j : j + 1] * inverse
                return jnp.where(here, pivot, rows - column * pivot)

            for i in range(j + 1, tile):
                spread[i] = cleared(spread[i])
            pivot_left, pivot_right = cleared(pivot_left), cleared(pivot_right)
        for i in range(n // tile):
            if i == k:
                continue
            old = left[i]
            new_left, new_right = old, right[i]
            for j in range(tile):
                scale = jnp.broadcast_to(old[:, at + j : at + j + 1], (tile, n))
                new_left = new_left - scale * pivot_left[j : j + 1]
                new_right = new_right - scale * pivot_right[j : j + 1]
            left[i], right[i] = new_left, new_right
        left[k], right[k] = pivot_left, pivot_right
    return jnp.concatenate(right, axis=0)


def exact(a, b):
    return jnp.dot(a, b, precision=HIGHEST, preferred_element_type=jnp.float32)


def symmetric(a):
    return (a + a.T) * 0.5


def halves(x):
    high = x.astype(jnp.bfloat16)
    low = (x - high.astype(jnp.float32)).astype(jnp.bfloat16)
    return jnp.concatenate([high, low], axis=1)


def folded(both):
    n = both.shape[1] // 2
    return both[:, :n] + both[:, n:]


def times(matrix, x, contracting=1):
    dims = (((contracting,), (0,)), ((), ()))
    if x.dtype == jnp.bfloat16:
        return lax.dot_general(matrix, x, dims, preferred_element_type=jnp.float32)
    return folded(lax.dot_general(matrix, halves(x), dims, preferred_element_type=jnp.float32))


def mixer(mixing):
    both = halves(mixing)
    return jnp.concatenate([both, both], axis=0)


def mix(block, mixer_value):
    return folded(jnp.dot(halves(block), mixer_value, preferred_element_type=jnp.float32))


def local_gram(weighted, right):
    n = weighted.shape[1]
    both = lax.dot_general(
        halves(weighted),
        halves(right),
        (((0,), (0,)), ((), ())),
        preferred_element_type=jnp.float32,
    )
    both = both[:n] + both[n:]
    return both[:, :n] + both[:, n:]


def packed(inner, cross):
    n = inner.shape[0]
    rows = lax.broadcasted_iota(jnp.int32, (n, n), 0)
    columns = lax.broadcasted_iota(jnp.int32, (n, n), 1)
    body = jnp.where(rows > columns, inner, jnp.where(rows < columns, cross, 0.0))
    tail_rows = lax.broadcasted_iota(jnp.int32, (TAIL, n), 0)
    first = jnp.sum(jnp.where(rows == columns, inner, 0.0), axis=0, keepdims=True)
    second = jnp.sum(jnp.where(rows == columns, cross, 0.0), axis=0, keepdims=True)
    tail = jnp.where(tail_rows == 0, first, jnp.where(tail_rows == 1, second, 0.0))
    return jnp.concatenate([body, tail], axis=0)


def unpacked(grams):
    n = grams.shape[1]
    rows = lax.broadcasted_iota(jnp.int32, (n, n), 0)
    columns = lax.broadcasted_iota(jnp.int32, (n, n), 1)
    body = grams[:n]
    lower = jnp.where(rows > columns, body, 0.0)
    upper = jnp.where(rows < columns, body, 0.0)
    inner = lower + lower.T + jnp.where(rows == columns, grams[n : n + 1], 0.0)
    cross = upper + upper.T + jnp.where(rows == columns, grams[n + 1 : n + 2], 0.0)
    return inner, cross


def zone_of(parity, slot):
    flip = parity[slot // 2]
    return 2 * (slot // 2) + (flip if slot % 2 == 0 else 1 - flip)


def assemble_into(parity, tables, slots, received, out):
    zone = slots[0].shape[0]
    for slot in range(4):
        start = pl.multiple_of(zone_of(parity, slot) * zone, zone)
        value = slots[slot][:zone].astype(jnp.float32) + times(tables[slot], received[slot][:zone])
        out[pl.ds(start, zone)] = value


def slots_from(parity, block, slots):
    zone = slots[0].shape[0]
    for slot in range(4):
        pair = 2 * (slot // 2)
        swapped = parity[slot // 2] == (1 if slot % 2 == 0 else 0)
        low, high = block[pair * zone : (pair + 1) * zone], block[(pair + 1) * zone : (pair + 2) * zone]
        slots[slot][:zone] = jnp.where(swapped, high, low)


def choice_kernel(first, maps, inverse_rows, out):
    count, modes, total_modes = out.shape
    rows_here, coarse_total = inverse_rows.shape
    unknown = lax.broadcasted_iota(jnp.int32, (coarse_total, total_modes), 0)
    columns = (unknown == maps[...]).astype(jnp.float32).astype(jnp.bfloat16)
    picked = jnp.dot(inverse_rows[...], columns, preferred_element_type=jnp.float32)
    here = lax.broadcasted_iota(jnp.int32, (rows_here, total_modes), 0) + first[0]
    rows = (here == maps[...]).astype(jnp.float32).astype(jnp.bfloat16)
    table = lax.dot_general(
        rows,
        picked.astype(jnp.bfloat16),
        (((0,), (0,)), ((), ())),
        preferred_element_type=jnp.float32,
    ).astype(jnp.bfloat16)
    source = lax.broadcasted_iota(jnp.int32, (total_modes, total_modes), 0)
    target = lax.broadcasted_iota(jnp.int32, (total_modes, total_modes), 1)
    for j in range(count):
        order = (source == (target ^ (j * modes))).astype(jnp.float32).astype(jnp.bfloat16)
        block = table[j * modes : (j + 1) * modes]
        out[j] = jnp.dot(block, order, preferred_element_type=jnp.float32).astype(jnp.bfloat16)


def fold_kernel(grams, own, received, out):
    count = own.shape[0] - grams
    if grams:
        out[:grams] = own[:grams] + received[:grams]
    out[grams : grams + count] = own[grams:]
    out[grams + count :] = received[grams:]


def tables_kernel(parity, rows, counts, tables, weight):
    capacity = rows.shape[2]
    place = lax.broadcasted_iota(jnp.int32, (capacity, capacity), 0)
    entry = lax.broadcasted_iota(jnp.int32, (1, capacity), 1)
    for slot in range(4):
        d = zone_of(parity, slot)
        partner_zone = zone_of(parity, slot ^ 1)
        own = rows[0, pl.ds(d, 1)] - d * capacity
        partner = rows[1, pl.ds(d, 1)] - partner_zone * capacity
        own = jnp.where(entry < counts[d], own, -1)
        to = (place == own).astype(jnp.float32).astype(jnp.bfloat16)
        source = (place == partner).astype(jnp.float32).astype(jnp.bfloat16)
        table = lax.dot_general(
            to, source, (((1,), (1,)), ((), ())), preferred_element_type=jnp.float32
        )
        tables[slot] = table.astype(jnp.bfloat16)
        ones = jnp.ones((capacity, weight.shape[1]), jnp.bfloat16)
        shared = jnp.dot(table.astype(jnp.bfloat16), ones, preferred_element_type=jnp.float32)
        weight[pl.ds(pl.multiple_of(d * capacity, capacity), capacity)] = 1.0 / (1.0 + shared)


def start_kernel(parity, tables, weight, basis, *refs):
    slots, received, (block, piece) = refs[:4], refs[4:8], refs[8:]
    assemble_into(parity, tables, slots, received, block)
    piece[...] = times(basis[...], weight[...] * block[...])


def gram_start_kernel(parity, tables, weight, basis, z, r, *refs):
    slots, received, (block, carried) = refs[:4], refs[4:8], refs[8:]
    n = z.shape[1]
    assemble_into(parity, tables, slots, received, block)
    carried[n + TAIL :] = times(basis[...], weight[...] * block[...])
    weighted = weight[...] * z[...]
    carried[: n + TAIL] = packed(local_gram(weighted, r[...]), local_gram(weighted, block[...]))


def local_kernel(weight, matrix, block, out):
    out[...] = times(matrix[...], weight[...] * block[...])


def finish_kernel(grams, parity, weight, basis, chosen, local, own, received, *slots):
    pieces = jnp.concatenate([own[grams:], received[grams:]], axis=0)
    picked = times(chosen[...], pieces)
    smoothed = weight[...] * (local[...] + times(basis[...], picked, contracting=0))
    slots_from(parity, smoothed, slots)
    if grams:
        slots[2][slots[0].shape[0] :] = own[:grams] + received[:grams]


def operator_kernel(parity, tables, matrix, *refs):
    slots, received, block, out = refs[:4], refs[4:8], refs[8], refs[9:13]
    zone = out[0].shape[0]
    assemble_into(parity, tables, slots, received, block)
    slots_from(parity, times(matrix[...], block[...]), out)
    for grams in refs[13:]:
        grams[...] = slots[2][zone:] + received[2][zone:]


def first_update_kernel(parity, tables, weight, basis, grams, z, w, r, m, *refs):
    slots, received = refs[:4], refs[4:8]
    x, r_out, z_out, w_out, image, curvature_out, carried = refs[8:]
    n = z.shape[1]
    assemble_into(parity, tables, slots, received, image)
    inner, cross = unpacked(grams[...])
    curvature_out[...] = cross
    alpha = mixer(eliminate(cross, inner))
    w_new = w[...] - mix(image[...], alpha)
    w_out[...] = w_new
    carried[n + TAIL :] = times(basis[...], weight[...] * w_new)
    x[...] = mix(z[...], alpha)
    r_new = r[...] - mix(w[...], alpha)
    r_out[...] = r_new
    z_new = z[...] - mix(m[...], alpha)
    z_out[...] = z_new
    weighted = weight[...] * z_new
    carried[: n + TAIL] = packed(local_gram(weighted, r_new), local_gram(weighted, w_new))


def step_sizes(grams, inner_inverse, curvature):
    inner, cross = unpacked(grams)
    beta = exact(inner_inverse[...], inner)
    bent = symmetric(cross - exact(beta.T, exact(curvature[...], beta)))
    return beta, bent, eliminate(bent, inner)


def next_update_kernel(
    parity, tables, weight, basis, grams, inner_inverse, curvature,
    z, w, r, m, p, s, q, t, x, *refs
):
    slots, received = refs[:4], refs[4:8]
    (
        x_out, r_out, z_out, w_out, p_out, s_out, q_out, t_out, curvature_out, *carried
    ) = refs[8:]
    assemble_into(parity, tables, slots, received, t_out)
    beta, bent, alpha = step_sizes(grams[...], inner_inverse, curvature)
    curvature_out[...] = bent
    beta, alpha = mixer(beta), mixer(alpha)
    t_out[...] = t_out[...] + mix(t[...], beta)
    w_new = w[...] - mix(t_out[...], alpha)
    w_out[...] = w_new
    p_out[...] = z[...] + mix(p[...], beta)
    s_out[...] = w[...] + mix(s[...], beta)
    q_out[...] = m[...] + mix(q[...], beta)
    x_out[...] = x[...] + mix(p_out[...], alpha)
    r_new = r[...] - mix(s_out[...], alpha)
    r_out[...] = r_new
    z_new = z[...] - mix(q_out[...], alpha)
    z_out[...] = z_new
    weighted = weight[...] * z_new
    sums = packed(local_gram(weighted, r_new), local_gram(weighted, w_new))
    if len(carried) == 1:
        rows = sums.shape[0]
        carried[0][:rows] = sums
        carried[0][rows:] = times(basis[...], weight[...] * w_new)
    else:
        kept, sent = carried
        low, high = sums[: kept.shape[0]], sums[kept.shape[0] :]
        kept[...] = jnp.where(parity[1] == 0, low, high)
        sent[...] = jnp.where(parity[1] == 0, high, low)


def last_update_kernel(parity, half, other, inner_inverse, curvature, z, w, r, p, s, x, x_out, r_out):
    low = jnp.where(parity[1] == 0, half[...], other[...])
    high = jnp.where(parity[1] == 0, other[...], half[...])
    sums = jnp.concatenate([low, high], axis=0)
    beta, _, alpha = step_sizes(sums, inner_inverse, curvature)
    beta, alpha = mixer(beta), mixer(alpha)
    x_out[...] = x[...] + mix(z[...] + mix(p[...], beta), alpha)
    r_out[...] = r[...] - mix(w[...] + mix(s[...], beta), alpha)


def inverse_kernel(grams, out):
    n = out.shape[0]
    rows = lax.broadcasted_iota(jnp.int32, (n, n), 0)
    columns = lax.broadcasted_iota(jnp.int32, (n, n), 1)
    inner, _ = unpacked(grams[...])
    out[...] = eliminate(inner, (rows == columns).astype(jnp.float32))


VMEM = pl.BlockSpec(memory_space=pltpu.VMEM)
SMEM = pl.BlockSpec(memory_space=pltpu.SMEM)


def call(kernel, name, flops, outs, *args):
    shapes = [jax.ShapeDtypeStruct(shape, dtype) for shape, dtype in outs]
    moved = sum(a.size * a.dtype.itemsize for a in (*args, *shapes))
    return pl.pallas_call(
        kernel,
        out_shape=shapes,
        in_specs=[SMEM if a.ndim == 1 else VMEM for a in args],
        out_specs=[VMEM] * len(shapes),
        name=name,
        compiler_params=pltpu.CompilerParams(vmem_limit_bytes=24 * 1024 * 1024),
        cost_estimate=pl.CostEstimate(flops=flops, bytes_accessed=moved, transcendentals=0),
    )(*args)


def pairs(axis, first):
    count = lax.axis_size(axis)
    low = range(first, count - 1, 2)
    return [(i, i + 1) for i in low] + [(i + 1, i) for i in low]


def exchange(slots):
    return [
        lax.ppermute(slot, axis, pairs(axis, first))
        for slot, (axis, first) in zip(
            slots, (("sub", 0), ("sub", 1), ("group", 0), ("group", 1))
        )
    ]


def shards(
    schur, local_inverse, rhs_parts, basis, coarse_map, coarse_inverse, shared_rows, shared_counts
):
    schur, local_inverse, basis = schur[0, 0], local_inverse[0, 0], basis[0, 0]
    rhs = rhs_parts[0, 0]
    rows, columns = rhs.shape
    zone = shared_rows.shape[-1]
    modes = basis.shape[0]
    parity = jnp.stack([lax.axis_index("sub") % 2, lax.axis_index("group") % 2]).astype(jnp.int32)
    block = ((rows, columns), jnp.float32)
    part = ((zone, columns), jnp.float32)
    square = ((columns, columns), jnp.float32)
    sums = columns + TAIL
    share = ((modes, columns), jnp.float32)
    carry = ((sums + modes, columns), jnp.float32)
    halves_out = [((sums // 2, columns), jnp.float32)] * 2
    solve_flops = 400_000_000
    product_flops = 4 * rows * rows * columns

    def rhs_zone(slot):
        return lax.dynamic_slice_in_dim(rhs, zone_of(parity, slot) * zone, zone, axis=0)

    rhs_slots = [rhs_zone(slot) for slot in range(4)]
    received = exchange(rhs_slots)
    tables, weight = call(
        tables_kernel,
        "shared_row_tables",
        16 * zone**3,
        [((4, zone, zone), jnp.bfloat16), block],
        parity,
        shared_rows[0, 0],
        shared_counts[0, 0],
    )
    subs = lax.axis_size("sub")
    inverse_rows = coarse_inverse[0]
    maps, (rhs_slots, (received[0], received[2]), (received[1], received[3], weight)) = gather_sub(
        coarse_map[0, 0],
        rhs_slots,
        (received[0], received[2]),
        (received[1], received[3], weight),
    )
    (chosen,) = call(
        choice_kernel,
        "selected_inverse",
        product_flops // 4,
        [((subs, modes, subs * modes), jnp.bfloat16)],
        (lax.axis_index("sub") * inverse_rows.shape[0]).astype(jnp.int32)[None],
        maps[None],
        inverse_rows,
    )
    r, pieces = call(
        start_kernel,
        "start",
        product_flops // 8,
        [block, share],
        parity,
        tables,
        weight,
        basis,
        *rhs_slots,
        *received,
    )
    for bit in reversed(bits_of("sub")):
        arrived = swap(chosen[bit:], "sub", bit)
        if bit == bits_of("sub")[-1]:
            arrived, r, pieces = lax.optimization_barrier((arrived, r, pieces))
        chosen = chosen[:bit] + arrived
    chosen = chosen[0]

    def precondition(vector, carried, ride=None):
        grams = carried.shape[0] - modes
        (local,) = call(
            local_kernel, "local_inverse", product_flops, [block], weight, local_inverse, vector
        )
        bits = bits_of("sub")
        for number, bit in enumerate(bits[:-1]):
            rows_out = 2 * carried.shape[0] - grams
            arrived = swap(carried, "sub", bit)
            if ride is not None and number == len(bits[:-1]) - 1:
                arrived, ride = lax.optimization_barrier((arrived, ride))
            (carried,) = call(
                functools.partial(fold_kernel, grams),
                "fold",
                columns * rows_out,
                [((rows_out, columns), jnp.float32)],
                carried,
                arrived,
            )
        slots = call(
            functools.partial(finish_kernel, grams),
            "coarse_part",
            product_flops // 8,
            [part, part, ((zone + grams, columns), jnp.float32), part],
            parity,
            weight,
            basis,
            chosen,
            local,
            carried,
            swap(carried, "sub", bits[-1]),
        )
        return slots, exchange(slots), ride

    def operator(slots, received):
        grams = slots[2].shape[0] - zone
        outs = [((grams, columns), jnp.float32)] if grams else []
        vector, *image = call(
            operator_kernel,
            "operator",
            product_flops,
            [block] + [part] * 4 + outs,
            parity,
            tables,
            schur,
            *slots,
            *received,
        )
        whole = image[4:]
        for bit in bits_of("group")[1:] if grams else ():
            whole = [whole[0] + swap(whole[0], "group", bit)]
        return vector, image[:4], exchange(image[:4]), *whole

    z, image, received = operator(*precondition(r, pieces)[:2])
    w, carried = call(
        gram_start_kernel,
        "start_grams",
        product_flops // 4,
        [block, carry],
        parity,
        tables,
        weight,
        basis,
        z,
        r,
        *image,
        *received,
    )
    ride = None
    for iteration in range(ITERS - 1):
        final = iteration + 2 == ITERS
        slots, received, inner_inverse = precondition(w, carried, ride)
        m, image, received, grams = operator(slots, received)
        common = (parity, tables, weight, basis, grams)
        if iteration == 0:
            p, s, q = z, w, m
            x, r, z, w, t, curvature, carried = call(
                first_update_kernel,
                "first_update",
                2 * solve_flops,
                [block] * 5 + [square, carry],
                *common,
                z,
                w,
                r,
                m,
                *image,
                *received,
            )
        else:
            x, r, z, w, p, s, q, t, curvature, *carried = call(
                next_update_kernel,
                "next_update",
                2 * solve_flops,
                [block] * 8 + [square] + (halves_out if final else [carry]),
                *common,
                inner_inverse,
                curvature,
                z,
                w,
                r,
                m,
                p,
                s,
                q,
                t,
                x,
                *image,
                *received,
            )
            if not final:
                (carried,) = carried
        grams, curvature = lax.optimization_barrier((grams, curvature))
        (ride,) = call(inverse_kernel, "inner_inverse", solve_flops, [square], grams)
    *grams, inner_inverse = total(*carried, ride)
    x, r = call(
        last_update_kernel,
        "last_update",
        2 * solve_flops,
        [block, block],
        parity,
        *grams,
        inner_inverse,
        curvature,
        z,
        w,
        r,
        p,
        s,
        x,
    )
    return x[None, None], r[None, None]


def solution(mesh):
    placed = (
        P("group", "sub", None, None),
        P("group", "sub", None, None),
        P("group", "sub", None, None),
        P("group", "sub", None, None),
        P("group", "sub", None),
        P("group", "sub", None),
        P("group", "sub", None, None, None),
        P("group", "sub", None),
    )
    return jax.shard_map(
        shards,
        mesh=mesh,
        in_specs=placed,
        out_specs=(P("group", "sub", None, None), P("group", "sub", None, None)),
        check_vma=False,
    )
```

```python
import functools

import jax
import jax.numpy as jnp
from jax import lax
from jax.experimental import pallas as pl
from jax.experimental.pallas import tpu as pltpu
from jax.sharding import PartitionSpec as P

ITERS = 3
TAIL = 16
HIGHEST = lax.Precision.HIGHEST


def swap(x, axis, bit):
    return lax.ppermute(x, axis, [(i, i ^ bit) for i in range(lax.axis_size(axis))])


def bits_of(axis):
    count = lax.axis_size(axis)
    if count & (count - 1):
        raise ValueError("axis size")
    return [1 << b for b in range(count.bit_length() - 1)]


def total(kept, sent, ride):
    half = kept + swap(sent, "group", 1)
    subs = bits_of("sub")
    rounds = [[("sub", bit)] for bit in subs[:-2]]
    rounds += [[("group", bit)] for bit in bits_of("group")[1:]]
    rounds += [[("sub", bit) for bit in (*subs[-2:], sum(subs[-2:]))]]
    for number, partners in enumerate(rounds):
        arrived = [swap(half, axis, bit) for axis, bit in partners]
        if number + 1 == len(rounds):
            arrived, ride = lax.optimization_barrier((arrived, ride))
        half = half + sum(arrived[1:], arrived[0])
    return half, swap(half, "group", 1), ride


def gather_sub(x, *rides):
    rides = list(rides)
    for number, bit in enumerate(bits_of("sub")):
        arrived = swap(x, "sub", bit)
        if number < len(rides):
            arrived, rides[number] = lax.optimization_barrier((arrived, rides[number]))
        x = jnp.concatenate([x, arrived], axis=0)
    return x, rides


def eliminate(matrix, block, tile=8):
    n, width = matrix.shape[0], block.shape[1]
    sublane = lax.broadcasted_iota(jnp.int32, (tile, 1), 0)
    left = [matrix[i : i + tile] for i in range(0, n, tile)]
    right = [block[i : i + tile] for i in range(0, n, tile)]
    for k in range(n // tile):
        pivot_left, pivot_right = left[k], right[k]
        at = k * tile
        spread = [
            jnp.broadcast_to(pivot_left[:, at + j : at + j + 1], (tile, n)) for j in range(tile)
        ]
        for j in range(tile):
            inverse = 1.0 / spread[j][j : j + 1]
            here = sublane == j
            column = spread[j]

            def cleared(rows, column=column, inverse=inverse, here=here, j=j):
                pivot = rows[j : j + 1] * inverse
                return jnp.where(here, pivot, rows - column * pivot)

            for i in range(j + 1, tile):
                spread[i] = cleared(spread[i])
            pivot_left, pivot_right = cleared(pivot_left), cleared(pivot_right)
        for i in range(n // tile):
            if i == k:
                continue
            old = left[i]
            new_left, new_right = old, right[i]
            for j in range(tile):
                scale = jnp.broadcast_to(old[:, at + j : at + j + 1], (tile, n))
                new_left = new_left - scale * pivot_left[j : j + 1]
                new_right = new_right - scale * pivot_right[j : j + 1]
            left[i], right[i] = new_left, new_right
        left[k], right[k] = pivot_left, pivot_right
    return jnp.concatenate(right, axis=0)


def exact(a, b):
    return jnp.dot(a, b, precision=HIGHEST, preferred_element_type=jnp.float32)


def symmetric(a):
    return (a + a.T) * 0.5


def halves(x):
    high = x.astype(jnp.bfloat16)
    low = (x - high.astype(jnp.float32)).astype(jnp.bfloat16)
    return jnp.concatenate([high, low], axis=1)


def folded(both):
    n = both.shape[1] // 2
    return both[:, :n] + both[:, n:]


def times(matrix, x, contracting=1):
    dims = (((contracting,), (0,)), ((), ()))
    if x.dtype == jnp.bfloat16:
        return lax.dot_general(matrix, x, dims, preferred_element_type=jnp.float32)
    return folded(lax.dot_general(matrix, halves(x), dims, preferred_element_type=jnp.float32))


def mixer(mixing):
    both = halves(mixing)
    return jnp.concatenate([both, both], axis=0)


def mix(block, mixer_value):
    return folded(jnp.dot(halves(block), mixer_value, preferred_element_type=jnp.float32))


def local_gram(weighted, right):
    n = weighted.shape[1]
    both = lax.dot_general(
        halves(weighted),
        halves(right),
        (((0,), (0,)), ((), ())),
        preferred_element_type=jnp.float32,
    )
    both = both[:n] + both[n:]
    return both[:, :n] + both[:, n:]


def packed(inner, cross):
    n = inner.shape[0]
    rows = lax.broadcasted_iota(jnp.int32, (n, n), 0)
    columns = lax.broadcasted_iota(jnp.int32, (n, n), 1)
    body = jnp.where(rows > columns, inner, jnp.where(rows < columns, cross, 0.0))
    tail_rows = lax.broadcasted_iota(jnp.int32, (TAIL, n), 0)
    first = jnp.sum(jnp.where(rows == columns, inner, 0.0), axis=0, keepdims=True)
    second = jnp.sum(jnp.where(rows == columns, cross, 0.0), axis=0, keepdims=True)
    tail = jnp.where(tail_rows == 0, first, jnp.where(tail_rows == 1, second, 0.0))
    return jnp.concatenate([body, tail], axis=0)


def unpacked(grams):
    n = grams.shape[1]
    rows = lax.broadcasted_iota(jnp.int32, (n, n), 0)
    columns = lax.broadcasted_iota(jnp.int32, (n, n), 1)
    body = grams[:n]
    lower = jnp.where(rows > columns, body, 0.0)
    upper = jnp.where(rows < columns, body, 0.0)
    inner = lower + lower.T + jnp.where(rows == columns, grams[n : n + 1], 0.0)
    cross = upper + upper.T + jnp.where(rows == columns, grams[n + 1 : n + 2], 0.0)
    return inner, cross


def zone_of(parity, slot):
    flip = parity[slot // 2]
    return 2 * (slot // 2) + (flip if slot % 2 == 0 else 1 - flip)


def assemble_into(parity, tables, slots, received, out):
    zone = slots[0].shape[0]
    for slot in range(4):
        start = pl.multiple_of(zone_of(parity, slot) * zone, zone)
        value = slots[slot][:zone].astype(jnp.float32) + times(tables[slot], received[slot][:zone])
        out[pl.ds(start, zone)] = value


def slots_from(parity, block, slots):
    zone = slots[0].shape[0]
    for slot in range(4):
        pair = 2 * (slot // 2)
        swapped = parity[slot // 2] == (1 if slot % 2 == 0 else 0)
        low, high = block[pair * zone : (pair + 1) * zone], block[(pair + 1) * zone : (pair + 2) * zone]
        slots[slot][:zone] = jnp.where(swapped, high, low)


def choice_kernel(first, maps, inverse_rows, out):
    count, modes, total_modes = out.shape
    rows_here, coarse_total = inverse_rows.shape
    unknown = lax.broadcasted_iota(jnp.int32, (coarse_total, total_modes), 0)
    columns = (unknown == maps[...]).astype(jnp.float32).astype(jnp.bfloat16)
    picked = jnp.dot(inverse_rows[...], columns, preferred_element_type=jnp.float32)
    here = lax.broadcasted_iota(jnp.int32, (rows_here, total_modes), 0) + first[0]
    rows = (here == maps[...]).astype(jnp.float32).astype(jnp.bfloat16)
    table = lax.dot_general(
        rows,
        picked.astype(jnp.bfloat16),
        (((0,), (0,)), ((), ())),
        preferred_element_type=jnp.float32,
    ).astype(jnp.bfloat16)
    source = lax.broadcasted_iota(jnp.int32, (total_modes, total_modes), 0)
    target = lax.broadcasted_iota(jnp.int32, (total_modes, total_modes), 1)
    for j in range(count):
        order = (source == (target ^ (j * modes))).astype(jnp.float32).astype(jnp.bfloat16)
        block = table[j * modes : (j + 1) * modes]
        out[j] = jnp.dot(block, order, preferred_element_type=jnp.float32).astype(jnp.bfloat16)


def fold_kernel(grams, own, received, out):
    count = own.shape[0] - grams
    if grams:
        out[:grams] = own[:grams] + received[:grams]
    out[grams : grams + count] = own[grams:]
    out[grams + count :] = received[grams:]


def tables_kernel(parity, rows, counts, tables, weight):
    capacity = rows.shape[2]
    place = lax.broadcasted_iota(jnp.int32, (capacity, capacity), 0)
    entry = lax.broadcasted_iota(jnp.int32, (1, capacity), 1)
    for slot in range(4):
        d = zone_of(parity, slot)
        partner_zone = zone_of(parity, slot ^ 1)
        own = rows[0, pl.ds(d, 1)] - d * capacity
        partner = rows[1, pl.ds(d, 1)] - partner_zone * capacity
        own = jnp.where(entry < counts[d], own, -1)
        to = (place == own).astype(jnp.float32).astype(jnp.bfloat16)
        source = (place == partner).astype(jnp.float32).astype(jnp.bfloat16)
        table = lax.dot_general(
            to, source, (((1,), (1,)), ((), ())), preferred_element_type=jnp.float32
        )
        tables[slot] = table.astype(jnp.bfloat16)
        ones = jnp.ones((capacity, weight.shape[1]), jnp.bfloat16)
        shared = jnp.dot(table.astype(jnp.bfloat16), ones, preferred_element_type=jnp.float32)
        weight[pl.ds(pl.multiple_of(d * capacity, capacity), capacity)] = 1.0 / (1.0 + shared)


def start_kernel(parity, tables, weight, basis, *refs):
    slots, received, (block, piece) = refs[:4], refs[4:8], refs[8:]
    assemble_into(parity, tables, slots, received, block)
    piece[...] = times(basis[...], weight[...] * block[...])


def gram_start_kernel(parity, tables, weight, basis, z, r, *refs):
    slots, received, (block, carried) = refs[:4], refs[4:8], refs[8:]
    n = z.shape[1]
    assemble_into(parity, tables, slots, received, block)
    carried[n + TAIL :] = times(basis[...], weight[...] * block[...])
    weighted = weight[...] * z[...]
    carried[: n + TAIL] = packed(local_gram(weighted, r[...]), local_gram(weighted, block[...]))


def local_kernel(weight, matrix, block, out):
    out[...] = times(matrix[...], weight[...] * block[...])


def finish_kernel(grams, parity, weight, basis, chosen, local, own, received, *slots):
    pieces = jnp.concatenate([own[grams:], received[grams:]], axis=0)
    picked = times(chosen[...], pieces)
    smoothed = weight[...] * (local[...] + times(basis[...], picked, contracting=0))
    slots_from(parity, smoothed, slots)
    if grams:
        slots[2][slots[0].shape[0] :] = own[:grams] + received[:grams]


def operator_kernel(parity, tables, matrix, *refs):
    slots, received, block, out = refs[:4], refs[4:8], refs[8], refs[9:13]
    zone = out[0].shape[0]
    assemble_into(parity, tables, slots, received, block)
    slots_from(parity, times(matrix[...], block[...]), out)
    for grams in refs[13:]:
        grams[...] = slots[2][zone:] + received[2][zone:]


def first_update_kernel(parity, tables, weight, basis, grams, z, w, r, m, *refs):
    slots, received = refs[:4], refs[4:8]
    x, r_out, z_out, w_out, image, curvature_out, carried = refs[8:]
    n = z.shape[1]
    assemble_into(parity, tables, slots, received, image)
    inner, cross = unpacked(grams[...])
    curvature_out[...] = cross
    alpha = mixer(eliminate(cross, inner))
    w_new = w[...] - mix(image[...], alpha)
    w_out[...] = w_new
    carried[n + TAIL :] = times(basis[...], weight[...] * w_new)
    x[...] = mix(z[...], alpha)
    r_new = r[...] - mix(w[...], alpha)
    r_out[...] = r_new
    z_new = z[...] - mix(m[...], alpha)
    z_out[...] = z_new
    weighted = weight[...] * z_new
    carried[: n + TAIL] = packed(local_gram(weighted, r_new), local_gram(weighted, w_new))


def step_sizes(grams, inner_inverse, curvature):
    inner, cross = unpacked(grams)
    beta = exact(inner_inverse[...], inner)
    bent = symmetric(cross - exact(beta.T, exact(curvature[...], beta)))
    return beta, bent, eliminate(bent, inner)


def next_update_kernel(
    parity, tables, weight, basis, grams, inner_inverse, curvature,
    z, w, r, m, p, s, q, t, x, *refs
):
    slots, received = refs[:4], refs[4:8]
    (
        x_out, r_out, z_out, w_out, p_out, s_out, q_out, t_out, curvature_out, *carried
    ) = refs[8:]
    assemble_into(parity, tables, slots, received, t_out)
    beta, bent, alpha = step_sizes(grams[...], inner_inverse, curvature)
    curvature_out[...] = bent
    beta, alpha = mixer(beta), mixer(alpha)
    t_out[...] = t_out[...] + mix(t[...], beta)
    w_new = w[...] - mix(t_out[...], alpha)
    w_out[...] = w_new
    p_out[...] = z[...] + mix(p[...], beta)
    s_out[...] = w[...] + mix(s[...], beta)
    q_out[...] = m[...] + mix(q[...], beta)
    x_out[...] = x[...] + mix(p_out[...], alpha)
    r_new = r[...] - mix(s_out[...], alpha)
    r_out[...] = r_new
    z_new = z[...] - mix(q_out[...], alpha)
    z_out[...] = z_new
    weighted = weight[...] * z_new
    sums = packed(local_gram(weighted, r_new), local_gram(weighted, w_new))
    if len(carried) == 1:
        rows = sums.shape[0]
        carried[0][:rows] = sums
        carried[0][rows:] = times(basis[...], weight[...] * w_new)
    else:
        kept, sent = carried
        low, high = sums[: kept.shape[0]], sums[kept.shape[0] :]
        kept[...] = jnp.where(parity[1] == 0, low, high)
        sent[...] = jnp.where(parity[1] == 0, high, low)


def last_update_kernel(parity, half, other, inner_inverse, curvature, z, w, r, p, s, x, x_out, r_out):
    low = jnp.where(parity[1] == 0, half[...], other[...])
    high = jnp.where(parity[1] == 0, other[...], half[...])
    sums = jnp.concatenate([low, high], axis=0)
    beta, _, alpha = step_sizes(sums, inner_inverse, curvature)
    beta, alpha = mixer(beta), mixer(alpha)
    x_out[...] = x[...] + mix(z[...] + mix(p[...], beta), alpha)
    r_out[...] = r[...] - mix(w[...] + mix(s[...], beta), alpha)


def inverse_kernel(grams, out):
    n = out.shape[0]
    rows = lax.broadcasted_iota(jnp.int32, (n, n), 0)
    columns = lax.broadcasted_iota(jnp.int32, (n, n), 1)
    inner, _ = unpacked(grams[...])
    out[...] = eliminate(inner, (rows == columns).astype(jnp.float32))


VMEM = pl.BlockSpec(memory_space=pltpu.VMEM)
SMEM = pl.BlockSpec(memory_space=pltpu.SMEM)


def call(kernel, name, flops, outs, *args):
    shapes = [jax.ShapeDtypeStruct(shape, dtype) for shape, dtype in outs]
    moved = sum(a.size * a.dtype.itemsize for a in (*args, *shapes))
    return pl.pallas_call(
        kernel,
        out_shape=shapes,
        in_specs=[SMEM if a.ndim == 1 else VMEM for a in args],
        out_specs=[VMEM] * len(shapes),
        name=name,
        compiler_params=pltpu.CompilerParams(vmem_limit_bytes=24 * 1024 * 1024),
        cost_estimate=pl.CostEstimate(flops=flops, bytes_accessed=moved, transcendentals=0),
    )(*args)


def pairs(axis, first):
    count = lax.axis_size(axis)
    low = range(first, count - 1, 2)
    return [(i, i + 1) for i in low] + [(i + 1, i) for i in low]


def exchange(slots):
    return [
        lax.ppermute(slot, axis, pairs(axis, first))
        for slot, (axis, first) in zip(
            slots, (("sub", 0), ("sub", 1), ("group", 0), ("group", 1))
        )
    ]


def shards(
    schur, local_inverse, rhs_parts, basis, coarse_map, coarse_inverse, shared_rows, shared_counts
):
    schur, local_inverse, basis = schur[0, 0], local_inverse[0, 0], basis[0, 0]
    rhs = rhs_parts[0, 0]
    rows, columns = rhs.shape
    zone = shared_rows.shape[-1]
    modes = basis.shape[0]
    parity = jnp.stack([lax.axis_index("sub") % 2, lax.axis_index("group") % 2]).astype(jnp.int32)
    block = ((rows, columns), jnp.float32)
    part = ((zone, columns), jnp.float32)
    square = ((columns, columns), jnp.float32)
    sums = columns + TAIL
    share = ((modes, columns), jnp.float32)
    carry = ((sums + modes, columns), jnp.float32)
    halves_out = [((sums // 2, columns), jnp.float32)] * 2
    solve_flops = 400_000_000
    product_flops = 4 * rows * rows * columns

    def rhs_zone(slot):
        return lax.dynamic_slice_in_dim(rhs, zone_of(parity, slot) * zone, zone, axis=0)

    rhs_slots = [rhs_zone(slot) for slot in range(4)]
    received = exchange(rhs_slots)
    tables, weight = call(
        tables_kernel,
        "shared_row_tables",
        16 * zone**3,
        [((4, zone, zone), jnp.bfloat16), block],
        parity,
        shared_rows[0, 0],
        shared_counts[0, 0],
    )
    subs = lax.axis_size("sub")
    inverse_rows = coarse_inverse[0]
    maps, (rhs_slots, (received[0], received[2]), (received[1], received[3], weight)) = gather_sub(
        coarse_map[0, 0],
        rhs_slots,
        (received[0], received[2]),
        (received[1], received[3], weight),
    )
    (chosen,) = call(
        choice_kernel,
        "selected_inverse",
        product_flops // 4,
        [((subs, modes, subs * modes), jnp.bfloat16)],
        (lax.axis_index("sub") * inverse_rows.shape[0]).astype(jnp.int32)[None],
        maps[None],
        inverse_rows,
    )
    r, pieces = call(
        start_kernel,
        "start",
        product_flops // 8,
        [block, share],
        parity,
        tables,
        weight,
        basis,
        *rhs_slots,
        *received,
    )
    for bit in reversed(bits_of("sub")):
        arrived = swap(chosen[bit:], "sub", bit)
        if bit == bits_of("sub")[-1]:
            arrived, r, pieces = lax.optimization_barrier((arrived, r, pieces))
        chosen = chosen[:bit] + arrived
    chosen = chosen[0]

    def precondition(vector, carried):
        grams = carried.shape[0] - modes
        (local,) = call(
            local_kernel, "local_inverse", product_flops, [block], weight, local_inverse, vector
        )
        bits = bits_of("sub")
        for bit in bits[:-1]:
            rows_out = 2 * carried.shape[0] - grams
            (carried,) = call(
                functools.partial(fold_kernel, grams),
                "fold",
                columns * rows_out,
                [((rows_out, columns), jnp.float32)],
                carried,
                swap(carried, "sub", bit),
            )
        slots = call(
            functools.partial(finish_kernel, grams),
            "coarse_part",
            product_flops // 8,
            [part, part, ((zone + grams, columns), jnp.float32), part],
            parity,
            weight,
            basis,
            chosen,
            local,
            carried,
            swap(carried, "sub", bits[-1]),
        )
        return slots, exchange(slots)

    def operator(slots, received):
        grams = slots[2].shape[0] - zone
        outs = [((grams, columns), jnp.float32)] if grams else []
        vector, *image = call(
            operator_kernel,
            "operator",
            product_flops,
            [block] + [part] * 4 + outs,
            parity,
            tables,
            schur,
            *slots,
            *received,
        )
        whole = image[4:]
        for bit in bits_of("group")[1:] if grams else ():
            whole = [whole[0] + swap(whole[0], "group", bit)]
        return vector, image[:4], exchange(image[:4]), *whole

    z, image, received = operator(*precondition(r, pieces))
    w, carried = call(
        gram_start_kernel,
        "start_grams",
        product_flops // 4,
        [block, carry],
        parity,
        tables,
        weight,
        basis,
        z,
        r,
        *image,
        *received,
    )
    for iteration in range(ITERS - 1):
        final = iteration + 2 == ITERS
        m, image, received, grams = operator(*precondition(w, carried))
        common = (parity, tables, weight, basis, grams)
        if iteration == 0:
            p, s, q = z, w, m
            x, r, z, w, t, curvature, carried = call(
                first_update_kernel,
                "first_update",
                2 * solve_flops,
                [block] * 5 + [square, carry],
                *common,
                z,
                w,
                r,
                m,
                *image,
                *received,
            )
        else:
            x, r, z, w, p, s, q, t, curvature, *carried = call(
                next_update_kernel,
                "next_update",
                2 * solve_flops,
                [block] * 8 + [square] + (halves_out if final else [carry]),
                *common,
                inner_inverse,
                curvature,
                z,
                w,
                r,
                m,
                p,
                s,
                q,
                t,
                x,
                *image,
                *received,
            )
            if not final:
                (carried,) = carried
        grams, curvature = lax.optimization_barrier((grams, curvature))
        (inner_inverse,) = call(inverse_kernel, "inner_inverse", solve_flops, [square], grams)
    *grams, inner_inverse = total(*carried, inner_inverse)
    x, r = call(
        last_update_kernel,
        "last_update",
        2 * solve_flops,
        [block, block],
        parity,
        *grams,
        inner_inverse,
        curvature,
        z,
        w,
        r,
        p,
        s,
        x,
    )
    return x[None, None], r[None, None]


def solution(mesh):
    placed = (
        P("group", "sub", None, None),
        P("group", "sub", None, None),
        P("group", "sub", None, None),
        P("group", "sub", None, None),
        P("group", "sub", None),
        P("group", "sub", None),
        P("group", "sub", None, None, None),
        P("group", "sub", None),
    )
    return jax.shard_map(
        shards,
        mesh=mesh,
        in_specs=placed,
        out_specs=(P("group", "sub", None, None), P("group", "sub", None, None)),
        check_vma=False,
    )
```
